32 devices in a mesh: ctx: 8 (over z, x), exp: 4 (over y, core).
Axes of the slice: x: 2, y: 2, z: 4, core: 2. Of those that a mesh axis runs over, the one named last changes fastest.
Arguments:
- queries: bfloat16 [1024, 6144], P('ctx', 'exp'), may hold values from -6 to 6
- keys: bfloat16 [1024, 6144], P('ctx', 'exp'), may hold values from -6 to 6
- values: bfloat16 [1024, 6144], P('ctx', 'exp'), may hold values from -6 to 6
- out_grad: bfloat16 [1024, 6144], P('ctx', 'exp'), may hold values from -6 to 6
- up_weight: bfloat16 [8, 6144, 2304], P('ctx', 'exp'), may hold values from -0.078125 to 0.078125
- down_weight: bfloat16 [8, 2304, 6144], P('ctx', None, 'exp'), may hold values from -0.09375 to 0.09375
- decay_rates: float32 [48], P('exp'), may hold values from 9.765625e-05 to 0.0333333333
- routes: int32 [1024, 2], P('ctx'), may hold values from 0 to 3, all different within a row; in each aligned block of 128 rows (0 to 127, 128 to 255, ...) at most 72 rows name the same one
- gate_weights: float32 [1024, 2], P('ctx'), may hold values from 0.1 to 1
Outputs:
- query_grad: bfloat16 [1024, 6144], P('ctx', 'exp')
- key_grad: bfloat16 [1024, 6144], P('ctx', 'exp')
- value_grad: bfloat16 [1024, 6144], P('ctx', 'exp')
The draws below stay inside these ranges and needn't reach their ends.
Inputs may be any that keep to these rules, and one draw needn't show every extreme that they name: `routes`: in each aligned block of 128 tokens a token's two experts differ and no expert is named by more than 72 tokens; in every draw some expert is named by exactly 72 tokens of some block.
All inputs are finite; a program needn't handle non-finite values.
Results may differ from the reference program's by a relative error of at most 0.0117.
Values may be sent and summed in bfloat16 or wider, within the bound.
No kernel may reach another device: no remote copies, remote signals or barrier semaphores. Data moves between devices by JAX's collectives and lax.ppermute only.
A program may use at most 128 MiB of HBM per device.

```python
import math
import jax
import jax.numpy as jnp
import numpy as np
from jax import lax

H = 48
DH = 128
D = 6144
FF = 4608
TOK_CTX = 128
TOKENS = 1024
EXPERTS = 4
CAP = 72
N_CTX = 8
N_EXP = 4


def draw_decay_rates(key, part):
    pick_key = jax.random.fold_in(key, 11)
    slow_key = jax.random.fold_in(key, 12)
    fast_key = jax.random.fold_in(key, 13)
    fast_share = 0.5
    slow_low = 0.2 / TOKENS
    slow_high = 2.0 / TOKENS
    slow_rates = jnp.exp(jax.random.uniform(slow_key, (H,), jnp.float32, minval=math.log(slow_low), maxval=math.log(slow_high)))
    fast_rates = jnp.exp(jax.random.uniform(fast_key, (H,), jnp.float32, minval=math.log(1.0 / 50.0), maxval=math.log(1.0 / 30.0)))
    chosen = jax.random.uniform(pick_key, (H,), jnp.float32) < fast_share
    return jnp.where(chosen, fast_rates, slow_rates).astype(jnp.float32)


def level_of(key, dims, split, smallest, largest):
    gain, own = 1.0, jax.random.fold_in(key, 6)
    for dim, parts in split:
        heights = jnp.exp(jax.random.uniform(jax.random.fold_in(own, dim), (parts,), jnp.float32, smallest / len(split), largest / len(split)))
        gain = gain * jnp.repeat(heights, dims[dim] // parts).reshape([-1 if axis == dim else 1 for axis in range(len(dims))])
    return gain


def routed_block(stream_key, own, number, rows, amount, top, limit, lean):
    sequence = jax.random.permutation(stream_key, amount)
    packed, ordinary = portions_of(amount, rows * top, limit, lean, True), portions_of(amount, rows * top, limit, lean, False)
    places = jnp.arange(amount)

    def named(lengths, offset_by):
        used = int((lengths > 0).sum())
        fixed = max(1, used // 4)
        shifted = fixed + (places - fixed + offset_by * (used - fixed)) % max(1, amount - fixed)
        return jnp.zeros((amount,), jnp.int32).at[sequence[jnp.where(places < fixed, places, shifted)]].set(jnp.asarray(lengths, jnp.int32))

    lengths = jnp.where(number % 4 == 0, named(packed, number // 4), named(ordinary, number - number // 4 - 1))
    mixed = jax.random.permutation(jax.random.fold_in(own, 3), amount)
    donor, taker = mixed[0:amount // 2 * 2:2], mixed[1:amount // 2 * 2:2]
    slack = jnp.minimum(lengths[donor] - 1, limit - lengths[taker]) // 2
    slack = jnp.where((donor == sequence[0]) | (taker == sequence[0]) | (lengths[taker] == 0), 0, jnp.maximum(slack, 0))
    shifted = jax.random.randint(jax.random.fold_in(own, 4), (amount // 2,), 0, 1 << 20) % (slack + 1)
    lengths = lengths.at[donor].add(-shifted).at[taker].add(shifted)
    labels = jnp.searchsorted(jnp.cumsum(lengths), jnp.arange(rows * top), side="right").astype(jnp.int32)
    listing = labels.reshape(top, rows).T
    listing = listing[jax.random.permutation(jax.random.fold_in(own, 1), rows)]
    offset_by = jax.random.randint(jax.random.fold_in(own, 2), (rows, 1), 0, top)
    return jnp.take_along_axis(listing, (jnp.arange(top)[None, :] + offset_by) % top, axis=1)


def portions_of(amount, total, limit, skew, full):
    loads = [(1 << 20) // math.isqrt(grade ** skew) + 1 for grade in range(1, amount + 1)]
    largest = limit if full else min(limit, max(-(-total // amount), total * loads[0] // sum(loads)))
    least = 1 if total - largest >= amount - 1 else 0
    given, rest = [largest] + [least] * (amount - 1), total - largest - least * (amount - 1)
    while rest > 0:
        candidates = [i for i in range(1, amount) if given[i] < largest] or [i for i in range(1, amount) if given[i] < limit]
        whole, budget = sum([loads[i] for i in candidates]), rest
        for i in candidates:
            addition = min(limit - given[i], max(1, budget * loads[i] // whole), rest)
            given[i] = given[i] + addition
            rest = rest - addition
    return np.array(given)


def scatter_about(stream_key, shape, spread, limit, split=(), kind=jnp.bfloat16):
    entries = spread * jax.random.normal(stream_key, shape, jnp.float32)
    if split:
        entries = entries * level_of(stream_key, shape, split, -0.22, 0.18)
    return jnp.clip(entries, -limit, limit).astype(kind)


def setup_inputs(seed: int = 0) -> dict:
    streams_of = jax.random.split(jax.random.key(seed), 10)
    queries = scatter_about(streams_of[0], (TOKENS, D), 1.0, 6.0, ((0, 8), (1, 4)))
    keys = scatter_about(streams_of[1], (TOKENS, D), 1.0, 6.0, ((0, 8), (1, 4)))
    values = scatter_about(streams_of[2], (TOKENS, D), 1.0, 6.0, ((0, 8), (1, 4)))
    out_grad = scatter_about(streams_of[3], (TOKENS, D), 1.0, 6.0, ((0, 8), (1, 4)))
    up_weight = scatter_about(streams_of[4], (2 * EXPERTS, D, FF // 2), D ** -0.5, 0.078125, ((0, 8), (1, 4)))
    down_weight = scatter_about(streams_of[5], (2 * EXPERTS, FF // 2, D), FF ** -0.5, 0.09375, ((0, 8), (2, 4)))
    decay_rates = draw_decay_rates(jax.random.fold_in(streams_of[9], 71), 0)
    routes_keys = jax.random.split(jax.random.fold_in(streams_of[7], 1), TOKENS // TOK_CTX)
    routes_turns = jax.random.permutation(jax.random.fold_in(streams_of[7], 3), TOKENS // TOK_CTX)
    routes = jax.vmap(lambda own, number: routed_block(jax.random.fold_in(streams_of[7], 2), own, number, TOK_CTX, EXPERTS, 2, CAP, 2))(routes_keys, routes_turns).reshape((TOKENS, 2))
    gate_weights = jnp.clip(0.1 + 0.9 * jax.random.uniform(streams_of[8], (TOKENS, 2), jnp.float32) ** level_of(streams_of[8], (TOKENS, 2), ((0, 8),), -0.2, 0.2), 0.1, 1.0)
    return dict(queries=queries, keys=keys, values=values, out_grad=out_grad, up_weight=up_weight, down_weight=down_weight, decay_rates=decay_rates, routes=routes, gate_weights=gate_weights)


HIGHEST = lax.Precision.HIGHEST

def silu_slope(value):
    sigma = jax.nn.sigmoid(value)
    return sigma * (1.0 + value * (1.0 - sigma))

def decay_tables(rates, block_len):
    offsets = jnp.arange(block_len).astype(jnp.float32)
    distance = offsets[:, None] - offsets[None, :]
    within = jnp.where(distance[None] >= 0.0, jnp.exp(-rates[:, None, None] * jnp.maximum(distance, 0.0)[None]), 0.0)
    start_pow = jnp.exp(-rates[None, :] * offsets[:, None])
    end_pow = jnp.exp(-rates[None, :] * (block_len - offsets)[:, None])
    last_pow = jnp.exp(-rates[None, :] * (block_len - 1.0 - offsets)[:, None])
    next_pow = jnp.exp(-rates[None, :] * (offsets + 1.0)[:, None])
    whole_pow = jnp.exp(-rates * block_len)
    return (within, start_pow, end_pow, last_pow, next_pow, whole_pow)

def slot_tables(route_block, gate_block, experts, capacity):
    flat = route_block.reshape(-1).astype(jnp.int32)
    hits = (flat[:, None] == jnp.arange(experts, dtype=jnp.int32)[None, :]).astype(jnp.int32)
    before = jnp.cumsum(hits, axis=0) - hits
    placed = lax.optimization_barrier(jnp.sum(before * hits, axis=1))
    target = flat * capacity + placed
    match = (target[None, :] == jnp.arange(experts * capacity, dtype=jnp.int32)[:, None]).astype(jnp.float32)
    match = match.reshape(experts * capacity, route_block.shape[0], route_block.shape[1])
    return (lax.optimization_barrier(jnp.sum(match, axis=2)), lax.optimization_barrier(jnp.sum(match * gate_block[None].astype(jnp.float32), axis=2)))

def reference(queries, keys, values, out_grad, up_weight, down_weight, decay_rates, routes, gate_weights):
    scale = 1.0 / DH
    blocks = N_CTX
    block_len = TOK_CTX
    group = D // N_EXP
    half_ff = FF // 2
    within, start_pow, end_pow, last_pow, next_pow, whole_pow = decay_tables(decay_rates, block_len)

    def blocked(array):
        return array.reshape(blocks, block_len, H, DH)

    def forward_step(state, items):
        query_blk, key_blk, value_blk = items
        query_wide = query_blk.astype(jnp.float32)
        key_wide = key_blk.astype(jnp.float32)
        value_wide = value_blk.astype(jnp.float32)
        scores = jnp.einsum('ihd,jhd->hij', query_wide, key_wide)
        weights = (scale * scores * within).astype(jnp.bfloat16)
        intra = jnp.einsum('hij,jhd->ihd', weights.astype(jnp.float32), value_wide)
        inter = scale * start_pow[:, :, None] * jnp.einsum('ihd,hde->ihe', query_wide, state, precision=HIGHEST)
        local = jnp.einsum('ihd,ihe->hde', key_wide * end_pow[:, :, None], value_wide, precision=HIGHEST)
        return (whole_pow[:, None, None] * state + local, ((intra + inter).astype(jnp.bfloat16), state))
    zero_state = jnp.zeros((H, DH, DH), jnp.float32)
    unused, (attn_out, entering) = lax.scan(forward_step, zero_state, (blocked(queries), blocked(keys), blocked(values)))
    choose, weigh = jax.vmap(lambda route_block, gate_block: slot_tables(route_block, gate_block, EXPERTS, CAP))(routes.reshape(blocks, block_len, 2), gate_weights.reshape(blocks, block_len, 2))

    def gather_rows(rows):
        buffer = jnp.einsum('bsl,bld->bsd', choose, rows.reshape(blocks, block_len, D).astype(jnp.float32))
        buffer = buffer.astype(jnp.bfloat16).reshape(blocks, EXPERTS, CAP, D)
        return buffer.transpose(1, 0, 2, 3).reshape(EXPERTS, blocks * CAP, D)

    def expert_grad(items):
        in_rows, grad_rows, up_pair, down_pair = items
        total = jnp.zeros((in_rows.shape[0], D), jnp.float32)
        for half in range(2):
            pre = jnp.zeros((in_rows.shape[0], half_ff), jnp.float32)
            hidden_grad = jnp.zeros((in_rows.shape[0], half_ff), jnp.float32)
            for part in range(N_EXP):
                lower = part * group
                upper = lower + group
                term = jnp.dot(in_rows[:, lower:upper], up_pair[half, lower:upper, :], preferred_element_type=jnp.float32)
                pre = pre + lax.optimization_barrier(term.astype(jnp.bfloat16)).astype(jnp.float32)
                other = lax.dot_general(grad_rows[:, lower:upper], down_pair[half, :, lower:upper], (((1,), (1,)), ((), ())), preferred_element_type=jnp.float32)
                hidden_grad = hidden_grad + lax.optimization_barrier(other.astype(jnp.bfloat16)).astype(jnp.float32)
            slope = (hidden_grad * silu_slope(pre)).astype(jnp.bfloat16)
            back = lax.dot_general(slope, up_pair[half], (((1,), (1,)), ((), ())), preferred_element_type=jnp.float32)
            total = total + lax.optimization_barrier(back.astype(jnp.bfloat16)).astype(jnp.float32)
        return total
    expert_out = lax.map(expert_grad, (gather_rows(attn_out), gather_rows(out_grad), up_weight.reshape(EXPERTS, 2, D, half_ff), down_weight.reshape(EXPERTS, 2, half_ff, D)))
    expert_out = expert_out.reshape(EXPERTS, blocks, CAP, D).transpose(1, 0, 2, 3).reshape(blocks, EXPERTS * CAP, D)
    moe_grad = jnp.einsum('bsl,bsd->bld', weigh, expert_out, precision=HIGHEST).reshape(TOKENS, D)
    grad_out = (out_grad.astype(jnp.float32) + moe_grad).astype(jnp.bfloat16)

    def backward_step(state, items):
        query_blk, key_blk, value_blk, grad_blk, ahead = items
        query_wide = query_blk.astype(jnp.float32)
        key_wide = key_blk.astype(jnp.float32)
        value_wide = value_blk.astype(jnp.float32)
        grad_wide = grad_blk.astype(jnp.float32)
        scores = jnp.einsum('ihd,jhd->hij', query_wide, key_wide)
        weights = (scale * scores * within).astype(jnp.bfloat16).astype(jnp.float32)
        dscores = jnp.einsum('ihd,jhd->hij', grad_wide, value_wide)
        dweights = (scale * dscores * within).astype(jnp.bfloat16).astype(jnp.float32)
        query_g = jnp.einsum('hij,jhd->ihd', dweights, key_wide) + scale * start_pow[:, :, None] * jnp.einsum('ihe,hde->ihd', grad_wide, ahead, precision=HIGHEST)
        key_g = jnp.einsum('hij,ihd->jhd', dweights, query_wide) + scale * last_pow[:, :, None] * jnp.einsum('jhe,hde->jhd', value_wide, state, precision=HIGHEST)
        value_g = jnp.einsum('hij,ihd->jhd', weights, grad_wide) + scale * last_pow[:, :, None] * jnp.einsum('jhd,hde->jhe', key_wide, state, precision=HIGHEST)
        local = jnp.einsum('ihd,ihe->hde', query_wide * next_pow[:, :, None], grad_wide, precision=HIGHEST)
        outs = (query_g.astype(jnp.bfloat16), key_g.astype(jnp.bfloat16), value_g.astype(jnp.bfloat16))
        return (whole_pow[:, None, None] * state + local, outs)
    unused_end, (query_grad, key_grad, value_grad) = lax.scan(backward_step, zero_state, (blocked(queries), blocked(keys), blocked(values), blocked(grad_out), entering), reverse=True)
    return (query_grad.reshape(TOKENS, D), key_grad.reshape(TOKENS, D), value_grad.reshape(TOKENS, D))
```

```python
import functools

import jax
import jax.numpy as jnp
from jax import lax
from jax.experimental import pallas as pl
from jax.experimental.pallas import tpu as pltpu
from jax.sharding import PartitionSpec as P

DH = 128
F32 = jnp.float32
BF16 = jnp.bfloat16
SCALE = 1.0 / DH

SMEM = pl.BlockSpec(memory_space=pltpu.SMEM)
VMEM = pl.BlockSpec(memory_space=pltpu.VMEM)


def dot(left, right, left_dim, right_dim):
    return lax.dot_general(
        left, right, (((left_dim,), (right_dim,)), ((), ())), preferred_element_type=F32
    )


def silu_slope(value):
    sigma = jax.nn.sigmoid(value)
    return sigma * (1.0 + value * (1.0 - sigma))


def lanes_of(place_ref, slot, heads):
    head = lax.rem(place_ref[0] * (heads // 2) + slot, heads)
    return head, pl.ds(pl.multiple_of(head * DH, DH), DH)


def column(block_len):
    return lax.broadcasted_iota(jnp.int32, (block_len, 1), 0).astype(F32)


def decay_within(rate, block_len):
    rows = lax.broadcasted_iota(jnp.int32, (block_len, block_len), 0)
    cols = lax.broadcasted_iota(jnp.int32, (block_len, block_len), 1)
    distance = (rows - cols).astype(F32)
    return jnp.where(distance >= 0.0, jnp.exp(-rate * jnp.maximum(distance, 0.0)), 0.0)


def key_state_kernel(place_ref, rates_ref, k_ref, v_ref, state_ref):
    block_len, heads = k_ref.shape[0], state_ref.shape[0]
    steps = column(block_len)
    for slot in range(heads):
        head, lanes = lanes_of(place_ref, slot, heads)
        power = jnp.exp(-rates_ref[head] * (block_len - steps))
        scaled = (k_ref[:, lanes].astype(F32) * power).astype(BF16)
        state_ref[slot] = dot(scaled, v_ref[:, lanes], 0, 0).astype(BF16)


def route_kernel(place_ref, routes_ref, gates_ref, grad_ref, choose_ref, weigh_ref, *send_refs):
    experts, block_len, capacity = choose_ref.shape
    routes = routes_ref[...]
    gates = gates_ref[...]
    first, second = routes[:, 0:1], routes[:, 1:2]
    wide = lax.broadcasted_iota(jnp.int32, (block_len, 128), 1)
    hit_first = jnp.where(wide == first, 1.0, 0.0)
    hit_second = jnp.where(wide == second, 1.0, 0.0)
    rows = lax.broadcasted_iota(jnp.int32, (block_len, block_len), 0)
    cols = lax.broadcasted_iota(jnp.int32, (block_len, block_len), 1)
    earlier = jnp.where(rows > cols, 1.0, 0.0).astype(BF16)
    before = dot(earlier, (hit_first + hit_second).astype(BF16), 1, 0)
    slot_first = jnp.sum(before * hit_first, axis=1, keepdims=True).astype(jnp.int32)
    slot_second = jnp.sum(before * hit_second, axis=1, keepdims=True).astype(jnp.int32)
    slots = lax.broadcasted_iota(jnp.int32, (block_len, capacity), 1)
    for k in range(experts):
        expert = place_ref[1] ^ k
        one = jnp.where((slots == slot_first) & (first == expert), 1.0, 0.0)
        two = jnp.where((slots == slot_second) & (second == expert), 1.0, 0.0)
        choose = (one + two).astype(BF16)
        choose_ref[k] = choose
        weigh_ref[k] = (one * gates[:, 0:1] + two * gates[:, 1:2]).astype(BF16)
        send_refs[k][...] = dot(choose, grad_ref[...], 0, 0).astype(BF16)


def intra_kernel(place_ref, rates_ref, q_ref, k_ref, v_ref, intra_ref, weights_ref):
    block_len, heads = q_ref.shape[0], weights_ref.shape[0]
    for slot in range(heads):
        head, lanes = lanes_of(place_ref, slot, heads)
        within = decay_within(rates_ref[head], block_len)
        scores = dot(q_ref[:, lanes], k_ref[:, lanes], 1, 1)
        weights = (SCALE * scores * within).astype(BF16)
        weights_ref[slot] = weights
        intra_ref[:, lanes] = dot(weights, v_ref[:, lanes], 1, 0)


def joined_state(far_refs, near_refs, slot, half, rate, block_len, use_near):
    far, near = far_refs[slot // half][slot % half], near_refs[slot // half][slot % half]
    whole = jnp.exp(jnp.full((1, DH), -rate * block_len, F32))
    step = jnp.where(use_near, whole, 1.0)
    return far.astype(F32) * step + jnp.where(use_near, near.astype(F32), 0.0)


def attend_kernel(
    place_ref, rates_ref, q_ref, intra_ref, choose_ref, far0, far1, near0, near1, enter_ref, *send_refs
):
    block_len, heads = q_ref.shape[0], enter_ref.shape[0]
    half = heads // 2
    steps = column(block_len)
    for slot in range(heads):
        head, lanes = lanes_of(place_ref, slot, heads)
        rate = rates_ref[head]
        entering = joined_state(
            (far0, far1), (near0, near1), slot, half, rate, block_len, place_ref[0] == 1
        ).astype(BF16)
        enter_ref[slot] = entering
        inter = SCALE * jnp.exp(-rate * steps) * dot(q_ref[:, lanes], entering, 1, 0)
        attn = (intra_ref[:, lanes] + inter).astype(BF16)
        for k in range(len(send_refs)):
            send_refs[k][:, lanes] = dot(choose_ref[k], attn, 0, 0).astype(BF16)


def grad_kernel(place_ref, rates_ref, q_ref, out_grad_ref, weigh_ref, *refs):
    experts = weigh_ref.shape[0]
    home_refs, (grad_ref, state_ref) = refs[:experts], refs[experts:]
    block_len, heads = q_ref.shape[0], state_ref.shape[0]
    steps = column(block_len)
    for slot in range(heads):
        head, lanes = lanes_of(place_ref, slot, heads)
        total = out_grad_ref[:, lanes].astype(F32)
        for k in range(experts):
            total = total + dot(weigh_ref[k], home_refs[k][:, lanes], 1, 0)
        grad = total.astype(BF16)
        grad_ref[:, lanes] = grad
        power = jnp.exp(-rates_ref[head] * (steps + 1.0))
        scaled = (q_ref[:, lanes].astype(F32) * power).astype(BF16)
        state_ref[slot] = dot(scaled, grad, 0, 0).astype(BF16)


def near_kernel(
    place_ref, rates_ref, q_ref, k_ref, v_ref, grad_ref, enter_ref, weights_ref,
    query_ref, key_ref, value_ref,
):
    block_len, heads = q_ref.shape[0], enter_ref.shape[0]
    steps = column(block_len)
    for slot in range(heads):
        head, lanes = lanes_of(place_ref, slot, heads)
        rate = rates_ref[head]
        grad = grad_ref[:, lanes]
        within = decay_within(rate, block_len)
        dweights = (SCALE * dot(grad, v_ref[:, lanes], 1, 1) * within).astype(BF16)
        query = dot(dweights, k_ref[:, lanes], 1, 0)
        query = query + SCALE * jnp.exp(-rate * steps) * dot(grad, enter_ref[slot], 1, 1)
        query_ref[:, lanes] = query.astype(BF16)
        key_ref[:, lanes] = dot(dweights, q_ref[:, lanes], 0, 0)
        value_ref[:, lanes] = dot(weights_ref[slot], grad, 0, 0)


def far_kernel(
    place_ref, rates_ref, k_ref, v_ref, key_near, value_near, far0, far1, near0, near1, key_ref, value_ref
):
    block_len = k_ref.shape[0]
    half = far0.shape[0]
    heads = 2 * half
    steps = column(block_len)
    for slot in range(heads):
        head, lanes = lanes_of(place_ref, slot, heads)
        rate = rates_ref[head]
        leaving = joined_state(
            (far0, far1), (near0, near1), slot, half, rate, block_len, place_ref[0] == 0
        ).astype(BF16)
        power = SCALE * jnp.exp(-rate * (block_len - 1.0 - steps))
        key_ref[:, lanes] = (
            key_near[:, lanes] + power * dot(v_ref[:, lanes], leaving, 1, 1)
        ).astype(BF16)
        value_ref[:, lanes] = (
            value_near[:, lanes] + power * dot(k_ref[:, lanes], leaving, 1, 0)
        ).astype(BF16)


def call(kernel, out_shapes, scalars, arrays, flops):
    size = sum(leaf.size * leaf.dtype.itemsize for leaf in list(arrays) + list(out_shapes))
    return pl.pallas_call(
        kernel,
        out_shape=list(out_shapes),
        in_specs=[SMEM] * len(scalars) + [VMEM] * len(arrays),
        out_specs=[VMEM] * len(out_shapes),
        compiler_params=pltpu.CompilerParams(vmem_limit_bytes=32 * 1024 * 1024),
        cost_estimate=pl.CostEstimate(flops=flops, bytes_accessed=size, transcendentals=0),
    )(*scalars, *arrays)


def swap(array, axis, distance):
    size = lax.axis_size(axis)
    return lax.ppermute(array, axis, [(i, i ^ distance) for i in range(size)])


def to_pair(array, pairs):
    return lax.ppermute(array, "ctx", [(2 * a + s, 2 * b + s) for a, b in pairs for s in (0, 1)])


def scan_states(state, rates, place, block_len, reverse):
    heads = state.shape[0]
    half = heads // 2
    pairs = lax.axis_size("ctx") // 2
    side, pair = place[0], place[1]
    if reverse:
        side, pair = 1 - side, pairs - 1 - pair
    mine = lax.dynamic_slice(rates, (place[0] * half,), (half,))[:, None, None]
    power = lambda tokens: jnp.exp(-mine * tokens)
    partner = swap(state[half:], "ctx", 1)
    first_end = 1 if reverse else 0
    other = lax.ppermute(
        state[:half], "ctx", [(2 * i + first_end, 2 * i + 1 - first_end) for i in range(pairs)]
    )
    whole = power(float(block_len))
    own_wide, partner_wide = state[:half].astype(F32), partner.astype(F32)
    total = jnp.where(
        side == 0, whole * own_wide + partner_wide, own_wide + whole * partner_wide
    ).astype(BF16)
    before = jnp.zeros_like(total)
    reach = 1
    while reach < pairs:
        if reach == 1:
            upto = total
        else:
            upto = (power(2.0 * block_len) * before.astype(F32) + total.astype(F32)).astype(BF16)
        got = []
        for j in range(reach):
            moves = [(g + reach - 1, g + reach + j) for g in range(0, pairs, 2 * reach)]
            if reverse:
                moves = [(pairs - 1 - a, pairs - 1 - b) for a, b in moves]
            got.append(to_pair(upto, moves))
        got = functools.reduce(lambda a, b: a + b, got)
        steps = lax.rem(pair, reach).astype(F32)
        if reach == 1:
            before = got
        else:
            before = (
                before.astype(F32) + power(2.0 * block_len * steps) * got.astype(F32)
            ).astype(BF16)
        reach *= 2
    return before, swap(before, "ctx", 1), partner, other


def to_experts(sends):
    pairs = len(sends)
    got = [sends[0]] + [swap(sends[k], "ctx", 2 * k) for k in range(1, pairs)]
    chunks = []
    for first in (0, pairs // 2):
        own = jnp.concatenate(got[first : first + pairs // 2], axis=0)
        chunks.append(jnp.concatenate([own, swap(own, "ctx", 1)], axis=0))
    return chunks


def scatter_sum(part, bits):
    for bit in range(bits):
        mine = (lax.axis_index("exp") >> bit) & 1
        halves = part.reshape(2, part.shape[0] // 2, part.shape[1])
        got = swap(lax.dynamic_index_in_dim(halves, 1 - mine, 0, False), "exp", 1 << bit)
        kept = lax.dynamic_index_in_dim(halves, mine, 0, False)
        part = kept.astype(F32) + got.astype(F32)
        if bit < bits - 1:
            part = part.astype(BF16)
    return part


def gather_all(part, bits):
    for bit in reversed(range(bits)):
        mine = (lax.axis_index("exp") >> bit) & 1
        got = swap(part, "exp", 1 << bit)
        part = jnp.concatenate(
            [jnp.where(mine == 0, part, got), jnp.where(mine == 0, got, part)], axis=0
        )
    return part


def on_device(
    queries, keys, values, out_grad, up_weight, down_weight, decay_rates, routes, gate_weights
):
    block_len, group = queries.shape
    heads = group // DH
    half = heads // 2
    experts = lax.axis_size("ctx") // 2
    bits = (lax.axis_size("exp") - 1).bit_length()
    capacity = block_len * 9 // (4 * experts)
    position = lax.axis_index("ctx").astype(jnp.int32)
    place = jnp.stack([position & 1, position >> 1])
    scalars = (place, decay_rates)
    up_local, down_local = up_weight[0], down_weight[0]

    states = jax.ShapeDtypeStruct((heads, DH, DH), BF16)
    weight_sq = jax.ShapeDtypeStruct((heads, block_len, block_len), BF16)
    wide = jax.ShapeDtypeStruct((block_len, group), F32)
    slim = jax.ShapeDtypeStruct((block_len, group), BF16)
    table = jax.ShapeDtypeStruct((experts, block_len, capacity), BF16)
    slots = jax.ShapeDtypeStruct((capacity, group), BF16)
    unit = 2 * block_len * DH * group

    (key_local,) = call(key_state_kernel, [states], scalars, (keys, values), unit)
    choose, weigh, *send_grad = call(
        route_kernel, [table, table] + [slots] * experts, (place,),
        (routes, gate_weights, out_grad), 3 * unit,
    )
    intra, weights = call(intra_kernel, [wide, weight_sq], scalars, (queries, keys, values), 2 * unit)
    enter_states = scan_states(key_local, decay_rates, place, block_len, False)
    entering, *send_in = call(
        attend_kernel, [states] + [slots] * experts, scalars,
        (queries, intra, choose) + enter_states, 4 * unit,
    )

    grad_chunks = to_experts(send_grad)
    in_chunks = to_experts(send_in)
    homes = []
    for in_rows, grad_rows in zip(in_chunks, grad_chunks):
        grad_part = dot(grad_rows, down_local, 1, 1).astype(BF16)
        hidden_grad = scatter_sum(grad_part, bits)
        pre_part = dot(in_rows, up_local, 1, 0).astype(BF16)
        pre = scatter_sum(pre_part, bits)
        slope = (hidden_grad * silu_slope(pre)).astype(BF16)
        slope = gather_all(slope, bits)
        back = dot(slope, up_local, 1, 1).astype(BF16)
        kept = back.shape[0] // 2
        got = swap(back[kept:], "ctx", 1)
        summed = (back[:kept].astype(F32) + got.astype(F32)).astype(BF16)
        for i in range(experts // 2):
            rows = summed[i * capacity : (i + 1) * capacity]
            k = len(homes)
            homes.append(swap(rows, "ctx", 2 * k) if k else rows)

    grad_out, query_local = call(
        grad_kernel, [slim, states], scalars, (queries, out_grad, weigh, *homes), 4 * unit
    )
    leave_states = scan_states(query_local, decay_rates, place, block_len, True)
    query_g, key_near, value_near = call(
        near_kernel, [slim, wide, wide], scalars,
        (queries, keys, values, grad_out, entering, weights), 5 * unit,
    )
    key_g, value_g = call(
        far_kernel, [slim, slim], scalars,
        (keys, values, key_near, value_near) + leave_states, 2 * unit,
    )
    return query_g, key_g, value_g


def solution(mesh):
    placed = (
        P("ctx", "exp"),
        P("ctx", "exp"),
        P("ctx", "exp"),
        P("ctx", "exp"),
        P("ctx", "exp", None),
        P("ctx", None, "exp"),
        P("exp"),
        P("ctx", None),
        P("ctx", None),
    )
    return jax.shard_map(
        on_device,
        mesh=mesh,
        in_specs=placed,
        out_specs=(P("ctx", "exp"), P("ctx", "exp"), P("ctx", "exp")),
        check_vma=False,
    )
```

```python
import functools

import jax
import jax.numpy as jnp
from jax import lax
from jax.experimental import pallas as pl
from jax.experimental.pallas import tpu as pltpu
from jax.sharding import PartitionSpec as P

DH = 128
F32 = jnp.float32
BF16 = jnp.bfloat16
SCALE = 1.0 / DH

SMEM = pl.BlockSpec(memory_space=pltpu.SMEM)
VMEM = pl.BlockSpec(memory_space=pltpu.VMEM)


def dot(left, right, left_dim, right_dim):
    return lax.dot_general(
        left, right, (((left_dim,), (right_dim,)), ((), ())), preferred_element_type=F32
    )


def silu_slope(value):
    sigma = jax.nn.sigmoid(value)
    return sigma * (1.0 + value * (1.0 - sigma))


def lanes_of(place_ref, slot, heads):
    head = lax.rem(place_ref[0] * (heads // 2) + slot, heads)
    return head, pl.ds(pl.multiple_of(head * DH, DH), DH)


def column(block_len):
    return lax.broadcasted_iota(jnp.int32, (block_len, 1), 0).astype(F32)


def decay_within(rate, block_len):
    rows = lax.broadcasted_iota(jnp.int32, (block_len, block_len), 0)
    cols = lax.broadcasted_iota(jnp.int32, (block_len, block_len), 1)
    distance = (rows - cols).astype(F32)
    return jnp.where(distance >= 0.0, jnp.exp(-rate * jnp.maximum(distance, 0.0)), 0.0)


def key_state_kernel(place_ref, rates_ref, k_ref, v_ref, state_ref):
    block_len, heads = k_ref.shape[0], state_ref.shape[0]
    steps = column(block_len)
    for slot in range(heads):
        head, lanes = lanes_of(place_ref, slot, heads)
        power = jnp.exp(-rates_ref[head] * (block_len - steps))
        scaled = (k_ref[:, lanes].astype(F32) * power).astype(BF16)
        state_ref[slot] = dot(scaled, v_ref[:, lanes], 0, 0).astype(BF16)


def route_kernel(place_ref, routes_ref, gates_ref, grad_ref, choose_ref, weigh_ref, *send_refs):
    experts, block_len, capacity = choose_ref.shape
    routes = routes_ref[...]
    gates = gates_ref[...]
    first, second = routes[:, 0:1], routes[:, 1:2]
    wide = lax.broadcasted_iota(jnp.int32, (block_len, 128), 1)
    hit_first = jnp.where(wide == first, 1.0, 0.0)
    hit_second = jnp.where(wide == second, 1.0, 0.0)
    rows = lax.broadcasted_iota(jnp.int32, (block_len, block_len), 0)
    cols = lax.broadcasted_iota(jnp.int32, (block_len, block_len), 1)
    earlier = jnp.where(rows > cols, 1.0, 0.0).astype(BF16)
    before = dot(earlier, (hit_first + hit_second).astype(BF16), 1, 0)
    slot_first = jnp.sum(before * hit_first, axis=1, keepdims=True).astype(jnp.int32)
    slot_second = jnp.sum(before * hit_second, axis=1, keepdims=True).astype(jnp.int32)
    slots = lax.broadcasted_iota(jnp.int32, (block_len, capacity), 1)
    for k in range(experts):
        expert = place_ref[1] ^ k
        one = jnp.where((slots == slot_first) & (first == expert), 1.0, 0.0)
        two = jnp.where((slots == slot_second) & (second == expert), 1.0, 0.0)
        choose = (one + two).astype(BF16)
        choose_ref[k] = choose
        weigh_ref[k] = (one * gates[:, 0:1] + two * gates[:, 1:2]).astype(BF16)
        send_refs[k][...] = dot(choose, grad_ref[...], 0, 0).astype(BF16)


def intra_kernel(place_ref, rates_ref, q_ref, k_ref, v_ref, intra_ref, weights_ref):
    block_len, heads = q_ref.shape[0], weights_ref.shape[0]
    for slot in range(heads):
        head, lanes = lanes_of(place_ref, slot, heads)
        within = decay_within(rates_ref[head], block_len)
        scores = dot(q_ref[:, lanes], k_ref[:, lanes], 1, 1)
        weights = (SCALE * scores * within).astype(BF16)
        weights_ref[slot] = weights
        intra_ref[:, lanes] = dot(weights, v_ref[:, lanes], 1, 0)


def joined_state(far_refs, near_refs, slot, half, rate, block_len, use_near):
    far, near = far_refs[slot // half][slot % half], near_refs[slot // half][slot % half]
    whole = jnp.exp(jnp.full((1, DH), -rate * block_len, F32))
    step = jnp.where(use_near, whole, 1.0)
    return far.astype(F32) * step + jnp.where(use_near, near.astype(F32), 0.0)


def attend_kernel(
    place_ref, rates_ref, q_ref, intra_ref, choose_ref, far0, far1, near0, near1, enter_ref, *send_refs
):
    block_len, heads = q_ref.shape[0], enter_ref.shape[0]
    half = heads // 2
    steps = column(block_len)
    for slot in range(heads):
        head, lanes = lanes_of(place_ref, slot, heads)
        rate = rates_ref[head]
        entering = joined_state(
            (far0, far1), (near0, near1), slot, half, rate, block_len, place_ref[0] == 1
        ).astype(BF16)
        enter_ref[slot] = entering
        inter = SCALE * jnp.exp(-rate * steps) * dot(q_ref[:, lanes], entering, 1, 0)
        attn = (intra_ref[:, lanes] + inter).astype(BF16)
        for k in range(len(send_refs)):
            send_refs[k][:, lanes] = dot(choose_ref[k], attn, 0, 0).astype(BF16)


def grad_kernel(place_ref, rates_ref, q_ref, out_grad_ref, weigh_ref, *refs):
    experts = weigh_ref.shape[0]
    home_refs, (grad_ref, state_ref) = refs[:experts], refs[experts:]
    block_len, heads = q_ref.shape[0], state_ref.shape[0]
    steps = column(block_len)
    for slot in range(heads):
        head, lanes = lanes_of(place_ref, slot, heads)
        total = out_grad_ref[:, lanes].astype(F32)
        for k in range(experts):
            total = total + dot(weigh_ref[k], home_refs[k][:, lanes], 1, 0)
        grad = total.astype(BF16)
        grad_ref[:, lanes] = grad
        power = jnp.exp(-rates_ref[head] * (steps + 1.0))
        scaled = (q_ref[:, lanes].astype(F32) * power).astype(BF16)
        state_ref[slot] = dot(scaled, grad, 0, 0).astype(BF16)


def near_kernel(
    place_ref, rates_ref, q_ref, k_ref, v_ref, grad_ref, enter_ref, weights_ref,
    query_ref, key_ref, value_ref,
):
    block_len, heads = q_ref.shape[0], enter_ref.shape[0]
    steps = column(block_len)
    for slot in range(heads):
        head, lanes = lanes_of(place_ref, slot, heads)
        rate = rates_ref[head]
        grad = grad_ref[:, lanes]
        within = decay_within(rate, block_len)
        dweights = (SCALE * dot(grad, v_ref[:, lanes], 1, 1) * within).astype(BF16)
        query = dot(dweights, k_ref[:, lanes], 1, 0)
        query = query + SCALE * jnp.exp(-rate * steps) * dot(grad, enter_ref[slot], 1, 1)
        query_ref[:, lanes] = query.astype(BF16)
        key_ref[:, lanes] = dot(dweights, q_ref[:, lanes], 0, 0)
        value_ref[:, lanes] = dot(weights_ref[slot], grad, 0, 0)


def far_kernel(
    place_ref, rates_ref, k_ref, v_ref, key_near, value_near, far0, far1, near0, near1, key_ref, value_ref
):
    block_len = k_ref.shape[0]
    half = far0.shape[0]
    heads = 2 * half
    steps = column(block_len)
    for slot in range(heads):
        head, lanes = lanes_of(place_ref, slot, heads)
        rate = rates_ref[head]
        leaving = joined_state(
            (far0, far1), (near0, near1), slot, half, rate, block_len, place_ref[0] == 0
        ).astype(BF16)
        power = SCALE * jnp.exp(-rate * (block_len - 1.0 - steps))
        key_ref[:, lanes] = (
            key_near[:, lanes] + power * dot(v_ref[:, lanes], leaving, 1, 1)
        ).astype(BF16)
        value_ref[:, lanes] = (
            value_near[:, lanes] + power * dot(k_ref[:, lanes], leaving, 1, 0)
        ).astype(BF16)


def call(kernel, out_shapes, scalars, arrays, flops):
    size = sum(leaf.size * leaf.dtype.itemsize for leaf in list(arrays) + list(out_shapes))
    return pl.pallas_call(
        kernel,
        out_shape=list(out_shapes),
        in_specs=[SMEM] * len(scalars) + [VMEM] * len(arrays),
        out_specs=[VMEM] * len(out_shapes),
        compiler_params=pltpu.CompilerParams(vmem_limit_bytes=32 * 1024 * 1024),
        cost_estimate=pl.CostEstimate(flops=flops, bytes_accessed=size, transcendentals=0),
    )(*scalars, *arrays)


def swap(array, axis, distance):
    size = lax.axis_size(axis)
    return lax.ppermute(array, axis, [(i, i ^ distance) for i in range(size)])


def trade(array, pairs, partner):
    return lax.ppermute(
        array, "ctx", [(2 * partner(i) + s, 2 * i + s) for i in range(pairs) for s in (0, 1)]
    )


def after(array, *events):
    return lax.optimization_barrier((array,) + events)[0]


def scan_total(state, rates, place, block_len, reverse, *events):
    half = state.shape[0] // 2
    side = 1 - place[0] if reverse else place[0]
    whole = head_power(rates, place, half, block_len)
    partner = after(swap(state[half:], "ctx", 1), *events)
    own_wide, partner_wide = state[:half].astype(F32), partner.astype(F32)
    total = jnp.where(
        side == 0, whole * own_wide + partner_wide, own_wide + whole * partner_wide
    ).astype(BF16)
    return total, partner


def head_power(rates, place, half, tokens):
    mine = lax.dynamic_slice(rates, (place[0] * half,), (half,))[:, None, None]
    return jnp.exp(-mine * tokens)


def scan_step(before, total, reach, rates, place, block_len, reverse, *events):
    half = total.shape[0]
    pairs = lax.axis_size("ctx") // 2
    pair = pairs - 1 - place[1] if reverse else place[1]
    if before is None:
        upto = total
    else:
        whole = head_power(rates, place, half, 2.0 * block_len)
        upto = (whole * before.astype(F32) + total.astype(F32)).astype(BF16)
    upto = after(upto, *events)
    lower, offset = (pair & reach) == 0, pair & (reach - 1)
    got = None
    for j in range(reach):

        def partner(i, j=j):
            i = pairs - 1 - i if reverse else i
            start = i - i % (2 * reach)
            first, second = start + reach - 1, start + reach + j
            i = {first: second, second: first}.get(i, i)
            return pairs - 1 - i if reverse else i

        one = trade(upto, pairs, partner)
        got = one if got is None else jnp.where(offset == j, one, got)
    scale = head_power(rates, place, half, 2.0 * block_len * offset.astype(F32))
    grown = scale * got.astype(F32)
    if before is not None:
        grown = grown + before.astype(F32)
    kept = jnp.zeros_like(total) if before is None else before
    return jnp.where(lower, kept, grown.astype(BF16)), upto


def scatter_part(part, bit):
    mine = (lax.axis_index("exp") >> bit) & 1
    halves = part.reshape(2, part.shape[0] // 2, part.shape[1])
    got = swap(lax.dynamic_index_in_dim(halves, 1 - mine, 0, False), "exp", 1 << bit)
    kept = lax.dynamic_index_in_dim(halves, mine, 0, False)
    return (kept.astype(F32) + got.astype(F32)).astype(BF16)


def scatter_rest(part, bits):
    for bit in range(1, bits):
        part = scatter_part(part, bit)
    return part.astype(F32)


def gather_all(part, bits, *events):
    for bit in reversed(range(bits)):
        mine = (lax.axis_index("exp") >> bit) & 1
        got = swap(part, "exp", 1 << bit)
        if bit == 0:
            got = after(got, *events)
        part = jnp.concatenate(
            [jnp.where(mine == 0, part, got), jnp.where(mine == 0, got, part)], axis=0
        )
    return part


def on_device(
    queries, keys, values, out_grad, up_weight, down_weight, decay_rates, routes, gate_weights
):
    block_len, group = queries.shape
    heads = group // DH
    half = heads // 2
    experts = lax.axis_size("ctx") // 2
    bits = (lax.axis_size("exp") - 1).bit_length()
    capacity = block_len * 9 // (4 * experts)
    position = lax.axis_index("ctx").astype(jnp.int32)
    place = jnp.stack([position & 1, position >> 1])
    scalars = (place, decay_rates)
    up_local, down_local = up_weight[0], down_weight[0]

    states = jax.ShapeDtypeStruct((heads, DH, DH), BF16)
    weight_sq = jax.ShapeDtypeStruct((heads, block_len, block_len), BF16)
    wide = jax.ShapeDtypeStruct((block_len, group), F32)
    slim = jax.ShapeDtypeStruct((block_len, group), BF16)
    table = jax.ShapeDtypeStruct((experts, block_len, capacity), BF16)
    slots = jax.ShapeDtypeStruct((capacity, group), BF16)
    unit = 2 * block_len * DH * group

    reaches = [1 << i for i in range((experts - 1).bit_length())]
    (key_local,) = call(key_state_kernel, [states], scalars, (keys, values), unit)
    choose, weigh, *send_grad = call(
        route_kernel, [table, table] + [slots] * experts, (place,),
        (routes, gate_weights, out_grad), 3 * unit,
    )
    key_total, near0 = scan_total(
        key_local, decay_rates, place, block_len, False, send_grad[0]
    )
    intra, weights = call(intra_kernel, [wide, weight_sq], scalars, (queries, keys, values), 2 * unit)
    near1 = swap(after(key_local[:half], key_total), "ctx", 1)
    half_experts = experts // 2
    pairs_of = lambda rows, k: swap(rows, "ctx", 2 * k) if k else rows

    grad_own, grad_other = {0: send_grad[0]}, {}
    for k in range(half_experts, experts - 1):
        grad_own[k] = pairs_of(send_grad[k], k)
    before = None
    for index, reach in enumerate(reaches):
        events = list(grad_own.values()) if index == 1 else []
        before, upto = scan_step(
            before, key_total, reach, decay_rates, place, block_len, False, *events
        )
        if index == 0:
            grad_other[0] = swap(after(grad_own[0], key_total), "ctx", 1)
    for k in range(half_experts, experts - 1):
        grad_other[k] = swap(after(grad_own[k], upto), "ctx", 1)
    for k in range(1, half_experts):
        grad_own[k] = pairs_of(after(send_grad[k], upto), k)
    before = after(before, grad_other[0], near1, *[grad_own[k] for k in range(1, half_experts)])
    grad_own[experts - 1] = pairs_of(after(send_grad[experts - 1], before), experts - 1)
    far0, far1 = before, swap(before, "ctx", 1)
    far1 = after(far1, *[grad_other[k] for k in range(half_experts, experts - 1)])
    entering, *send_in = call(
        attend_kernel, [states] + [slots] * experts, scalars,
        (queries, intra, choose, far0, far1, near0, near1), 4 * unit,
    )
    for k in [*range(1, half_experts), experts - 1]:
        grad_other[k] = swap(after(grad_own[k], send_in[0]), "ctx", 1)

    in_own, in_other = {0: send_in[0]}, {}
    for k in [experts - 1, *range(1, half_experts)]:
        in_own[k] = pairs_of(send_in[k], k)
    for k in range(half_experts, experts - 1):
        in_own[k] = pairs_of(after(send_in[k], in_own[experts - 1]), k)
    for k in range(experts):
        in_other[k] = swap(in_own[k], "ctx", 1)

    parts = [range(half_experts), range(half_experts, experts)]
    gather = lambda own, other, part: jnp.concatenate(
        [own[k] for k in part] + [other[k] for k in part], axis=0
    )
    hidden = []
    for part in parts:
        rows = gather(grad_own, grad_other, part)
        if not hidden:
            rows = after(rows, in_other[0])
        hidden.append(scatter_part(dot(rows, down_local, 1, 1).astype(BF16), 0))
    rows = after(gather(in_own, in_other, parts[0]), *hidden)
    pre = [scatter_part(dot(rows, up_local, 1, 0).astype(BF16), 0)]
    hidden = [scatter_rest(rows, bits) for rows in hidden]
    rows = after(gather(in_own, in_other, parts[1]), hidden[0], pre[0])
    pre.append(scatter_part(dot(rows, up_local, 1, 0).astype(BF16), 0))
    pre = [scatter_rest(rows, bits) for rows in pre]
    slopes = [(h * silu_slope(p)).astype(BF16) for h, p in zip(hidden, pre)]
    homes = {}
    slopes = lax.optimization_barrier(slopes)
    backs = []
    for part, slope in zip(parts[::-1], slopes[::-1]):
        back = dot(gather_all(slope, bits, *backs), up_local, 1, 1).astype(BF16)
        backs.append(back)
        back = back.reshape(2, len(part), capacity, group)
        events = []
        for i in reversed(range(len(part))):
            got = after(swap(back[1, i], "ctx", 1), *events)
            summed = (back[0, i].astype(F32) + got.astype(F32)).astype(BF16)
            events = [summed]
            homes[part[i]] = pairs_of(summed, part[i])

    grad_out, query_local = call(
        grad_kernel, [slim, states], scalars,
        (queries, out_grad, weigh, *[homes[k] for k in range(experts)]), 4 * unit,
    )
    query_total, near0 = scan_total(query_local, decay_rates, place, block_len, True)
    near1 = swap(after(query_local[:half], query_total), "ctx", 1)
    before = None
    for reach in reaches:
        before, _ = scan_step(before, query_total, reach, decay_rates, place, block_len, True)
    far0, far1 = before, swap(before, "ctx", 1)
    query_g, key_near, value_near = call(
        near_kernel, [slim, wide, wide], scalars,
        (queries, keys, values, grad_out, entering, weights), 5 * unit,
    )
    key_g, value_g = call(
        far_kernel, [slim, slim], scalars,
        (keys, values, key_near, value_near, far0, far1, near0, near1), 2 * unit,
    )
    return query_g, key_g, value_g


def solution(mesh):
    placed = (
        P("ctx", "exp"),
        P("ctx", "exp"),
        P("ctx", "exp"),
        P("ctx", "exp"),
        P("ctx", "exp", None),
        P("ctx", None, "exp"),
        P("exp"),
        P("ctx", None),
        P("ctx", None),
    )
    return jax.shard_map(
        on_device,
        mesh=mesh,
        in_specs=placed,
        out_specs=(P("ctx", "exp"), P("ctx", "exp"), P("ctx", "exp")),
        check_vma=False,
    )
```

```python
import functools

import jax
import jax.numpy as jnp
from jax import lax
from jax.experimental import pallas as pl
from jax.experimental.pallas import tpu as pltpu
from jax.sharding import PartitionSpec as P

DH = 128
F32 = jnp.float32
BF16 = jnp.bfloat16
SCALE = 1.0 / DH

SMEM = pl.BlockSpec(memory_space=pltpu.SMEM)
VMEM = pl.BlockSpec(memory_space=pltpu.VMEM)


def dot(left, right, left_dim, right_dim):
    return lax.dot_general(
        left, right, (((left_dim,), (right_dim,)), ((), ())), preferred_element_type=F32
    )


def silu_slope(value):
    sigma = jax.nn.sigmoid(value)
    return sigma * (1.0 + value * (1.0 - sigma))


def lanes_of(place_ref, slot, heads):
    head = lax.rem(place_ref[0] * (heads // 2) + slot, heads)
    return head, pl.ds(pl.multiple_of(head * DH, DH), DH)


def column(block_len):
    return lax.broadcasted_iota(jnp.int32, (block_len, 1), 0).astype(F32)


def decay_within(rate, block_len):
    rows = lax.broadcasted_iota(jnp.int32, (block_len, block_len), 0)
    cols = lax.broadcasted_iota(jnp.int32, (block_len, block_len), 1)
    distance = (rows - cols).astype(F32)
    return jnp.where(distance >= 0.0, jnp.exp(-rate * jnp.maximum(distance, 0.0)), 0.0)


def key_state_kernel(place_ref, rates_ref, k_ref, v_ref, mine_ref, other_ref):
    block_len, half = k_ref.shape[0], mine_ref.shape[0]
    steps = column(block_len)
    for slot in [*range(half, 2 * half), *range(half)]:
        head, lanes = lanes_of(place_ref, slot, 2 * half)
        power = jnp.exp(-rates_ref[head] * (block_len - steps))
        scaled = (k_ref[:, lanes].astype(F32) * power).astype(BF16)
        state_ref = (mine_ref, other_ref)[slot // half]
        state_ref[slot % half] = dot(scaled, v_ref[:, lanes], 0, 0).astype(BF16)


def pick_rows(choose_ref, rows, send_refs):
    capacity = choose_ref.shape[1]
    if capacity % 8:
        for k, send_ref in enumerate(send_refs):
            send_ref[...] = dot(choose_ref[k], rows, 1, 0).astype(BF16)
        return
    table = choose_ref[...].reshape(len(send_refs) * capacity, rows.shape[0])
    picked = dot(table.astype(BF16), rows, 1, 0)
    for k, send_ref in enumerate(send_refs):
        send_ref[...] = picked[k * capacity : (k + 1) * capacity].astype(BF16)


def route_kernel(
    order, place_ref, routes_ref, turned_ref, gates_ref, grad_ref, choose_ref, weigh_ref, *send_refs
):
    experts, capacity, block_len = choose_ref.shape
    rows = lax.broadcasted_iota(jnp.int32, (block_len, block_len), 0)
    cols = lax.broadcasted_iota(jnp.int32, (block_len, block_len), 1)

    first, second = turned_ref[0:1, :], turned_ref[1:2, :]
    names = lax.broadcasted_iota(jnp.int32, (32, block_len), 0)
    hit_first = jnp.where(names == first, 1.0, 0.0)
    hit_second = jnp.where(names == second, 1.0, 0.0)
    earlier = jnp.where(rows < cols, 1.0, 0.0).astype(BF16)
    before = dot((hit_first + hit_second).astype(BF16), earlier, 1, 0)
    slot_first = jnp.sum(before * hit_first, axis=0, keepdims=True).astype(jnp.int32)
    slot_second = jnp.sum(before * hit_second, axis=0, keepdims=True).astype(jnp.int32)
    slots = lax.broadcasted_iota(jnp.int32, (capacity, block_len), 0)
    for k in range(experts):
        expert = place_ref[1] ^ k
        named = ((slots == slot_first) & (first == expert)) | (
            (slots == slot_second) & (second == expert)
        )
        choose_ref[k] = jnp.where(named, 1.0, 0.0)
    pick_rows(choose_ref, grad_ref[...], send_refs)

    first, second = routes_ref[:, 0:1], routes_ref[:, 1:2]
    names = lax.broadcasted_iota(jnp.int32, (block_len, 128), 1)
    hit_first = jnp.where(names == first, 1.0, 0.0)
    hit_second = jnp.where(names == second, 1.0, 0.0)
    earlier = jnp.where(rows > cols, 1.0, 0.0).astype(BF16)
    before = dot(earlier, (hit_first + hit_second).astype(BF16), 1, 0)
    slot_first = jnp.sum(before * hit_first, axis=1, keepdims=True).astype(jnp.int32)
    slot_second = jnp.sum(before * hit_second, axis=1, keepdims=True).astype(jnp.int32)
    slots = lax.broadcasted_iota(jnp.int32, (block_len, capacity), 1)
    for position, (even, odd) in enumerate(order):
        expert = place_ref[1] ^ jnp.where(place_ref[2] == 0, even, odd)
        one = jnp.where((slots == slot_first) & (first == expert), gates_ref[:, 0:1], 0.0)
        two = jnp.where((slots == slot_second) & (second == expert), gates_ref[:, 1:2], 0.0)
        weigh_ref[position] = (one + two).astype(BF16)


def intra_kernel(place_ref, rates_ref, q_ref, k_ref, v_ref, intra_ref, weights_ref):
    block_len, heads = q_ref.shape[0], weights_ref.shape[0]
    for slot in range(heads):
        head, lanes = lanes_of(place_ref, slot, heads)
        within = decay_within(rates_ref[head], block_len)
        scores = dot(q_ref[:, lanes], k_ref[:, lanes], 1, 1)
        weights = (SCALE * scores * within).astype(BF16)
        weights_ref[slot] = weights
        intra_ref[:, lanes] = dot(weights, v_ref[:, lanes], 1, 0)


def attend_kernel(
    place_ref, rates_ref, q_ref, intra_ref, choose_ref, mine_ref, other_ref, *refs
):
    send_refs, attn_ref = refs[:-1], refs[-1]
    block_len, half = q_ref.shape[0], mine_ref.shape[0]
    steps = column(block_len)
    for slot in range(2 * half):
        head, lanes = lanes_of(place_ref, slot, 2 * half)
        entering = (mine_ref, other_ref)[slot // half][slot % half]
        power = SCALE * jnp.exp(-rates_ref[head] * steps)
        inter = power * dot(q_ref[:, lanes], entering, 1, 0)
        attn_ref[:, lanes] = (intra_ref[:, lanes] + inter).astype(BF16)
    pick_rows(choose_ref, attn_ref[...], send_refs)


def grad_kernel(place_ref, rates_ref, q_ref, out_grad_ref, weigh_ref, *refs):
    experts = weigh_ref.shape[0]
    home_refs, (grad_ref, mine_ref, other_ref) = refs[:experts], refs[experts:]
    block_len, half = q_ref.shape[0], mine_ref.shape[0]
    steps = column(block_len)
    total = out_grad_ref[...].astype(F32)
    for k in range(experts):
        total = total + dot(weigh_ref[k], home_refs[k][...], 1, 0)
    grad_ref[...] = total.astype(BF16)
    for slot in [*range(half, 2 * half), *range(half)]:
        head, lanes = lanes_of(place_ref, slot, 2 * half)
        power = jnp.exp(-rates_ref[head] * (steps + 1.0))
        scaled = (q_ref[:, lanes].astype(F32) * power).astype(BF16)
        state_ref = (mine_ref, other_ref)[slot // half]
        state_ref[slot % half] = dot(scaled, grad_ref[:, lanes], 0, 0).astype(BF16)


def near_kernel(
    place_ref, rates_ref, q_ref, k_ref, v_ref, grad_ref, mine_ref, other_ref, weights_ref,
    query_ref, key_ref, value_ref,
):
    block_len, half = q_ref.shape[0], mine_ref.shape[0]
    steps = column(block_len)
    for slot in range(2 * half):
        head, lanes = lanes_of(place_ref, slot, 2 * half)
        rate = rates_ref[head]
        grad = grad_ref[:, lanes]
        entering = (mine_ref, other_ref)[slot // half][slot % half]
        within = decay_within(rate, block_len)
        dweights = (SCALE * dot(grad, v_ref[:, lanes], 1, 1) * within).astype(BF16)
        query = dot(dweights, k_ref[:, lanes], 1, 0)
        query = query + SCALE * jnp.exp(-rate * steps) * dot(grad, entering, 1, 1)
        query_ref[:, lanes] = query.astype(BF16)
        key_ref[:, lanes] = dot(dweights, q_ref[:, lanes], 0, 0)
        value_ref[:, lanes] = dot(weights_ref[slot], grad, 0, 0)


def far_kernel(
    place_ref, rates_ref, k_ref, v_ref, key_near, value_near, mine_ref, other_ref, key_ref, value_ref
):
    block_len, half = k_ref.shape[0], mine_ref.shape[0]
    steps = column(block_len)
    for slot in range(2 * half):
        head, lanes = lanes_of(place_ref, slot, 2 * half)
        leaving = (mine_ref, other_ref)[slot // half][slot % half]
        power = SCALE * jnp.exp(-rates_ref[head] * (block_len - 1.0 - steps))
        key_ref[:, lanes] = (
            key_near[:, lanes] + power * dot(v_ref[:, lanes], leaving, 1, 1)
        ).astype(BF16)
        value_ref[:, lanes] = (
            value_near[:, lanes] + power * dot(k_ref[:, lanes], leaving, 1, 0)
        ).astype(BF16)


def call(kernel, out_shapes, scalars, arrays, flops, scratch=()):
    size = sum(leaf.size * leaf.dtype.itemsize for leaf in list(arrays) + list(out_shapes))
    return pl.pallas_call(
        kernel,
        out_shape=list(out_shapes),
        in_specs=[SMEM] * len(scalars) + [VMEM] * len(arrays),
        out_specs=[VMEM] * len(out_shapes),
        scratch_shapes=list(scratch),
        compiler_params=pltpu.CompilerParams(vmem_limit_bytes=16 * 1024 * 1024),
        cost_estimate=pl.CostEstimate(flops=flops, bytes_accessed=size, transcendentals=0),
    )(*scalars, *arrays)


def swap(array, axis, distance):
    size = lax.axis_size(axis)
    return lax.ppermute(array, axis, [(i, i ^ distance) for i in range(size)])


def trade(array, pairs, partner):
    return lax.ppermute(
        array, "ctx", [(2 * partner(i) + s, 2 * i + s) for i in range(pairs) for s in (0, 1)]
    )


def after(array, *events):
    return lax.optimization_barrier((array,) + events)[0]


def head_power(rates, place, half, tokens):
    mine = lax.dynamic_slice(rates, (place[0] * half,), (half,))[:, None, None]
    return jnp.exp(-mine * tokens)


def scan_total(mine, other, rates, place, block_len, reverse, *events):
    side = 1 - place[0] if reverse else place[0]
    whole = head_power(rates, place, mine.shape[0], block_len)
    partner = after(swap(other, "ctx", 1), *events)
    first = jnp.where(side == 0, mine, partner).astype(F32)
    second = jnp.where(side == 0, partner, mine).astype(F32)
    return (whole * first + second).astype(BF16), partner


def scan_step(before, total, reach, rates, place, block_len, reverse, *events):
    half = total.shape[0]
    pairs = lax.axis_size("ctx") // 2
    pair = pairs - 1 - place[1] if reverse else place[1]
    if before is None:
        upto = total
    else:
        whole = head_power(rates, place, half, 2.0 * block_len)
        upto = (whole * before + total.astype(F32)).astype(BF16)
    upto = after(upto, *events)
    lower, offset = (pair & reach) == 0, pair & (reach - 1)
    got = None
    for j in range(reach):

        def partner(i, j=j):
            i = pairs - 1 - i if reverse else i
            start = i - i % (2 * reach)
            first, second = start + reach - 1, start + reach + j
            i = {first: second, second: first}.get(i, i)
            return pairs - 1 - i if reverse else i

        one = trade(upto, pairs, partner)
        got = one if got is None else jnp.where(offset == j, one, got)
    scale = head_power(rates, place, half, 2.0 * block_len * offset.astype(F32))
    grown = scale * got.astype(F32)
    kept = 0.0 if before is None else before
    return jnp.where(lower, kept, kept + grown), upto


def scan_ends(before, mine, partner, rates, place, block_len, reverse):
    side = 1 - place[0] if reverse else place[0]
    whole = head_power(rates, place, mine.shape[0], block_len)
    first = jnp.where(side == 0, mine, partner).astype(F32)
    second_meets = whole * before + first
    keep = jnp.where(side == 0, before, second_meets).astype(BF16)
    give = jnp.where(side == 0, second_meets, before).astype(BF16)
    return keep, give


def split_rows(own, other, part, flag):
    count = len(part) // 2
    blocks = [
        jnp.where(flag == 0, side[part[i]], side[part[count + i]])
        for side in (own, other)
        for i in range(count)
    ]
    return jnp.concatenate(blocks, axis=0)


def sum_over_cores(own, other, part, multiply, *events):
    mine = lax.axis_index("exp") & 1
    sent = multiply(after(split_rows(own, other, part, 1 - mine), *events)).astype(BF16)
    got = swap(sent, "exp", 1)
    kept = multiply(after(split_rows(own, other, part, mine), sent))
    return (kept + got.astype(F32)).astype(BF16)


def sum_over_rest(part, bits):
    for bit in range(1, bits):
        part = (part.astype(F32) + swap(part, "exp", 1 << bit).astype(F32)).astype(BF16)
    return part


def on_device(
    queries, keys, values, out_grad, up_weight, down_weight, decay_rates, routes, gate_weights
):
    block_len, group = queries.shape
    heads = group // DH
    half = heads // 2
    experts = lax.axis_size("ctx") // 2
    bits = (lax.axis_size("exp") - 1).bit_length()
    capacity = block_len * 9 // (4 * experts)
    position = lax.axis_index("ctx").astype(jnp.int32)
    core = lax.axis_index("exp").astype(jnp.int32) & 1
    place = jnp.stack([position & 1, position >> 1, core])
    scalars = (place, decay_rates)
    up_local, down_local = up_weight[0], down_weight[0]
    near_part, far_part = range(experts // 2), range(experts // 2, experts)
    quarter = experts // 4
    order = [(k, k) for k in near_part]
    order += [(far_part[i], far_part[quarter + i]) for i in range(quarter)]
    order += [(far_part[quarter + i], far_part[i]) for i in range(quarter)]

    states = jax.ShapeDtypeStruct((half, DH, DH), BF16)
    weight_sq = jax.ShapeDtypeStruct((heads, block_len, block_len), BF16)
    wide = jax.ShapeDtypeStruct((block_len, group), F32)
    slim = jax.ShapeDtypeStruct((block_len, group), BF16)
    choose_table = jax.ShapeDtypeStruct((experts, capacity, block_len), F32)
    weigh_table = jax.ShapeDtypeStruct((experts, block_len, capacity), BF16)
    slots = jax.ShapeDtypeStruct((capacity, group), BF16)
    unit = 2 * block_len * DH * group

    reaches = [1 << i for i in range((experts - 1).bit_length())]
    pairs_of = lambda rows, k: swap(rows, "ctx", 2 * k) if k else rows

    key_mine, key_other = call(key_state_kernel, [states] * 2, scalars, (keys, values), unit)
    choose, weigh, *send_grad = call(
        functools.partial(route_kernel, order), [choose_table, weigh_table] + [slots] * experts,
        (place,), (routes, routes.T, gate_weights, out_grad), 3 * unit,
    )
    intra, weights = call(intra_kernel, [wide, weight_sq], scalars, (queries, keys, values), 2 * unit)

    grad_own, grad_other = {0: send_grad[0]}, {}
    for k in near_part[1:]:
        grad_own[k] = pairs_of(send_grad[k], k)
    total, partner = scan_total(
        key_mine, key_other, decay_rates, place, block_len, False,
        *[grad_own[k] for k in near_part],
    )
    for k in near_part:
        grad_other[k] = swap(after(grad_own[k], total), "ctx", 1)
    before = None
    for index, reach in enumerate(reaches):
        events = list(grad_other.values()) + [intra] if index == 1 else []
        before, upto = scan_step(
            before, total, reach, decay_rates, place, block_len, False, *events
        )
    keep, give = scan_ends(before, key_mine, partner, decay_rates, place, block_len, False)
    hidden_near = sum_over_cores(
        grad_own, grad_other, near_part, lambda rows: dot(rows, down_local, 1, 1), upto
    )
    give, hidden_near = lax.optimization_barrier((give, hidden_near))
    entering = (keep, swap(give, "ctx", 1))
    for k in far_part:
        grad_own[k] = pairs_of(after(send_grad[k], give), k)
    send_in = call(
        attend_kernel, [slots] * experts, scalars, (queries, intra, choose) + entering, 4 * unit,
        [pltpu.VMEM((block_len, group), BF16)],
    )
    for k in far_part:
        grad_other[k] = swap(after(grad_own[k], send_in[0]), "ctx", 1)

    in_own, in_other = {0: send_in[0]}, {}
    for k in [experts - 1, *near_part[1:]]:
        in_own[k] = pairs_of(send_in[k], k)
    for k in far_part[:-1]:
        in_own[k] = pairs_of(after(send_in[k], in_own[experts - 1]), k)
    for k in range(experts):
        in_other[k] = swap(in_own[k], "ctx", 1)

    by_down = lambda rows: dot(rows, down_local, 1, 1)
    by_up = lambda rows: dot(rows, up_local, 1, 0)
    hidden_near = sum_over_rest(hidden_near, bits)
    hidden_far = sum_over_cores(grad_own, grad_other, far_part, by_down, in_other[0])
    pre_near = sum_over_cores(in_own, in_other, near_part, by_up, hidden_near, hidden_far)
    hidden_far = sum_over_rest(hidden_far, bits)
    pre_far = sum_over_cores(in_own, in_other, far_part, by_up, pre_near)
    pre_near, pre_far = sum_over_rest(pre_near, bits), sum_over_rest(pre_far, bits)

    def returned(pre, hidden, *events):
        slope = (hidden.astype(F32) * silu_slope(pre.astype(F32))).astype(BF16)
        slope = after(slope, *events)
        slopes = (slope, swap(slope, "exp", 1))
        summed = []
        for slope in slopes:
            back = dot(after(slope, *events), up_local, 1, 1).astype(BF16)
            back = back.reshape(2, quarter * capacity, group)
            got = swap(back[1], "ctx", 1)
            events = events + (back,)
            summed.append((back[0], got))
        return summed

    def joined(item, *events):
        kept, got = item
        rows = (kept.astype(F32) + after(got, *events).astype(F32)).astype(BF16)
        return rows, [rows[i * capacity : (i + 1) * capacity] for i in range(quarter)]

    def far_home(rows, kept, i):
        moves = []
        size = lax.axis_size("exp")
        for c in range(2 * experts):
            for e in range(size):
                k = far_part[((e & 1) ^ (0 if kept else 1)) * quarter + i]
                moves.append((c * size + e, (c ^ (2 * k)) * size + e))
        return lax.ppermute(rows, ("ctx", "exp"), moves)

    near_items = returned(pre_near, hidden_near)
    far_items = returned(pre_far, hidden_far, near_items[0][0], near_items[1][0])
    first, near_first = joined(near_items[0])
    second, near_second = joined(near_items[1], first)
    homes = [jnp.where(core == 0, a, b) for a, b in zip(near_first, near_second)]
    homes += [jnp.where(core == 0, b, a) for a, b in zip(near_first, near_second)]
    homes = [pairs_of(rows, k) for k, rows in enumerate(homes)]
    first, far_first = joined(far_items[0])
    second, far_second = joined(far_items[1], first)
    homes += [far_home(rows, True, i) for i, rows in enumerate(far_first)]
    homes += [far_home(rows, False, i) for i, rows in enumerate(far_second)]

    grad_out, query_mine, query_other = call(
        grad_kernel, [slim, states, states], scalars, (queries, out_grad, weigh, *homes), 4 * unit
    )
    total, partner = scan_total(
        query_mine, query_other, decay_rates, place, block_len, True
    )
    before = None
    for reach in reaches:
        before, _ = scan_step(before, total, reach, decay_rates, place, block_len, True)
    keep, give = scan_ends(before, query_mine, partner, decay_rates, place, block_len, True)
    leaving = (keep, swap(give, "ctx", 1))
    query_g, key_near, value_near = call(
        near_kernel, [slim, wide, wide], scalars,
        (queries, keys, values, grad_out) + entering + (weights,), 5 * unit,
    )
    key_g, value_g = call(
        far_kernel, [slim, slim], scalars,
        (keys, values, key_near, value_near) + leaving, 2 * unit,
    )
    return query_g, key_g, value_g


def solution(mesh):
    placed = (
        P("ctx", "exp"),
        P("ctx", "exp"),
        P("ctx", "exp"),
        P("ctx", "exp"),
        P("ctx", "exp", None),
        P("ctx", None, "exp"),
        P("exp"),
        P("ctx", None),
        P("ctx", None),
    )
    return jax.shard_map(
        on_device,
        mesh=mesh,
        in_specs=placed,
        out_specs=(P("ctx", "exp"), P("ctx", "exp"), P("ctx", "exp")),
        check_vma=False,
    )
```

```python
import functools

import jax
import jax.numpy as jnp
from jax import lax
from jax.experimental import pallas as pl
from jax.experimental.pallas import tpu as pltpu
from jax.sharding import PartitionSpec as P

DH = 128
F32 = jnp.float32
BF16 = jnp.bfloat16
SCALE = 1.0 / DH

SMEM = pl.BlockSpec(memory_space=pltpu.SMEM)
VMEM = pl.BlockSpec(memory_space=pltpu.VMEM)
SMALL = pl.CostEstimate(flops=1, bytes_accessed=1, transcendentals=0)


def dot(left, right, left_dim, right_dim):
    return lax.dot_general(
        left, right, (((left_dim,), (right_dim,)), ((), ())), preferred_element_type=F32
    )


def silu_slope(value):
    sigma = jax.nn.sigmoid(value)
    return sigma * (1.0 + value * (1.0 - sigma))


def lanes_of(place_ref, slot, heads):
    head = lax.rem(place_ref[0] * (heads // 2) + slot, heads)
    return head, pl.ds(pl.multiple_of(head * DH, DH), DH)


def column(block_len):
    return lax.broadcasted_iota(jnp.int32, (block_len, 1), 0).astype(F32)


def decay_within(rate, block_len):
    rows = lax.broadcasted_iota(jnp.int32, (block_len, block_len), 0)
    cols = lax.broadcasted_iota(jnp.int32, (block_len, block_len), 1)
    distance = (rows - cols).astype(F32)
    return jnp.where(distance >= 0.0, jnp.exp(-rate * jnp.maximum(distance, 0.0)), 0.0)


def key_state_kernel(place_ref, rates_ref, k_ref, v_ref, mine_ref, other_ref):
    block_len, half = k_ref.shape[0], mine_ref.shape[0]
    steps = column(block_len)
    for slot in [*range(half, 2 * half), *range(half)]:
        head, lanes = lanes_of(place_ref, slot, 2 * half)
        power = jnp.exp(-rates_ref[head] * (block_len - steps))
        scaled = (k_ref[:, lanes].astype(F32) * power).astype(BF16)
        state_ref = (mine_ref, other_ref)[slot // half]
        state_ref[slot % half] = dot(scaled, v_ref[:, lanes], 0, 0).astype(BF16)


def pick_rows(choose_ref, rows, send_refs):
    capacity = choose_ref.shape[1]
    if capacity % 8:
        for k, send_ref in enumerate(send_refs):
            send_ref[...] = dot(choose_ref[k], rows, 1, 0).astype(BF16)
        return
    table = choose_ref[...].reshape(len(send_refs) * capacity, rows.shape[0])
    picked = dot(table.astype(BF16), rows, 1, 0)
    for k, send_ref in enumerate(send_refs):
        send_ref[...] = picked[k * capacity : (k + 1) * capacity].astype(BF16)


def route_kernel(
    order, place_ref, routes_ref, gates_ref, grad_ref, choose_ref, weigh_ref, *send_refs
):
    experts, capacity, block_len = choose_ref.shape
    rows = lax.broadcasted_iota(jnp.int32, (block_len, block_len), 0)
    cols = lax.broadcasted_iota(jnp.int32, (block_len, block_len), 1)

    first, second = routes_ref[0:1, :], routes_ref[1:2, :]
    names = lax.broadcasted_iota(jnp.int32, (32, block_len), 0)
    hit_first = jnp.where(names == first, 1.0, 0.0)
    hit_second = jnp.where(names == second, 1.0, 0.0)
    earlier = jnp.where(rows < cols, 1.0, 0.0).astype(BF16)
    before = dot((hit_first + hit_second).astype(BF16), earlier, 1, 0)
    slot_first = jnp.sum(before * hit_first, axis=0, keepdims=True).astype(jnp.int32)
    slot_second = jnp.sum(before * hit_second, axis=0, keepdims=True).astype(jnp.int32)
    slots = lax.broadcasted_iota(jnp.int32, (capacity, block_len), 0)
    for k in range(experts):
        expert = place_ref[1] ^ k
        named = ((slots == slot_first) & (first == expert)) | (
            (slots == slot_second) & (second == expert)
        )
        choose_ref[k] = jnp.where(named, 1.0, 0.0)
    pick_rows(choose_ref, grad_ref[...], send_refs)

    columns = jnp.concatenate(
        [first.astype(F32), second.astype(F32), slot_first.astype(F32), slot_second.astype(F32)]
        + [gates_ref[0:1, :], gates_ref[1:2, :]] + [jnp.zeros((2, block_len), F32)],
        axis=0,
    ).T
    first, second, slot_first, slot_second = [
        columns[:, i : i + 1].astype(jnp.int32) for i in range(4)
    ]
    slots = lax.broadcasted_iota(jnp.int32, (block_len, capacity), 1)
    for position, (even, odd) in enumerate(order):
        expert = place_ref[1] ^ jnp.where(place_ref[2] == 0, even, odd)
        one = jnp.where((slots == slot_first) & (first == expert), columns[:, 4:5], 0.0)
        two = jnp.where((slots == slot_second) & (second == expert), columns[:, 5:6], 0.0)
        weigh_ref[position] = (one + two).astype(BF16)


def intra_kernel(place_ref, rates_ref, q_ref, k_ref, v_ref, intra_ref, weights_ref):
    block_len, heads = q_ref.shape[0], weights_ref.shape[0]
    for slot in range(heads):
        head, lanes = lanes_of(place_ref, slot, heads)
        within = decay_within(rates_ref[head], block_len)
        scores = dot(q_ref[:, lanes], k_ref[:, lanes], 1, 1)
        weights = (SCALE * scores * within).astype(BF16)
        weights_ref[slot] = weights
        intra_ref[:, lanes] = dot(weights, v_ref[:, lanes], 1, 0)


def attend_kernel(
    place_ref, rates_ref, q_ref, intra_ref, choose_ref, mine_ref, other_ref, *refs
):
    send_refs, attn_ref = refs[:-1], refs[-1]
    block_len, half = q_ref.shape[0], mine_ref.shape[0]
    steps = column(block_len)
    for slot in range(2 * half):
        head, lanes = lanes_of(place_ref, slot, 2 * half)
        entering = (mine_ref, other_ref)[slot // half][slot % half]
        power = SCALE * jnp.exp(-rates_ref[head] * steps)
        inter = power * dot(q_ref[:, lanes], entering, 1, 0)
        attn_ref[:, lanes] = (intra_ref[:, lanes] + inter).astype(BF16)
    pick_rows(choose_ref, attn_ref[...], send_refs)


def grad_kernel(place_ref, rates_ref, q_ref, out_grad_ref, weigh_ref, *refs):
    experts = weigh_ref.shape[0]
    home_refs, (grad_ref, mine_ref, other_ref) = refs[:experts], refs[experts:]
    block_len, half = q_ref.shape[0], mine_ref.shape[0]
    steps = column(block_len)
    total = out_grad_ref[...].astype(F32)
    for k in range(experts):
        total = total + dot(weigh_ref[k], home_refs[k][...], 1, 0)
    grad_ref[...] = total.astype(BF16)
    for slot in [*range(half, 2 * half), *range(half)]:
        head, lanes = lanes_of(place_ref, slot, 2 * half)
        power = jnp.exp(-rates_ref[head] * (steps + 1.0))
        scaled = (q_ref[:, lanes].astype(F32) * power).astype(BF16)
        state_ref = (mine_ref, other_ref)[slot // half]
        state_ref[slot % half] = dot(scaled, grad_ref[:, lanes], 0, 0).astype(BF16)


def near_kernel(
    place_ref, rates_ref, q_ref, k_ref, v_ref, grad_ref, mine_ref, other_ref, weights_ref,
    query_ref, key_ref, value_ref,
):
    block_len, half = q_ref.shape[0], mine_ref.shape[0]
    steps = column(block_len)
    for slot in range(2 * half):
        head, lanes = lanes_of(place_ref, slot, 2 * half)
        rate = rates_ref[head]
        grad = grad_ref[:, lanes]
        entering = (mine_ref, other_ref)[slot // half][slot % half]
        within = decay_within(rate, block_len)
        dweights = (SCALE * dot(grad, v_ref[:, lanes], 1, 1) * within).astype(BF16)
        query = dot(dweights, k_ref[:, lanes], 1, 0)
        query = query + SCALE * jnp.exp(-rate * steps) * dot(grad, entering, 1, 1)
        query_ref[:, lanes] = query.astype(BF16)
        key_ref[:, lanes] = dot(dweights, q_ref[:, lanes], 0, 0)
        value_ref[:, lanes] = dot(weights_ref[slot], grad, 0, 0)


def far_kernel(
    place_ref, rates_ref, k_ref, v_ref, key_near, value_near, mine_ref, other_ref, key_ref, value_ref
):
    block_len, half = k_ref.shape[0], mine_ref.shape[0]
    steps = column(block_len)
    for slot in range(2 * half):
        head, lanes = lanes_of(place_ref, slot, 2 * half)
        leaving = (mine_ref, other_ref)[slot // half][slot % half]
        power = SCALE * jnp.exp(-rates_ref[head] * (block_len - 1.0 - steps))
        key_ref[:, lanes] = (
            key_near[:, lanes] + power * dot(v_ref[:, lanes], leaving, 1, 1)
        ).astype(BF16)
        value_ref[:, lanes] = (
            value_near[:, lanes] + power * dot(k_ref[:, lanes], leaving, 1, 0)
        ).astype(BF16)


def call(kernel, out_shapes, scalars, arrays, scratch=()):
    return pl.pallas_call(
        kernel,
        out_shape=list(out_shapes),
        in_specs=[SMEM] * len(scalars) + [VMEM] * len(arrays),
        out_specs=[VMEM] * len(out_shapes),
        scratch_shapes=list(scratch),
        compiler_params=pltpu.CompilerParams(vmem_limit_bytes=16 * 1024 * 1024),
        cost_estimate=SMALL,
    )(*scalars, *arrays)


def halves_kernel(place_ref, own0, own1, other0, other1, weight_ref, sent_ref, kept_ref, rows_ref):
    count = sent_ref.shape[0]

    @pl.when(pl.program_id(0) == 0)
    def _():
        even = jnp.concatenate([own0[...].astype(F32), other0[...].astype(F32)], axis=0)
        odd = jnp.concatenate([own1[...].astype(F32), other1[...].astype(F32)], axis=0)
        first = place_ref[2] == 0
        rows_ref[:count] = jnp.where(first, odd, even).astype(BF16)
        rows_ref[count:] = jnp.where(first, even, odd).astype(BF16)

    out = dot(rows_ref[...], weight_ref[...], 1, 1).astype(BF16)
    sent_ref[...] = out[:count]
    kept_ref[...] = out[count:]


def halves_by_down(place, own, other, part, weight, tile=384):
    count = len(part) // 2
    join = lambda side, first: (
        side[part[first]] if count == 1
        else jnp.concatenate([side[part[first + i]] for i in range(count)], axis=0)
    )
    blocks = [join(own, 0), join(own, count), join(other, 0), join(other, count)]
    rows, depth = blocks[0].shape
    width = weight.shape[0]
    whole = pl.BlockSpec((rows, depth), lambda j: (0, 0))
    out = jax.ShapeDtypeStruct((2 * rows, width), BF16)
    return pl.pallas_call(
        halves_kernel,
        grid=(width // tile,),
        out_shape=[out, out],
        in_specs=[SMEM] + [whole] * 4 + [pl.BlockSpec((tile, depth), lambda j: (j, 0))],
        out_specs=[pl.BlockSpec((2 * rows, tile), lambda j: (0, j))] * 2,
        scratch_shapes=[pltpu.VMEM((4 * rows, depth), BF16)],
        compiler_params=pltpu.CompilerParams(vmem_limit_bytes=16 * 1024 * 1024),
        cost_estimate=SMALL,
    )(place, *blocks, weight)


def swap(array, axis, distance):
    size = lax.axis_size(axis)
    return lax.ppermute(array, axis, [(i, i ^ distance) for i in range(size)])


def trade(array, pairs, partner):
    return lax.ppermute(
        array, "ctx", [(2 * partner(i) + s, 2 * i + s) for i in range(pairs) for s in (0, 1)]
    )


def after(array, *events):
    return lax.optimization_barrier((array,) + events)[0]


def head_power(rates, place, half, tokens):
    mine = lax.dynamic_slice(rates, (place[0] * half,), (half,))[:, None, None]
    return jnp.exp(-mine * tokens)


def scan_total(mine, other, rates, place, block_len, reverse, *events):
    side = 1 - place[0] if reverse else place[0]
    whole = head_power(rates, place, mine.shape[0], block_len)
    partner = after(swap(other, "ctx", 1), *events)
    first = jnp.where(side == 0, mine, partner).astype(F32)
    second = jnp.where(side == 0, partner, mine).astype(F32)
    return (whole * first + second).astype(BF16), partner


def scan_step(before, total, reach, rates, place, block_len, reverse, *events):
    half = total.shape[0]
    pairs = lax.axis_size("ctx") // 2
    pair = pairs - 1 - place[1] if reverse else place[1]
    if before is None:
        upto = total
    else:
        whole = head_power(rates, place, half, 2.0 * block_len)
        upto = (whole * before + total.astype(F32)).astype(BF16)
    upto = after(upto, *events)
    lower, offset = (pair & reach) == 0, pair & (reach - 1)
    got = None
    for j in range(reach):

        def partner(i, j=j):
            i = pairs - 1 - i if reverse else i
            start = i - i % (2 * reach)
            first, second = start + reach - 1, start + reach + j
            i = {first: second, second: first}.get(i, i)
            return pairs - 1 - i if reverse else i

        one = trade(upto, pairs, partner)
        got = one if got is None else jnp.where(offset == j, one, got)
    scale = head_power(rates, place, half, 2.0 * block_len * offset.astype(F32))
    grown = scale * got.astype(F32)
    kept = 0.0 if before is None else before
    return jnp.where(lower, kept, kept + grown), upto


def scan_ends(before, mine, partner, rates, place, block_len, reverse):
    side = 1 - place[0] if reverse else place[0]
    whole = head_power(rates, place, mine.shape[0], block_len)
    first = jnp.where(side == 0, mine, partner).astype(F32)
    second_meets = whole * before + first
    keep = jnp.where(side == 0, before, second_meets).astype(BF16)
    give = jnp.where(side == 0, second_meets, before).astype(BF16)
    return keep, give


def split_rows(own, other, part, flag):
    count = len(part) // 2
    blocks = [
        jnp.where(flag == 0, side[part[i]], side[part[count + i]])
        for side in (own, other)
        for i in range(count)
    ]
    return jnp.concatenate(blocks, axis=0)


def sum_over_cores(own, other, part, multiply, *events):
    mine = lax.axis_index("exp") & 1
    sent = multiply(after(split_rows(own, other, part, 1 - mine), *events)).astype(BF16)
    got = swap(sent, "exp", 1)
    kept = multiply(after(split_rows(own, other, part, mine), sent))
    return (kept + got.astype(F32)).astype(BF16)


def sum_over_rest(part, bits):
    for bit in range(1, bits):
        part = (part.astype(F32) + swap(part, "exp", 1 << bit).astype(F32)).astype(BF16)
    return part


def on_device(
    queries, keys, values, out_grad, up_weight, down_weight, decay_rates, routes, gate_weights
):
    block_len, group = queries.shape
    heads = group // DH
    half = heads // 2
    experts = lax.axis_size("ctx") // 2
    bits = (lax.axis_size("exp") - 1).bit_length()
    capacity = block_len * 9 // (4 * experts)
    position = lax.axis_index("ctx").astype(jnp.int32)
    core = lax.axis_index("exp").astype(jnp.int32) & 1
    place = jnp.stack([position & 1, position >> 1, core])
    scalars = (place, decay_rates)
    up_local, down_local = up_weight[0], down_weight[0]
    near_part, far_part = range(experts // 2), range(experts // 2, experts)
    quarter = experts // 4
    order = [(k, k) for k in near_part]
    order += [(far_part[i], far_part[quarter + i]) for i in range(quarter)]
    order += [(far_part[quarter + i], far_part[i]) for i in range(quarter)]

    states = jax.ShapeDtypeStruct((half, DH, DH), BF16)
    weight_sq = jax.ShapeDtypeStruct((heads, block_len, block_len), BF16)
    wide = jax.ShapeDtypeStruct((block_len, group), F32)
    slim = jax.ShapeDtypeStruct((block_len, group), BF16)
    choose_table = jax.ShapeDtypeStruct((experts, capacity, block_len), F32)
    weigh_table = jax.ShapeDtypeStruct((experts, block_len, capacity), BF16)
    slots = jax.ShapeDtypeStruct((capacity, group), BF16)

    reaches = [1 << i for i in range((experts - 1).bit_length())]
    pairs_of = lambda rows, k: swap(rows, "ctx", 2 * k) if k else rows

    key_mine, key_other = call(key_state_kernel, [states] * 2, scalars, (keys, values))
    choose, weigh, *send_grad = call(
        functools.partial(route_kernel, order), [choose_table, weigh_table] + [slots] * experts,
        (place,), (routes.T, gate_weights.T, out_grad)
    )
    intra, weights = call(intra_kernel, [wide, weight_sq], scalars, (queries, keys, values))

    grad_own = {k: pairs_of(send_grad[k], k) for k in reversed(range(experts))}
    total, partner = scan_total(
        key_mine, key_other, decay_rates, place, block_len, False, send_grad[0]
    )
    before = None
    for index, reach in enumerate(reaches):
        events = list(grad_own.values()) + [intra] if index == 1 else []
        before, upto = scan_step(
            before, total, reach, decay_rates, place, block_len, False, *events
        )
    grad_other = {k: swap(after(grad_own[k], upto if k else total), "ctx", 1) for k in near_part}
    keep, give = scan_ends(before, key_mine, partner, decay_rates, place, block_len, False)
    entering = [keep, swap(give, "ctx", 1)]

    def over_cores(sent, kept):
        return (kept.astype(F32) + swap(sent, "exp", 1).astype(F32)).astype(BF16)

    grad_own[0] = after(grad_own[0], give)
    near_halves = halves_by_down(place, grad_own, grad_other, near_part, down_local)
    entering[1], *near_halves = lax.optimization_barrier((entering[1], *near_halves))
    for k in far_part:
        grad_other[k] = swap(after(grad_own[k], entering[1]), "ctx", 1)
    entering = tuple(entering)
    send_in = call(
        attend_kernel, [slots] * experts, scalars, (queries, intra, choose) + entering,
        [pltpu.VMEM((block_len, group), BF16)],
    )
    hidden_near = over_cores(*near_halves)
    grad_own[far_part[0]] = after(grad_own[far_part[0]], send_in[0], hidden_near)
    hidden_far = over_cores(*halves_by_down(place, grad_own, grad_other, far_part, down_local))
    in_own, in_other = {0: send_in[0]}, {}
    for k in [experts - 1, *near_part[1:]]:
        in_own[k] = pairs_of(send_in[k], k)
    for k in far_part[:-1]:
        in_own[k] = pairs_of(after(send_in[k], in_own[experts - 1]), k)
    for k in range(experts):
        in_other[k] = swap(in_own[k], "ctx", 1)

    by_up = lambda rows: dot(rows, up_local, 1, 0)
    hidden_near = sum_over_rest(hidden_near, bits)
    pre_near = sum_over_cores(in_own, in_other, near_part, by_up, hidden_near, hidden_far)
    hidden_far = sum_over_rest(hidden_far, bits)
    pre_far = sum_over_cores(in_own, in_other, far_part, by_up, pre_near)
    pre_near, pre_far = sum_over_rest(pre_near, bits), sum_over_rest(pre_far, bits)

    def returned(pre, hidden, *events):
        slope = (hidden.astype(F32) * silu_slope(pre.astype(F32))).astype(BF16)
        slope = after(slope, *events)
        slopes = (slope, swap(slope, "exp", 1))
        summed = []
        for slope in slopes:
            back = dot(after(slope, *events), up_local, 1, 1).astype(BF16)
            back = back.reshape(2, quarter * capacity, group)
            got = swap(back[1], "ctx", 1)
            events = events + (back,)
            summed.append((back[0], got))
        return summed

    def joined(item, *events):
        kept, got = item
        rows = (kept.astype(F32) + after(got, *events).astype(F32)).astype(BF16)
        return rows, [rows[i * capacity : (i + 1) * capacity] for i in range(quarter)]

    def far_home(rows, kept, i):
        moves = []
        size = lax.axis_size("exp")
        for c in range(2 * experts):
            for e in range(size):
                k = far_part[((e & 1) ^ (0 if kept else 1)) * quarter + i]
                moves.append((c * size + e, (c ^ (2 * k)) * size + e))
        return lax.ppermute(rows, ("ctx", "exp"), moves)

    near_items = returned(pre_near, hidden_near)
    far_items = returned(pre_far, hidden_far, near_items[0][0], near_items[1][0])
    first, near_first = joined(near_items[0])
    second, near_second = joined(near_items[1], first)
    homes = [jnp.where(core == 0, a, b) for a, b in zip(near_first, near_second)]
    homes += [jnp.where(core == 0, b, a) for a, b in zip(near_first, near_second)]
    homes = [pairs_of(rows, k) for k, rows in enumerate(homes)]
    first, far_first = joined(far_items[0])
    second, far_second = joined(far_items[1], first)
    homes += [far_home(rows, True, i) for i, rows in enumerate(far_first)]
    homes += [far_home(rows, False, i) for i, rows in enumerate(far_second)]

    grad_out, query_mine, query_other = call(
        grad_kernel, [slim, states, states], scalars, (queries, out_grad, weigh, *homes)
    )
    total, partner = scan_total(
        query_mine, query_other, decay_rates, place, block_len, True
    )
    before = None
    for reach in reaches:
        before, _ = scan_step(before, total, reach, decay_rates, place, block_len, True)
    keep, give = scan_ends(before, query_mine, partner, decay_rates, place, block_len, True)
    leaving = (keep, swap(give, "ctx", 1))
    query_g, key_near, value_near = call(
        near_kernel, [slim, wide, wide], scalars,
        (queries, keys, values, grad_out) + entering + (weights,)
    )
    key_g, value_g = call(
        far_kernel, [slim, slim], scalars,
        (keys, values, key_near, value_near) + leaving
    )
    return query_g, key_g, value_g


def solution(mesh):
    placed = (
        P("ctx", "exp"),
        P("ctx", "exp"),
        P("ctx", "exp"),
        P("ctx", "exp"),
        P("ctx", "exp", None),
        P("ctx", None, "exp"),
        P("exp"),
        P("ctx", None),
        P("ctx", None),
    )
    return jax.shard_map(
        on_device,
        mesh=mesh,
        in_specs=placed,
        out_specs=(P("ctx", "exp"), P("ctx", "exp"), P("ctx", "exp")),
        check_vma=False,
    )
```

```python
import functools

import jax
import jax.numpy as jnp
from jax import lax
from jax.experimental import pallas as pl
from jax.experimental.pallas import tpu as pltpu
from jax.sharding import PartitionSpec as P

DH = 128
F32 = jnp.float32
BF16 = jnp.bfloat16
SCALE = 1.0 / DH

SMEM = pl.BlockSpec(memory_space=pltpu.SMEM)
VMEM = pl.BlockSpec(memory_space=pltpu.VMEM)
LARGE = pl.CostEstimate(flops=1, bytes_accessed=40_000_000, transcendentals=0)
SMALL = pl.CostEstimate(flops=1, bytes_accessed=1, transcendentals=0)


def dot(left, right, left_dim, right_dim):
    return lax.dot_general(
        left, right, (((left_dim,), (right_dim,)), ((), ())), preferred_element_type=F32
    )


def silu_slope(value):
    sigma = jax.nn.sigmoid(value)
    return sigma * (1.0 + value * (1.0 - sigma))


def lanes_of(place_ref, slot, heads):
    head = lax.rem(place_ref[0] * (heads // 2) + slot, heads)
    return head, pl.ds(pl.multiple_of(head * DH, DH), DH)


def column(block_len):
    return lax.broadcasted_iota(jnp.int32, (block_len, 1), 0).astype(F32)


def decay_within(rate, block_len):
    rows = lax.broadcasted_iota(jnp.int32, (block_len, block_len), 0)
    cols = lax.broadcasted_iota(jnp.int32, (block_len, block_len), 1)
    distance = (rows - cols).astype(F32)
    return jnp.where(distance >= 0.0, jnp.exp(-rate * jnp.maximum(distance, 0.0)), 0.0)


def key_state_kernel(place_ref, rates_ref, k_ref, v_ref, mine_ref, other_ref):
    block_len, half = k_ref.shape[0], mine_ref.shape[0]
    steps = column(block_len)
    for slot in [*range(half, 2 * half), *range(half)]:
        head, lanes = lanes_of(place_ref, slot, 2 * half)
        power = jnp.exp(-rates_ref[head] * (block_len - steps))
        scaled = (k_ref[:, lanes].astype(F32) * power).astype(BF16)
        state_ref = (mine_ref, other_ref)[slot // half]
        state_ref[slot % half] = dot(scaled, v_ref[:, lanes], 0, 0).astype(BF16)


def pick_rows(choose_ref, rows, send_refs):
    capacity = choose_ref.shape[1]
    if capacity % 8:
        for k, send_ref in enumerate(send_refs):
            send_ref[...] = dot(choose_ref[k], rows, 1, 0).astype(BF16)
        return
    table = choose_ref[...].reshape(len(send_refs) * capacity, rows.shape[0])
    picked = dot(table.astype(BF16), rows, 1, 0)
    for k, send_ref in enumerate(send_refs):
        send_ref[...] = picked[k * capacity : (k + 1) * capacity].astype(BF16)


def route_kernel(
    place_ref, routes_ref, gates_ref, grad_ref, choose_ref, weigh_ref, *send_refs
):
    experts, capacity, block_len = choose_ref.shape
    rows = lax.broadcasted_iota(jnp.int32, (block_len, block_len), 0)
    cols = lax.broadcasted_iota(jnp.int32, (block_len, block_len), 1)

    first, second = routes_ref[0:1, :], routes_ref[1:2, :]
    names = lax.broadcasted_iota(jnp.int32, (32, block_len), 0)
    hit_first = jnp.where(names == first, 1.0, 0.0)
    hit_second = jnp.where(names == second, 1.0, 0.0)
    earlier = jnp.where(rows < cols, 1.0, 0.0).astype(BF16)
    before = dot((hit_first + hit_second).astype(BF16), earlier, 1, 0)
    slot_first = jnp.sum(before * hit_first, axis=0, keepdims=True).astype(jnp.int32)
    slot_second = jnp.sum(before * hit_second, axis=0, keepdims=True).astype(jnp.int32)
    slots = lax.broadcasted_iota(jnp.int32, (capacity, block_len), 0)
    for k in range(experts):
        expert = place_ref[1] ^ k
        named = ((slots == slot_first) & (first == expert)) | (
            (slots == slot_second) & (second == expert)
        )
        choose_ref[k] = jnp.where(named, 1.0, 0.0)
    pick_rows(choose_ref, grad_ref[...], send_refs)

    columns = jnp.concatenate(
        [first.astype(F32), second.astype(F32), slot_first.astype(F32), slot_second.astype(F32)]
        + [gates_ref[0:1, :], gates_ref[1:2, :]] + [jnp.zeros((2, block_len), F32)],
        axis=0,
    ).T
    first, second, slot_first, slot_second = [
        columns[:, i : i + 1].astype(jnp.int32) for i in range(4)
    ]
    slots = lax.broadcasted_iota(jnp.int32, (block_len, capacity), 1)
    for k in range(experts):
        expert = place_ref[1] ^ k
        one = jnp.where((slots == slot_first) & (first == expert), columns[:, 4:5], 0.0)
        two = jnp.where((slots == slot_second) & (second == expert), columns[:, 5:6], 0.0)
        weigh_ref[k] = (one + two).astype(BF16)


def intra_kernel(place_ref, rates_ref, q_ref, k_ref, v_ref, intra_ref, weights_ref):
    block_len, heads = q_ref.shape[0], weights_ref.shape[0]
    for slot in range(heads):
        head, lanes = lanes_of(place_ref, slot, heads)
        within = decay_within(rates_ref[head], block_len)
        scores = dot(q_ref[:, lanes], k_ref[:, lanes], 1, 1)
        weights = (SCALE * scores * within).astype(BF16)
        weights_ref[slot] = weights
        intra_ref[:, lanes] = dot(weights, v_ref[:, lanes], 1, 0)


def attend_kernel(
    place_ref, rates_ref, q_ref, intra_ref, choose_ref, mine_ref, other_ref, *refs
):
    send_refs, attn_ref = refs[:-1], refs[-1]
    block_len, half = q_ref.shape[0], mine_ref.shape[0]
    steps = column(block_len)
    for slot in range(2 * half):
        head, lanes = lanes_of(place_ref, slot, 2 * half)
        entering = (mine_ref, other_ref)[slot // half][slot % half]
        power = SCALE * jnp.exp(-rates_ref[head] * steps)
        inter = power * dot(q_ref[:, lanes], entering, 1, 0)
        attn_ref[:, lanes] = (intra_ref[:, lanes] + inter).astype(BF16)
    pick_rows(choose_ref, attn_ref[...], send_refs)


def grad_kernel(place_ref, rates_ref, q_ref, out_grad_ref, weigh_ref, *refs):
    experts = weigh_ref.shape[0]
    home_refs, (grad_ref, mine_ref, other_ref) = refs[:experts], refs[experts:]
    block_len, half = q_ref.shape[0], mine_ref.shape[0]
    steps = column(block_len)
    total = out_grad_ref[...].astype(F32)
    for k in range(experts):
        total = total + dot(weigh_ref[k], home_refs[k][...], 1, 0)
    grad_ref[...] = total.astype(BF16)
    for slot in [*range(half, 2 * half), *range(half)]:
        head, lanes = lanes_of(place_ref, slot, 2 * half)
        power = jnp.exp(-rates_ref[head] * (steps + 1.0))
        scaled = (q_ref[:, lanes].astype(F32) * power).astype(BF16)
        state_ref = (mine_ref, other_ref)[slot // half]
        state_ref[slot % half] = dot(scaled, grad_ref[:, lanes], 0, 0).astype(BF16)


def near_kernel(
    place_ref, rates_ref, q_ref, k_ref, v_ref, grad_ref, mine_ref, other_ref, weights_ref,
    query_ref, key_ref, value_ref,
):
    block_len, half = q_ref.shape[0], mine_ref.shape[0]
    steps = column(block_len)
    for slot in range(2 * half):
        head, lanes = lanes_of(place_ref, slot, 2 * half)
        rate = rates_ref[head]
        grad = grad_ref[:, lanes]
        entering = (mine_ref, other_ref)[slot // half][slot % half]
        within = decay_within(rate, block_len)
        dweights = (SCALE * dot(grad, v_ref[:, lanes], 1, 1) * within).astype(BF16)
        query = dot(dweights, k_ref[:, lanes], 1, 0)
        query = query + SCALE * jnp.exp(-rate * steps) * dot(grad, entering, 1, 1)
        query_ref[:, lanes] = query.astype(BF16)
        key_ref[:, lanes] = dot(dweights, q_ref[:, lanes], 0, 0)
        value_ref[:, lanes] = dot(weights_ref[slot], grad, 0, 0)


def far_kernel(
    place_ref, rates_ref, k_ref, v_ref, key_near, value_near, mine_ref, other_ref, key_ref, value_ref
):
    block_len, half = k_ref.shape[0], mine_ref.shape[0]
    steps = column(block_len)
    for slot in range(2 * half):
        head, lanes = lanes_of(place_ref, slot, 2 * half)
        leaving = (mine_ref, other_ref)[slot // half][slot % half]
        power = SCALE * jnp.exp(-rates_ref[head] * (block_len - 1.0 - steps))
        key_ref[:, lanes] = (
            key_near[:, lanes] + power * dot(v_ref[:, lanes], leaving, 1, 1)
        ).astype(BF16)
        value_ref[:, lanes] = (
            value_near[:, lanes] + power * dot(k_ref[:, lanes], leaving, 1, 0)
        ).astype(BF16)


def call(kernel, out_shapes, scalars, arrays, scratch=(), cost=SMALL):
    return pl.pallas_call(
        kernel,
        out_shape=list(out_shapes),
        in_specs=[SMEM] * len(scalars) + [VMEM] * len(arrays),
        out_specs=[VMEM] * len(out_shapes),
        scratch_shapes=list(scratch),
        compiler_params=pltpu.CompilerParams(vmem_limit_bytes=16 * 1024 * 1024),
        cost_estimate=cost,
    )(*scalars, *arrays)


def swap(array, axis, distance):
    size = lax.axis_size(axis)
    return lax.ppermute(array, axis, [(i, i ^ distance) for i in range(size)])


def trade(array, pairs, partner):
    return lax.ppermute(
        array, "ctx", [(2 * partner(i) + s, 2 * i + s) for i in range(pairs) for s in (0, 1)]
    )


def after(array, *events):
    return lax.optimization_barrier((array,) + events)[0]


def head_power(rates, place, half, tokens):
    mine = lax.dynamic_slice(rates, (place[0] * half,), (half,))[:, None, None]
    return jnp.exp(-mine * tokens)


def scan_total(mine, other, rates, place, block_len, reverse, *events):
    side = 1 - place[0] if reverse else place[0]
    whole = head_power(rates, place, mine.shape[0], block_len)
    partner = after(swap(other, "ctx", 1), *events)
    first = jnp.where(side == 0, mine, partner).astype(F32)
    second = jnp.where(side == 0, partner, mine).astype(F32)
    return (whole * first + second).astype(BF16), partner


def scan_step(before, total, reach, rates, place, block_len, reverse, *events):
    half = total.shape[0]
    pairs = lax.axis_size("ctx") // 2
    pair = pairs - 1 - place[1] if reverse else place[1]
    if before is None:
        upto = total
    else:
        whole = head_power(rates, place, half, 2.0 * block_len)
        upto = (whole * before + total.astype(F32)).astype(BF16)
    upto = after(upto, *events)
    lower, offset = (pair & reach) == 0, pair & (reach - 1)
    got = None
    for j in range(reach):

        def partner(i, j=j):
            i = pairs - 1 - i if reverse else i
            start = i - i % (2 * reach)
            first, second = start + reach - 1, start + reach + j
            i = {first: second, second: first}.get(i, i)
            return pairs - 1 - i if reverse else i

        one = trade(upto, pairs, partner)
        got = one if got is None else jnp.where(offset == j, one, got)
    scale = head_power(rates, place, half, 2.0 * block_len * offset.astype(F32))
    grown = scale * got.astype(F32)
    kept = 0.0 if before is None else before
    return jnp.where(lower, kept, kept + grown), upto


def scan_ends(before, mine, partner, rates, place, block_len, reverse):
    side = 1 - place[0] if reverse else place[0]
    whole = head_power(rates, place, mine.shape[0], block_len)
    first = jnp.where(side == 0, mine, partner).astype(F32)
    second_meets = whole * before + first
    keep = jnp.where(side == 0, before, second_meets).astype(BF16)
    give = jnp.where(side == 0, second_meets, before).astype(BF16)
    return keep, give


def sum_over_cores(own, other, part, multiply, *events):
    mine = lax.axis_index("exp") & 1
    rows = lambda flag: jnp.concatenate(
        [jnp.where(flag == 0, own[k], other[k]) for k in part], axis=0
    )
    sent = multiply(after(rows(1 - mine), *events)).astype(BF16)
    kept = multiply(after(rows(mine), sent)).astype(BF16)
    return sent, kept


def over_cores(sent, kept):
    return (kept.astype(F32) + swap(sent, "exp", 1).astype(F32)).astype(BF16)


def sum_over_rest(part, bits):
    for bit in range(1, bits):
        part = (part.astype(F32) + swap(part, "exp", 1 << bit).astype(F32)).astype(BF16)
    return part


def on_device(
    queries, keys, values, out_grad, up_weight, down_weight, decay_rates, routes, gate_weights
):
    block_len, group = queries.shape
    heads = group // DH
    half = heads // 2
    experts = lax.axis_size("ctx") // 2
    bits = (lax.axis_size("exp") - 1).bit_length()
    capacity = block_len * 9 // (4 * experts)
    position = lax.axis_index("ctx").astype(jnp.int32)
    core = lax.axis_index("exp").astype(jnp.int32) & 1
    place = jnp.stack([position & 1, position >> 1, core])
    scalars = (place, decay_rates)
    up_local, down_local = up_weight[0], down_weight[0]
    quarter = max(experts // 4, 1)
    near_part = range(experts // 2)
    first_far = range(experts - quarter, experts)
    second_far = range(experts // 2, experts - quarter)
    states = jax.ShapeDtypeStruct((half, DH, DH), BF16)
    weight_sq = jax.ShapeDtypeStruct((heads, block_len, block_len), BF16)
    wide = jax.ShapeDtypeStruct((block_len, group), F32)
    slim = jax.ShapeDtypeStruct((block_len, group), BF16)
    choose_table = jax.ShapeDtypeStruct((experts, capacity, block_len), F32)
    weigh_table = jax.ShapeDtypeStruct((experts, block_len, capacity), BF16)
    slots = jax.ShapeDtypeStruct((capacity, group), BF16)

    reaches = [1 << i for i in range((experts - 1).bit_length())]
    pairs_of = lambda rows, k: swap(rows, "ctx", 2 * k) if k else rows

    key_mine, key_other = call(key_state_kernel, [states] * 2, scalars, (keys, values))
    choose, weigh, *send_grad = call(
        route_kernel, [choose_table, weigh_table] + [slots] * experts,
        (place,), (routes.T, gate_weights.T, out_grad)
    )
    intra, weights = call(
        intra_kernel, [wide, weight_sq], scalars, (queries, keys, values), cost=LARGE
    )

    total, partner = scan_total(
        key_mine, key_other, decay_rates, place, block_len, False, send_grad[0]
    )
    grad_own = {0: send_grad[0]}
    for k in [*near_part[1:], *first_far]:
        grad_own[k] = pairs_of(after(send_grad[k], total), k)
    before = None
    for index, reach in enumerate(reaches):
        events = [intra] if index == 1 else []
        before, upto = scan_step(
            before, total, reach, decay_rates, place, block_len, False, *events
        )
    keep, give = scan_ends(before, key_mine, partner, decay_rates, place, block_len, False)
    grad_other = {0: swap(after(grad_own[0], total), "ctx", 1)}
    for k in [*near_part[1:], *first_far]:
        grad_other[k] = swap(after(grad_own[k], upto), "ctx", 1)
    for k in second_far:
        grad_own[k] = pairs_of(after(send_grad[k], give), k)

    by_down = lambda rows: dot(rows, down_local, 1, 1)
    by_up = lambda rows: dot(rows, up_local, 1, 0)
    given = swap(give, "ctx", 1)
    hidden_near = over_cores(*sum_over_cores(grad_own, grad_other, near_part, by_down, give))
    given, hidden_near = lax.optimization_barrier((given, hidden_near))
    send_in = call(
        attend_kernel, [slots] * experts, scalars, (queries, intra, choose, keep, given),
        [pltpu.VMEM((block_len, group), BF16)],
    )
    for k in second_far:
        grad_other[k] = swap(after(grad_own[k], send_in[0]), "ctx", 1)
    hidden_first = over_cores(
        *sum_over_cores(grad_own, grad_other, first_far, by_down, send_in[0])
    )

    in_own, in_other = {0: send_in[0]}, {}
    for k in [*near_part[1:], *first_far]:
        in_own[k] = pairs_of(send_in[k], k)
    for k in second_far:
        in_own[k] = pairs_of(after(send_in[k], in_own[first_far[0]], hidden_first), k)
    for k in range(experts):
        in_other[k] = swap(in_own[k], "ctx", 1)

    pre_near = over_cores(*sum_over_cores(in_own, in_other, near_part, by_up, hidden_first))
    pre_first = over_cores(*sum_over_cores(in_own, in_other, first_far, by_up, pre_near))
    hidden_second = over_cores(
        *sum_over_cores(grad_own, grad_other, second_far, by_down, pre_first)
    )
    pre_second = over_cores(*sum_over_cores(in_own, in_other, second_far, by_up, hidden_second))

    homes = {}
    back = None
    for part, pre, hidden in (
        (near_part, pre_near, hidden_near),
        (first_far, pre_first, hidden_first),
        (second_far, pre_second, hidden_second),
    ):
        pre, hidden = sum_over_rest(pre, bits), sum_over_rest(hidden, bits)
        slope = (hidden.astype(F32) * silu_slope(pre.astype(F32))).astype(BF16)
        got = swap(slope, "exp", 1)
        if back is not None:
            got = after(got, back)
        slope = jnp.concatenate(
            [jnp.where(core == 0, slope, got), jnp.where(core == 0, got, slope)], axis=0
        )
        back = dot(slope, up_local, 1, 1).astype(BF16)
        blocks = back.reshape(2, len(part) * capacity, group)
        got = swap(blocks[1], "ctx", 1)
        rows = (blocks[0].astype(F32) + got.astype(F32)).astype(BF16)
        for i, k in enumerate(part):
            homes[k] = pairs_of(rows[i * capacity : (i + 1) * capacity], k)
    homes = [homes[k] for k in range(experts)]

    grad_out, query_mine, query_other = call(
        grad_kernel, [slim, states, states], scalars, (queries, out_grad, weigh, *homes)
    )
    total, partner = scan_total(
        query_mine, query_other, decay_rates, place, block_len, True
    )
    before = None
    for reach in reaches:
        before, _ = scan_step(before, total, reach, decay_rates, place, block_len, True)
    keep_in = keep
    keep, give = scan_ends(before, query_mine, partner, decay_rates, place, block_len, True)
    leaving = (keep, swap(give, "ctx", 1))
    query_g, key_near, value_near = call(
        near_kernel, [slim, wide, wide], scalars,
        (queries, keys, values, grad_out, keep_in, given, weights)
    )
    key_g, value_g = call(
        far_kernel, [slim, slim], scalars,
        (keys, values, key_near, value_near) + leaving
    )
    return query_g, key_g, value_g


def solution(mesh):
    placed = (
        P("ctx", "exp"),
        P("ctx", "exp"),
        P("ctx", "exp"),
        P("ctx", "exp"),
        P("ctx", "exp", None),
        P("ctx", None, "exp"),
        P("exp"),
        P("ctx", None),
        P("ctx", None),
    )
    return jax.shard_map(
        on_device,
        mesh=mesh,
        in_specs=placed,
        out_specs=(P("ctx", "exp"), P("ctx", "exp"), P("ctx", "exp")),
        check_vma=False,
    )
```

```python
import functools

import jax
import jax.numpy as jnp
from jax import lax
from jax.experimental import pallas as pl
from jax.experimental.pallas import tpu as pltpu
from jax.sharding import PartitionSpec as P

DH = 128
F32 = jnp.float32
BF16 = jnp.bfloat16
SCALE = 1.0 / DH

SMEM = pl.BlockSpec(memory_space=pltpu.SMEM)
VMEM = pl.BlockSpec(memory_space=pltpu.VMEM)
HBM = pl.BlockSpec(memory_space=pl.ANY)
LARGE = pl.CostEstimate(flops=1, bytes_accessed=40_000_000, transcendentals=0)
SMALL = pl.CostEstimate(flops=1, bytes_accessed=1, transcendentals=0)


def dot(left, right, left_dim, right_dim):
    return lax.dot_general(
        left, right, (((left_dim,), (right_dim,)), ((), ())), preferred_element_type=F32
    )


def silu_slope(value):
    sigma = jax.nn.sigmoid(value)
    return sigma * (1.0 + value * (1.0 - sigma))


def lanes_of(place_ref, slot, heads):
    head = lax.rem(place_ref[0] * (heads // 2) + slot, heads)
    return head, pl.ds(pl.multiple_of(head * DH, DH), DH)


def column(block_len):
    return lax.broadcasted_iota(jnp.int32, (block_len, 1), 0).astype(F32)


def decay_within(rate, block_len):
    rows = lax.broadcasted_iota(jnp.int32, (block_len, block_len), 0)
    cols = lax.broadcasted_iota(jnp.int32, (block_len, block_len), 1)
    distance = (rows - cols).astype(F32)
    return jnp.where(distance >= 0.0, jnp.exp(-rate * jnp.maximum(distance, 0.0)), 0.0)


def key_state_kernel(place_ref, rates_ref, k_ref, v_ref, mine_ref, other_ref):
    block_len, half = k_ref.shape[0], mine_ref.shape[0]
    steps = column(block_len)
    for slot in [*range(half, 2 * half), *range(half)]:
        head, lanes = lanes_of(place_ref, slot, 2 * half)
        power = jnp.exp(-rates_ref[head] * (block_len - steps))
        scaled = (k_ref[:, lanes].astype(F32) * power).astype(BF16)
        state_ref = (mine_ref, other_ref)[slot // half]
        state_ref[slot % half] = dot(scaled, v_ref[:, lanes], 0, 0).astype(BF16)


def pick_rows(choose_ref, rows, send_refs):
    capacity = choose_ref.shape[1]
    if capacity % 8:
        for k, send_ref in enumerate(send_refs):
            send_ref[...] = dot(choose_ref[k], rows, 1, 0).astype(BF16)
        return
    table = choose_ref[...].reshape(len(send_refs) * capacity, rows.shape[0])
    picked = dot(table.astype(BF16), rows, 1, 0)
    for k, send_ref in enumerate(send_refs):
        send_ref[...] = picked[k * capacity : (k + 1) * capacity].astype(BF16)


def route_kernel(
    place_ref, grad_ref, routes_ref, gates_ref, choose_ref, weigh_ref, *send_refs
):
    experts, capacity, block_len = choose_ref.shape
    rows = lax.broadcasted_iota(jnp.int32, (block_len, block_len), 0)
    cols = lax.broadcasted_iota(jnp.int32, (block_len, block_len), 1)

    first, second = routes_ref[0:1, :], routes_ref[1:2, :]
    names = lax.broadcasted_iota(jnp.int32, (32, block_len), 0)
    hit_first = jnp.where(names == first, 1.0, 0.0)
    hit_second = jnp.where(names == second, 1.0, 0.0)
    earlier = jnp.where(rows < cols, 1.0, 0.0).astype(BF16)
    before = dot((hit_first + hit_second).astype(BF16), earlier, 1, 0)
    slot_first = jnp.sum(before * hit_first, axis=0, keepdims=True).astype(jnp.int32)
    slot_second = jnp.sum(before * hit_second, axis=0, keepdims=True).astype(jnp.int32)
    slots = lax.broadcasted_iota(jnp.int32, (capacity, block_len), 0)
    for k in range(experts):
        expert = place_ref[1] ^ k
        named = ((slots == slot_first) & (first == expert)) | (
            (slots == slot_second) & (second == expert)
        )
        choose_ref[k] = jnp.where(named, 1.0, 0.0)
    pick_rows(choose_ref, grad_ref[...], send_refs)

    columns = jnp.concatenate(
        [first.astype(F32), second.astype(F32), slot_first.astype(F32), slot_second.astype(F32)]
        + [gates_ref[0:1, :], gates_ref[1:2, :]] + [jnp.zeros((2, block_len), F32)],
        axis=0,
    ).T
    first, second, slot_first, slot_second = [
        columns[:, i : i + 1].astype(jnp.int32) for i in range(4)
    ]
    slots = lax.broadcasted_iota(jnp.int32, (block_len, capacity), 1)
    for k in range(experts):
        expert = place_ref[1] ^ k
        one = jnp.where((slots == slot_first) & (first == expert), columns[:, 4:5], 0.0)
        two = jnp.where((slots == slot_second) & (second == expert), columns[:, 5:6], 0.0)
        weigh_ref[k] = (one + two).astype(BF16)


def intra_kernel(place_ref, rates_ref, q_ref, k_ref, v_ref, intra_ref, weights_ref):
    block_len, heads = q_ref.shape[0], weights_ref.shape[0]
    for slot in range(heads):
        head, lanes = lanes_of(place_ref, slot, heads)
        within = decay_within(rates_ref[head], block_len)
        scores = dot(q_ref[:, lanes], k_ref[:, lanes], 1, 1)
        weights = (SCALE * scores * within).astype(BF16)
        weights_ref[slot] = weights
        intra_ref[:, lanes] = dot(weights, v_ref[:, lanes], 1, 0)


def attend_kernel(
    place_ref, rates_ref, q_ref, intra_ref, choose_ref, mine_ref, other_ref, *refs
):
    send_refs, attn_ref = refs[:-1], refs[-1]
    block_len, half = q_ref.shape[0], mine_ref.shape[0]
    steps = column(block_len)
    for slot in range(2 * half):
        head, lanes = lanes_of(place_ref, slot, 2 * half)
        entering = (mine_ref, other_ref)[slot // half][slot % half]
        power = SCALE * jnp.exp(-rates_ref[head] * steps)
        inter = power * dot(q_ref[:, lanes], entering, 1, 0)
        attn_ref[:, lanes] = (intra_ref[:, lanes] + inter).astype(BF16)
    pick_rows(choose_ref, attn_ref[...], send_refs)


def grad_kernel(place_ref, rates_ref, q_ref, out_grad_ref, weigh_ref, *refs):
    experts = weigh_ref.shape[0]
    home_refs, (grad_ref, mine_ref, other_ref) = refs[:experts], refs[experts:]
    block_len, half = q_ref.shape[0], mine_ref.shape[0]
    steps = column(block_len)
    total = out_grad_ref[...].astype(F32)
    for k in range(experts):
        total = total + dot(weigh_ref[k], home_refs[k][...], 1, 0)
    grad_ref[...] = total.astype(BF16)
    for slot in [*range(half, 2 * half), *range(half)]:
        head, lanes = lanes_of(place_ref, slot, 2 * half)
        power = jnp.exp(-rates_ref[head] * (steps + 1.0))
        scaled = (q_ref[:, lanes].astype(F32) * power).astype(BF16)
        state_ref = (mine_ref, other_ref)[slot // half]
        state_ref[slot % half] = dot(scaled, grad_ref[:, lanes], 0, 0).astype(BF16)


def near_kernel(
    place_ref, rates_ref, q_ref, k_ref, v_ref, grad_ref, mine_ref, other_ref, weights_ref,
    query_ref, key_ref, value_ref,
):
    block_len, half = q_ref.shape[0], mine_ref.shape[0]
    steps = column(block_len)
    for slot in range(2 * half):
        head, lanes = lanes_of(place_ref, slot, 2 * half)
        rate = rates_ref[head]
        grad = grad_ref[:, lanes]
        entering = (mine_ref, other_ref)[slot // half][slot % half]
        within = decay_within(rate, block_len)
        dweights = (SCALE * dot(grad, v_ref[:, lanes], 1, 1) * within).astype(BF16)
        query = dot(dweights, k_ref[:, lanes], 1, 0)
        query = query + SCALE * jnp.exp(-rate * steps) * dot(grad, entering, 1, 1)
        query_ref[:, lanes] = query.astype(BF16)
        key_ref[:, lanes] = dot(dweights, q_ref[:, lanes], 0, 0)
        value_ref[:, lanes] = dot(weights_ref[slot], grad, 0, 0)


def far_kernel(
    place_ref, rates_ref, k_ref, v_ref, key_near, value_near, mine_ref, other_ref, key_ref, value_ref
):
    block_len, half = k_ref.shape[0], mine_ref.shape[0]
    steps = column(block_len)
    for slot in range(2 * half):
        head, lanes = lanes_of(place_ref, slot, 2 * half)
        leaving = (mine_ref, other_ref)[slot // half][slot % half]
        power = SCALE * jnp.exp(-rates_ref[head] * (block_len - 1.0 - steps))
        key_ref[:, lanes] = (
            key_near[:, lanes] + power * dot(v_ref[:, lanes], leaving, 1, 1)
        ).astype(BF16)
        value_ref[:, lanes] = (
            value_near[:, lanes] + power * dot(k_ref[:, lanes], leaving, 1, 0)
        ).astype(BF16)


def fetched(kernel, scalars, count, *refs):
    sources, rest = refs[scalars : scalars + count], refs[scalars + count : -1 - count]
    buffers, sems = refs[-1 - count : -1], refs[-1]
    copies = [
        pltpu.make_async_copy(source, buffer, sems.at[i])
        for i, (source, buffer) in enumerate(zip(sources, buffers))
    ]
    for copy in copies:
        copy.start()
    for copy in copies:
        copy.wait()
    kernel(*refs[:scalars], *buffers, *rest)


def call(kernel, out_shapes, scalars, arrays, scratch=(), cost=SMALL, fetch=0):
    scratch = list(scratch)
    if fetch:
        kernel = functools.partial(fetched, kernel, len(scalars), fetch)
        scratch += [pltpu.VMEM(array.shape, array.dtype) for array in arrays[:fetch]]
        scratch += [pltpu.SemaphoreType.DMA((fetch,))]
    return pl.pallas_call(
        kernel,
        out_shape=list(out_shapes),
        in_specs=[SMEM] * len(scalars) + [HBM] * fetch + [VMEM] * (len(arrays) - fetch),
        out_specs=[VMEM] * len(out_shapes),
        scratch_shapes=scratch,
        compiler_params=pltpu.CompilerParams(vmem_limit_bytes=16 * 1024 * 1024),
        cost_estimate=cost,
    )(*scalars, *arrays)


def swap(array, axis, distance):
    size = lax.axis_size(axis)
    return lax.ppermute(array, axis, [(i, i ^ distance) for i in range(size)])


def trade(array, pairs, partner):
    return lax.ppermute(
        array, "ctx", [(2 * partner(i) + s, 2 * i + s) for i in range(pairs) for s in (0, 1)]
    )


def after(array, *events):
    return lax.optimization_barrier((array,) + events)[0]


def head_power(rates, place, half, tokens):
    mine = lax.dynamic_slice(rates, (place[0] * half,), (half,))[:, None, None]
    return jnp.exp(-mine * tokens)


def scan_total(mine, other, rates, place, block_len, reverse, *events):
    side = 1 - place[0] if reverse else place[0]
    whole = head_power(rates, place, mine.shape[0], block_len)
    partner = after(swap(other, "ctx", 1), *events)
    first = jnp.where(side == 0, mine, partner).astype(F32)
    second = jnp.where(side == 0, partner, mine).astype(F32)
    return (whole * first + second).astype(BF16), partner


def scan_step(before, total, reach, rates, place, block_len, reverse, *events):
    half = total.shape[0]
    pairs = lax.axis_size("ctx") // 2
    pair = pairs - 1 - place[1] if reverse else place[1]
    if before is None:
        upto = total
    else:
        whole = head_power(rates, place, half, 2.0 * block_len)
        upto = (whole * before + total.astype(F32)).astype(BF16)
    upto = after(upto, *events)
    lower, offset = (pair & reach) == 0, pair & (reach - 1)
    got = None
    for j in range(reach):

        def partner(i, j=j):
            i = pairs - 1 - i if reverse else i
            start = i - i % (2 * reach)
            first, second = start + reach - 1, start + reach + j
            i = {first: second, second: first}.get(i, i)
            return pairs - 1 - i if reverse else i

        one = trade(upto, pairs, partner)
        got = one if got is None else jnp.where(offset == j, one, got)
    scale = head_power(rates, place, half, 2.0 * block_len * offset.astype(F32))
    grown = scale * got.astype(F32)
    kept = 0.0 if before is None else before
    return jnp.where(lower, kept, kept + grown), upto


def scan_ends(before, mine, partner, rates, place, block_len, reverse):
    side = 1 - place[0] if reverse else place[0]
    whole = head_power(rates, place, mine.shape[0], block_len)
    first = jnp.where(side == 0, mine, partner).astype(F32)
    second_meets = whole * before + first
    keep = jnp.where(side == 0, before, second_meets).astype(BF16)
    give = jnp.where(side == 0, second_meets, before).astype(BF16)
    return keep, give


def sum_over_cores(own, other, part, multiply, *events):
    mine = lax.axis_index("exp") & 1
    rows = lambda flag: jnp.concatenate(
        [jnp.where(flag == 0, own[k], other[k]) for k in part], axis=0
    )
    sent = multiply(after(rows(1 - mine), *events)).astype(BF16)
    kept = multiply(after(rows(mine), sent)).astype(BF16)
    return sent, kept


def over_cores(sent, kept):
    return (kept.astype(F32) + swap(sent, "exp", 1).astype(F32)).astype(BF16)


def sum_over_rest(part, bits):
    for bit in range(1, bits):
        part = (part.astype(F32) + swap(part, "exp", 1 << bit).astype(F32)).astype(BF16)
    return part


def on_device(
    queries, keys, values, out_grad, up_weight, down_weight, decay_rates, routes, gate_weights
):
    block_len, group = queries.shape
    heads = group // DH
    half = heads // 2
    experts = lax.axis_size("ctx") // 2
    bits = (lax.axis_size("exp") - 1).bit_length()
    capacity = block_len * 9 // (4 * experts)
    position = lax.axis_index("ctx").astype(jnp.int32)
    core = lax.axis_index("exp").astype(jnp.int32) & 1
    place = jnp.stack([position & 1, position >> 1, core])
    scalars = (place, decay_rates)
    up_local, down_local = up_weight[0], down_weight[0]
    quarter = max(experts // 4, 1)
    near_part = range(experts // 2)
    first_far = range(experts - quarter, experts)
    second_far = range(experts // 2, experts - quarter)
    states = jax.ShapeDtypeStruct((half, DH, DH), BF16)
    weight_sq = jax.ShapeDtypeStruct((heads, block_len, block_len), BF16)
    wide = jax.ShapeDtypeStruct((block_len, group), F32)
    slim = jax.ShapeDtypeStruct((block_len, group), BF16)
    choose_table = jax.ShapeDtypeStruct((experts, capacity, block_len), F32)
    weigh_table = jax.ShapeDtypeStruct((experts, block_len, capacity), BF16)
    slots = jax.ShapeDtypeStruct((capacity, group), BF16)

    reaches = [1 << i for i in range((experts - 1).bit_length())]
    pairs_of = lambda rows, k: swap(rows, "ctx", 2 * k) if k else rows

    key_mine, key_other = call(
        key_state_kernel, [states] * 2, scalars, (keys, values), cost=LARGE, fetch=2
    )
    choose, weigh, *send_grad = call(
        route_kernel, [choose_table, weigh_table] + [slots] * experts,
        (place,), (out_grad, routes.T, gate_weights.T), cost=LARGE, fetch=1,
    )
    intra, weights = call(
        intra_kernel, [wide, weight_sq], scalars, (queries, keys, values), cost=LARGE, fetch=3
    )
    by_down = lambda rows: dot(rows, down_local, 1, 1)
    by_up = lambda rows: dot(rows, up_local, 1, 0)

    def hidden_of(part, *events):
        return over_cores(*sum_over_cores(grad_own, grad_other, part, by_down, *events))

    total, partner = scan_total(
        key_mine, key_other, decay_rates, place, block_len, False, send_grad[0]
    )
    grad_own, grad_other = {0: send_grad[0]}, {0: swap(send_grad[0], "ctx", 1)}
    before = None
    for index, reach in enumerate(reaches):
        events = [intra, grad_other[0]] if index == 1 else []
        before, upto = scan_step(
            before, total, reach, decay_rates, place, block_len, False, *events
        )
    for k in near_part[1:]:
        grad_own[k] = pairs_of(after(send_grad[k], upto), k)
        grad_other[k] = swap(grad_own[k], "ctx", 1)
    hidden = {0: hidden_of([0], upto)}
    before = after(before, hidden[0], *[grad_own[k] for k in near_part[1:]])
    keep, give = scan_ends(before, key_mine, partner, decay_rates, place, block_len, False)
    for k in first_far:
        grad_own[k] = pairs_of(after(send_grad[k], give), k)
    given = swap(give, "ctx", 1)
    for k in near_part[1:]:
        hidden[k] = hidden_of([k], give)
    given, *ready = lax.optimization_barrier((given, *[hidden[k] for k in near_part[1:]]))
    for k, rows in zip(near_part[1:], ready):
        hidden[k] = rows
    send_in = call(
        attend_kernel, [slots] * experts, scalars, (queries, intra, choose, keep, given),
        [pltpu.VMEM((block_len, group), BF16)],
    )
    in_own, in_other = {0: send_in[0]}, {}
    for k in [*near_part[1:], *first_far]:
        in_own[k] = pairs_of(send_in[k], k)
    for k in first_far:
        grad_other[k] = swap(after(grad_own[k], send_in[0]), "ctx", 1)
        hidden[k] = hidden_of([k])
    ready = [hidden[k] for k in first_far]
    for k in second_far:
        in_own[k] = pairs_of(after(send_in[k], in_own[first_far[0]]), k)
        grad_own[k] = pairs_of(after(send_grad[k], in_own[first_far[0]]), k)
    for k in near_part:
        in_other[k] = swap(in_own[k], "ctx", 1)
    for k in first_far:
        in_other[k] = swap(after(in_own[k], in_other[near_part[-1]]), "ctx", 1)
    pre_near = over_cores(*sum_over_cores(in_own, in_other, near_part, by_up, *ready))
    for k in second_far:
        in_other[k] = swap(after(in_own[k], pre_near), "ctx", 1)
        grad_other[k] = swap(after(grad_own[k], in_other[k]), "ctx", 1)
    pre_first = over_cores(*sum_over_cores(in_own, in_other, first_far, by_up, pre_near))
    for k in second_far:
        hidden[k] = hidden_of([k], pre_first)
    pre_near = sum_over_rest(pre_near, bits)
    ready = [hidden[k] for k in second_far]
    pre_second = over_cores(
        *sum_over_cores(in_own, in_other, second_far, by_up, pre_near, *ready)
    )

    homes = {}
    back = None
    for part, pre in (
        (near_part, pre_near),
        (first_far, pre_first),
        (second_far, pre_second),
    ):
        if back is not None:
            pre = after(sum_over_rest(pre, bits), back)
        rows = [sum_over_rest(hidden[k], bits) for k in part]
        grad = rows[0] if len(rows) == 1 else jnp.concatenate(rows, axis=0)
        slope = (grad.astype(F32) * silu_slope(pre.astype(F32))).astype(BF16)
        got = swap(slope, "exp", 1)
        slope = jnp.concatenate(
            [jnp.where(core == 0, slope, got), jnp.where(core == 0, got, slope)], axis=0
        )
        back = dot(slope, up_local, 1, 1).astype(BF16)
        blocks = back.reshape(2, len(part) * capacity, group)
        got = swap(blocks[1], "ctx", 1)
        rows = (blocks[0].astype(F32) + got.astype(F32)).astype(BF16)
        for i, k in enumerate(part):
            homes[k] = pairs_of(rows[i * capacity : (i + 1) * capacity], k)
    homes = [homes[k] for k in range(experts)]

    grad_out, query_mine, query_other = call(
        grad_kernel, [slim, states, states], scalars, (queries, out_grad, weigh, *homes)
    )
    total, partner = scan_total(
        query_mine, query_other, decay_rates, place, block_len, True
    )
    before = None
    for reach in reaches:
        before, _ = scan_step(before, total, reach, decay_rates, place, block_len, True)
    keep_in = keep
    keep, give = scan_ends(before, query_mine, partner, decay_rates, place, block_len, True)
    leaving = (keep, swap(give, "ctx", 1))
    query_g, key_near, value_near = call(
        near_kernel, [slim, wide, wide], scalars,
        (queries, keys, values, grad_out, keep_in, given, weights)
    )
    key_g, value_g = call(
        far_kernel, [slim, slim], scalars,
        (keys, values, key_near, value_near) + leaving
    )
    return query_g, key_g, value_g


def solution(mesh):
    placed = (
        P("ctx", "exp"),
        P("ctx", "exp"),
        P("ctx", "exp"),
        P("ctx", "exp"),
        P("ctx", "exp", None),
        P("ctx", None, "exp"),
        P("exp"),
        P("ctx", None),
        P("ctx", None),
    )
    return jax.shard_map(
        on_device,
        mesh=mesh,
        in_specs=placed,
        out_specs=(P("ctx", "exp"), P("ctx", "exp"), P("ctx", "exp")),
        check_vma=False,
    )
```

```python
import functools

import jax
import jax.numpy as jnp
from jax import lax
from jax.experimental import pallas as pl
from jax.experimental.pallas import tpu as pltpu
from jax.sharding import PartitionSpec as P

DH = 128
TILE = 256
F32 = jnp.float32
BF16 = jnp.bfloat16
SCALE = 1.0 / DH

SMEM = pl.BlockSpec(memory_space=pltpu.SMEM)
VMEM = pl.BlockSpec(memory_space=pltpu.VMEM)
HBM = pl.BlockSpec(memory_space=pltpu.HBM)
LARGE = pl.CostEstimate(flops=1, bytes_accessed=40_000_000, transcendentals=0)
SMALL = pl.CostEstimate(flops=1, bytes_accessed=1, transcendentals=0)


def dot(left, right, left_dim, right_dim):
    return lax.dot_general(
        left, right, (((left_dim,), (right_dim,)), ((), ())), preferred_element_type=F32
    )


def silu_slope(value):
    sigma = jax.nn.sigmoid(value)
    return sigma * (1.0 + value * (1.0 - sigma))


def lanes_of(place_ref, slot, heads):
    head = lax.rem(place_ref[0] * (heads // 2) + slot, heads)
    return head, pl.ds(pl.multiple_of(head * DH, DH), DH)


def column(block_len):
    return lax.broadcasted_iota(jnp.int32, (block_len, 1), 0).astype(F32)


def decay_within(rate, block_len):
    rows = lax.broadcasted_iota(jnp.int32, (block_len, block_len), 0)
    cols = lax.broadcasted_iota(jnp.int32, (block_len, block_len), 1)
    distance = (rows - cols).astype(F32)
    return jnp.where(distance >= 0.0, jnp.exp(-rate * jnp.maximum(distance, 0.0)), 0.0)


def key_state_kernel(place_ref, rates_ref, k_ref, v_ref, mine_ref, other_ref):
    block_len, half = k_ref.shape[0], mine_ref.shape[0]
    steps = column(block_len)
    for slot in [*range(half, 2 * half), *range(half)]:
        head, lanes = lanes_of(place_ref, slot, 2 * half)
        power = jnp.exp(-rates_ref[head] * (block_len - steps))
        scaled = (k_ref[:, lanes].astype(F32) * power).astype(BF16)
        state_ref = (mine_ref, other_ref)[slot // half]
        state_ref[slot % half] = dot(scaled, v_ref[:, lanes], 0, 0).astype(BF16)


def pick_rows(choose_ref, rows, send_refs):
    capacity = choose_ref.shape[1]
    if capacity % 8:
        for k, send_ref in enumerate(send_refs):
            send_ref[...] = dot(choose_ref[k], rows, 1, 0).astype(BF16)
        return
    table = choose_ref[...].reshape(len(send_refs) * capacity, rows.shape[0])
    picked = dot(table.astype(BF16), rows, 1, 0)
    for k, send_ref in enumerate(send_refs):
        send_ref[...] = picked[k * capacity : (k + 1) * capacity].astype(BF16)


def route_kernel(
    place_ref, grad_ref, routes_ref, gates_ref, choose_ref, weigh_ref, *send_refs
):
    experts, capacity, block_len = choose_ref.shape
    rows = lax.broadcasted_iota(jnp.int32, (block_len, block_len), 0)
    cols = lax.broadcasted_iota(jnp.int32, (block_len, block_len), 1)

    first, second = routes_ref[0:1, :], routes_ref[1:2, :]
    names = lax.broadcasted_iota(jnp.int32, (32, block_len), 0)
    hit_first = jnp.where(names == first, 1.0, 0.0)
    hit_second = jnp.where(names == second, 1.0, 0.0)
    earlier = jnp.where(rows < cols, 1.0, 0.0).astype(BF16)
    before = dot((hit_first + hit_second).astype(BF16), earlier, 1, 0)
    slot_first = jnp.sum(before * hit_first, axis=0, keepdims=True).astype(jnp.int32)
    slot_second = jnp.sum(before * hit_second, axis=0, keepdims=True).astype(jnp.int32)
    slots = lax.broadcasted_iota(jnp.int32, (capacity, block_len), 0)
    for k in range(experts):
        expert = place_ref[1] ^ k
        named = ((slots == slot_first) & (first == expert)) | (
            (slots == slot_second) & (second == expert)
        )
        choose_ref[k] = jnp.where(named, 1.0, 0.0)
    pick_rows(choose_ref, grad_ref[...], send_refs)

    columns = jnp.concatenate(
        [first.astype(F32), second.astype(F32), slot_first.astype(F32), slot_second.astype(F32)]
        + [gates_ref[0:1, :], gates_ref[1:2, :]] + [jnp.zeros((2, block_len), F32)],
        axis=0,
    ).T
    first, second, slot_first, slot_second = [
        columns[:, i : i + 1].astype(jnp.int32) for i in range(4)
    ]
    slots = lax.broadcasted_iota(jnp.int32, (block_len, capacity), 1)
    for k in range(experts):
        expert = place_ref[1] ^ k
        one = jnp.where((slots == slot_first) & (first == expert), columns[:, 4:5], 0.0)
        two = jnp.where((slots == slot_second) & (second == expert), columns[:, 5:6], 0.0)
        weigh_ref[k] = (one + two).astype(BF16)


def intra_kernel(place_ref, rates_ref, q_ref, k_ref, v_ref, intra_ref, weights_ref):
    block_len, heads = q_ref.shape[0], weights_ref.shape[0]
    for slot in range(heads):
        head, lanes = lanes_of(place_ref, slot, heads)
        within = decay_within(rates_ref[head], block_len)
        scores = dot(q_ref[:, lanes], k_ref[:, lanes], 1, 1)
        weights = (SCALE * scores * within).astype(BF16)
        weights_ref[slot] = weights
        intra_ref[:, lanes] = dot(weights, v_ref[:, lanes], 1, 0)


def attend_kernel(
    place_ref, rates_ref, q_ref, intra_ref, choose_ref, mine_ref, other_ref, *refs
):
    send_refs, attn_ref = refs[:-1], refs[-1]
    block_len, half = q_ref.shape[0], mine_ref.shape[0]
    steps = column(block_len)
    for slot in range(2 * half):
        head, lanes = lanes_of(place_ref, slot, 2 * half)
        entering = (mine_ref, other_ref)[slot // half][slot % half]
        power = SCALE * jnp.exp(-rates_ref[head] * steps)
        inter = power * dot(q_ref[:, lanes], entering, 1, 0)
        attn_ref[:, lanes] = (intra_ref[:, lanes] + inter).astype(BF16)
    pick_rows(choose_ref, attn_ref[...], send_refs)


def grad_kernel(place_ref, rates_ref, q_ref, out_grad_ref, weigh_ref, *refs):
    experts = weigh_ref.shape[0]
    home_refs, (grad_ref, mine_ref, other_ref) = refs[:experts], refs[experts:]
    block_len, half = q_ref.shape[0], mine_ref.shape[0]
    steps = column(block_len)
    total = out_grad_ref[...].astype(F32)
    for k in range(experts):
        total = total + dot(weigh_ref[k], home_refs[k][...], 1, 0)
    grad_ref[...] = total.astype(BF16)
    for slot in [*range(half, 2 * half), *range(half)]:
        head, lanes = lanes_of(place_ref, slot, 2 * half)
        power = jnp.exp(-rates_ref[head] * (steps + 1.0))
        scaled = (q_ref[:, lanes].astype(F32) * power).astype(BF16)
        state_ref = (mine_ref, other_ref)[slot // half]
        state_ref[slot % half] = dot(scaled, grad_ref[:, lanes], 0, 0).astype(BF16)


def near_kernel(
    place_ref, rates_ref, q_ref, k_ref, v_ref, grad_ref, mine_ref, other_ref, weights_ref,
    query_ref, key_ref, value_ref,
):
    block_len, half = q_ref.shape[0], mine_ref.shape[0]
    steps = column(block_len)
    for slot in range(2 * half):
        head, lanes = lanes_of(place_ref, slot, 2 * half)
        rate = rates_ref[head]
        grad = grad_ref[:, lanes]
        entering = (mine_ref, other_ref)[slot // half][slot % half]
        within = decay_within(rate, block_len)
        dweights = (SCALE * dot(grad, v_ref[:, lanes], 1, 1) * within).astype(BF16)
        query = dot(dweights, k_ref[:, lanes], 1, 0)
        query = query + SCALE * jnp.exp(-rate * steps) * dot(grad, entering, 1, 1)
        query_ref[:, lanes] = query.astype(BF16)
        key_ref[:, lanes] = dot(dweights, q_ref[:, lanes], 0, 0)
        value_ref[:, lanes] = dot(weights_ref[slot], grad, 0, 0)


def far_kernel(
    place_ref, rates_ref, k_ref, v_ref, key_near, value_near, mine_ref, other_ref, key_ref, value_ref
):
    block_len, half = k_ref.shape[0], mine_ref.shape[0]
    steps = column(block_len)
    for slot in range(2 * half):
        head, lanes = lanes_of(place_ref, slot, 2 * half)
        leaving = (mine_ref, other_ref)[slot // half][slot % half]
        power = SCALE * jnp.exp(-rates_ref[head] * (block_len - 1.0 - steps))
        key_ref[:, lanes] = (
            key_near[:, lanes] + power * dot(v_ref[:, lanes], leaving, 1, 1)
        ).astype(BF16)
        value_ref[:, lanes] = (
            value_near[:, lanes] + power * dot(k_ref[:, lanes], leaving, 1, 0)
        ).astype(BF16)


def fetched(kernel, scalars, count, *refs):
    sources, rest = refs[scalars : scalars + count], refs[scalars + count : -1 - count]
    buffers, sems = refs[-1 - count : -1], refs[-1]
    copies = [
        pltpu.make_async_copy(source, buffer, sems.at[i])
        for i, (source, buffer) in enumerate(zip(sources, buffers))
    ]
    for copy in copies:
        copy.start()
    for copy in copies:
        copy.wait()
    kernel(*refs[:scalars], *buffers, *rest)


def call(kernel, out_shapes, scalars, arrays, scratch=(), cost=SMALL, fetch=0, limit=16):
    scratch = list(scratch)
    if fetch:
        kernel = functools.partial(fetched, kernel, len(scalars), fetch)
        scratch += [pltpu.VMEM(array.shape, array.dtype) for array in arrays[:fetch]]
        scratch += [pltpu.SemaphoreType.DMA((fetch,))]
    return pl.pallas_call(
        kernel,
        out_shape=list(out_shapes),
        in_specs=[SMEM] * len(scalars) + [HBM] * fetch + [VMEM] * (len(arrays) - fetch),
        out_specs=[VMEM] * len(out_shapes),
        scratch_shapes=scratch,
        compiler_params=pltpu.CompilerParams(vmem_limit_bytes=limit * 1024 * 1024),
        cost_estimate=cost,
    )(*scalars, *arrays)


def joined(refs):
    rows = [ref[...].astype(F32) for ref in refs]
    return rows[0] if len(rows) == 1 else jnp.concatenate(rows, axis=0)


def halves_kernel(turned, place_ref, weight_ref, *refs):
    sent_ref, kept_ref, rows_ref = refs[-3:]
    count = (len(refs) - 3) // 2
    own, other = joined(refs[:count]), joined(refs[count:-3])
    first = place_ref[2] == 0
    rows = [jnp.where(first, other, own), jnp.where(first, own, other)]
    rows_ref[...] = jnp.concatenate(rows, axis=0).astype(BF16)
    half, width = sent_ref.shape
    for start in range(0, width, TILE):
        lanes = slice(start, start + TILE)
        weight = weight_ref[lanes, :] if turned else weight_ref[:, lanes]
        out = dot(rows_ref[...], weight, 1, 1 if turned else 0)
        sent_ref[:, lanes] = out[:half].astype(BF16)
        kept_ref[:, lanes] = out[half:].astype(BF16)


def back_kernel(place_ref, weight_ref, mine_ref, got_ref, own_ref, other_ref, rows_ref):
    mine, got = mine_ref[...].astype(F32), got_ref[...].astype(F32)
    first = place_ref[2] == 0
    rows = [jnp.where(first, mine, got), jnp.where(first, got, mine)]
    rows_ref[...] = jnp.concatenate(rows, axis=0).astype(BF16)
    half, width = own_ref.shape
    for start in range(0, width, TILE):
        lanes = slice(start, start + TILE)
        out = dot(rows_ref[...], weight_ref[lanes, :], 1, 1)
        own_ref[:, lanes] = out[:half].astype(BF16)
        other_ref[:, lanes] = out[half:].astype(BF16)


def matmul_call(kernel, place, weight, arrays, rows, depth, width):
    out = jax.ShapeDtypeStruct((rows, width), BF16)
    return call(
        kernel, [out, out], (place,), (weight, *arrays),
        [pltpu.VMEM((2 * rows, depth), BF16)], limit=24,
    )


def sides_times(place, own, other, part, weight, turned, *events):
    blocks = 2 if len(part) * own[part[0]].shape[0] > 72 else 1
    each = len(part) // blocks
    join = lambda rows: rows[0] if len(rows) == 1 else jnp.concatenate(rows, axis=0)
    arrays = [
        join([side[k] for k in part[i * each : (i + 1) * each]])
        for side in (own, other)
        for i in range(blocks)
    ]
    arrays[0] = after(arrays[0], *events)
    rows, depth = blocks * arrays[0].shape[0], arrays[0].shape[1]
    width = weight.shape[0] if turned else weight.shape[1]
    return matmul_call(
        functools.partial(halves_kernel, turned), place, weight, arrays, rows, depth, width
    )


def swap(array, axis, distance):
    size = lax.axis_size(axis)
    return lax.ppermute(array, axis, [(i, i ^ distance) for i in range(size)])


def trade(array, pairs, partner):
    return lax.ppermute(
        array, "ctx", [(2 * partner(i) + s, 2 * i + s) for i in range(pairs) for s in (0, 1)]
    )


def after(array, *events):
    return lax.optimization_barrier((array,) + events)[0]


def head_power(rates, place, half, tokens):
    mine = lax.dynamic_slice(rates, (place[0] * half,), (half,))[:, None, None]
    return jnp.exp(-mine * tokens)


def scan_total(mine, other, rates, place, block_len, reverse, *events):
    side = 1 - place[0] if reverse else place[0]
    whole = head_power(rates, place, mine.shape[0], block_len)
    partner = after(swap(other, "ctx", 1), *events)
    first = jnp.where(side == 0, mine, partner).astype(F32)
    second = jnp.where(side == 0, partner, mine).astype(F32)
    return (whole * first + second).astype(BF16), partner


def scan_step(before, total, reach, rates, place, block_len, reverse, *events):
    half = total.shape[0]
    pairs = lax.axis_size("ctx") // 2
    pair = pairs - 1 - place[1] if reverse else place[1]
    if before is None:
        upto = total
    else:
        whole = head_power(rates, place, half, 2.0 * block_len)
        upto = (whole * before + total.astype(F32)).astype(BF16)
    upto = after(upto, *events)
    lower, offset = (pair & reach) == 0, pair & (reach - 1)
    got = None
    for j in range(reach):

        def partner(i, j=j):
            i = pairs - 1 - i if reverse else i
            start = i - i % (2 * reach)
            first, second = start + reach - 1, start + reach + j
            i = {first: second, second: first}.get(i, i)
            return pairs - 1 - i if reverse else i

        one = trade(upto, pairs, partner)
        got = one if got is None else jnp.where(offset == j, one, got)
    scale = head_power(rates, place, half, 2.0 * block_len * offset.astype(F32))
    grown = scale * got.astype(F32)
    kept = 0.0 if before is None else before
    return jnp.where(lower, kept, kept + grown), upto


def scan_ends(before, mine, partner, rates, place, block_len, reverse):
    side = 1 - place[0] if reverse else place[0]
    whole = head_power(rates, place, mine.shape[0], block_len)
    first = jnp.where(side == 0, mine, partner).astype(F32)
    second_meets = whole * before + first
    keep = jnp.where(side == 0, before, second_meets).astype(BF16)
    give = jnp.where(side == 0, second_meets, before).astype(BF16)
    return keep, give


def over_cores(sent, kept):
    return (kept.astype(F32) + swap(sent, "exp", 1).astype(F32)).astype(BF16)


def scatter_rest(part, bits):
    for bit in range(1, bits):
        mine = (lax.axis_index("exp") >> bit) & 1
        width = part.shape[1] // 2
        sent = lax.dynamic_slice_in_dim(part, (1 - mine) * width, width, 1)
        kept = lax.dynamic_slice_in_dim(part, mine * width, width, 1)
        part = (kept.astype(F32) + swap(sent, "exp", 1 << bit).astype(F32)).astype(BF16)
    return part


def gather_rest(part, bits):
    for bit in reversed(range(1, bits)):
        mine = (lax.axis_index("exp") >> bit) & 1
        got = swap(part, "exp", 1 << bit)
        part = jnp.concatenate(
            [jnp.where(mine == 0, part, got), jnp.where(mine == 0, got, part)], axis=1
        )
    return part


def on_device(
    queries, keys, values, out_grad, up_weight, down_weight, decay_rates, routes, gate_weights
):
    block_len, group = queries.shape
    heads = group // DH
    half = heads // 2
    experts = lax.axis_size("ctx") // 2
    bits = (lax.axis_size("exp") - 1).bit_length()
    capacity = block_len * 9 // (4 * experts)
    position = lax.axis_index("ctx").astype(jnp.int32)
    core = lax.axis_index("exp").astype(jnp.int32) & 1
    place = jnp.stack([position & 1, position >> 1, core])
    scalars = (place, decay_rates)
    up_local, down_local = up_weight[0], down_weight[0]
    quarter = max(experts // 4, 1)
    near_part = range(experts // 2)
    first_far = range(experts - quarter, experts)
    second_far = range(experts // 2, experts - quarter)
    states = jax.ShapeDtypeStruct((half, DH, DH), BF16)
    weight_sq = jax.ShapeDtypeStruct((heads, block_len, block_len), BF16)
    wide = jax.ShapeDtypeStruct((block_len, group), F32)
    slim = jax.ShapeDtypeStruct((block_len, group), BF16)
    choose_table = jax.ShapeDtypeStruct((experts, capacity, block_len), F32)
    weigh_table = jax.ShapeDtypeStruct((experts, block_len, capacity), BF16)
    slots = jax.ShapeDtypeStruct((capacity, group), BF16)

    reaches = [1 << i for i in range((experts - 1).bit_length())]
    pairs_of = lambda rows, k: swap(rows, "ctx", 2 * k) if k else rows

    key_mine, key_other = call(
        key_state_kernel, [states] * 2, scalars, (keys, values), cost=LARGE, fetch=2
    )
    choose, weigh, *send_grad = call(
        route_kernel, [choose_table, weigh_table] + [slots] * experts,
        (place,), (out_grad, routes.T, gate_weights.T), cost=LARGE, fetch=1,
    )
    intra, weights = call(
        intra_kernel, [wide, weight_sq], scalars, (queries, keys, values), cost=LARGE, fetch=3
    )
    def hidden_of(part, *events):
        return sides_times(place, grad_own, grad_other, part, down_local, True, *events)

    def pre_of(part, *events):
        return sides_times(place, in_own, in_other, part, up_local, False, *events)

    def over_exp(sent, kept):
        return scatter_rest(over_cores(sent, kept), bits)

    total, partner = scan_total(
        key_mine, key_other, decay_rates, place, block_len, False, send_grad[0]
    )
    grad_own, grad_other = {0: send_grad[0]}, {0: swap(send_grad[0], "ctx", 1)}
    before = None
    for index, reach in enumerate(reaches):
        events = [intra, grad_other[0]] if index == 1 else []
        before, upto = scan_step(
            before, total, reach, decay_rates, place, block_len, False, *events
        )
    for k in near_part[1:]:
        grad_own[k] = pairs_of(after(send_grad[k], upto), k)
        grad_other[k] = swap(grad_own[k], "ctx", 1)
    keep, give = scan_ends(before, key_mine, partner, decay_rates, place, block_len, False)
    for k in first_far:
        grad_own[k] = pairs_of(after(send_grad[k], give), k)
    given = swap(give, "ctx", 1)
    send_in = call(
        attend_kernel, [slots] * experts, scalars, (queries, intra, choose, keep, given),
        [pltpu.VMEM((block_len, group), BF16)],
    )
    in_own, in_other = {0: send_in[0]}, {0: swap(send_in[0], "ctx", 1)}
    for k in [*near_part[1:], *first_far]:
        in_own[k] = pairs_of(send_in[k], k)
    for k in first_far:
        grad_other[k] = swap(after(grad_own[k], send_in[0]), "ctx", 1)
    near_ready = [in_other[0], *[in_own[k] for k in near_part[1:]]]
    first_ready = [in_own[k] for k in first_far]
    hidden_near = hidden_of(near_part, *near_ready)
    hidden_first = hidden_of(first_far, hidden_near[0], *first_ready)
    for k in near_part[1:]:
        in_other[k] = swap(in_own[k], "ctx", 1)
    for k in first_far:
        in_other[k] = swap(in_own[k], "ctx", 1)
    for k in second_far:
        in_own[k] = pairs_of(after(send_in[k], *first_ready), k)
        grad_own[k] = pairs_of(after(send_grad[k], *first_ready), k)
    hidden_near = over_exp(*hidden_near)
    pre_near = pre_of(near_part, hidden_first[0], hidden_near)
    for k in second_far:
        in_other[k] = swap(after(in_own[k], pre_near[0]), "ctx", 1)
        grad_other[k] = swap(after(grad_own[k], pre_near[0]), "ctx", 1)
    hidden_first = over_exp(*hidden_first)
    pre_first = pre_of(first_far, pre_near[0], hidden_first)
    pre_near = over_exp(*pre_near)
    hidden_second = hidden_of(second_far, pre_first[0], pre_near)
    pre_second = pre_of(second_far, hidden_second[0])

    def slope_of(pre, grad):
        return (grad.astype(F32) * silu_slope(pre.astype(F32))).astype(BF16)

    returned = []

    def give_back(slope, *events):
        slope = gather_rest(slope, bits)
        got = swap(slope, "exp", 1)
        got = after(got, *events)
        back, other = matmul_call(
            back_kernel, place, up_local, (slope, got), *slope.shape, group
        )
        returned.append((back, swap(other, "ctx", 1)))
        return back

    event = give_back(slope_of(pre_near, hidden_near), pre_second[0])
    pre_first = over_exp(*pre_first)
    event = give_back(slope_of(pre_first, hidden_first), event)
    hidden_second, pre_second = over_exp(*hidden_second), over_exp(*pre_second)
    give_back(slope_of(pre_second, hidden_second), event)
    homes = {}
    for index, part in enumerate((near_part, first_far, second_far)):
        back, got = returned[index]
        if index < 2:
            got = after(got, returned[index + 1][0])
        rows = (back.astype(F32) + got.astype(F32)).astype(BF16)
        for i, k in enumerate(part):
            homes[k] = pairs_of(rows[i * capacity : (i + 1) * capacity], k)
    homes = [homes[k] for k in range(experts)]

    grad_out, query_mine, query_other = call(
        grad_kernel, [slim, states, states], scalars, (queries, out_grad, weigh, *homes)
    )
    total, partner = scan_total(
        query_mine, query_other, decay_rates, place, block_len, True
    )
    before = None
    for reach in reaches:
        before, _ = scan_step(before, total, reach, decay_rates, place, block_len, True)
    keep_in = keep
    keep, give = scan_ends(before, query_mine, partner, decay_rates, place, block_len, True)
    leaving = (keep, swap(give, "ctx", 1))
    query_g, key_near, value_near = call(
        near_kernel, [slim, wide, wide], scalars,
        (queries, keys, values, grad_out, keep_in, given, weights)
    )
    key_g, value_g = call(
        far_kernel, [slim, slim], scalars,
        (keys, values, key_near, value_near) + leaving
    )
    return query_g, key_g, value_g


def solution(mesh):
    placed = (
        P("ctx", "exp"),
        P("ctx", "exp"),
        P("ctx", "exp"),
        P("ctx", "exp"),
        P("ctx", "exp", None),
        P("ctx", None, "exp"),
        P("exp"),
        P("ctx", None),
        P("ctx", None),
    )
    return jax.shard_map(
        on_device,
        mesh=mesh,
        in_specs=placed,
        out_specs=(P("ctx", "exp"), P("ctx", "exp"), P("ctx", "exp")),
        check_vma=False,
    )
```

```python
import functools

import jax
import jax.numpy as jnp
from jax import lax
from jax.experimental import pallas as pl
from jax.experimental.pallas import tpu as pltpu
from jax.sharding import PartitionSpec as P

DH = 128
F32 = jnp.float32
BF16 = jnp.bfloat16
SCALE = 1.0 / DH

SMEM = pl.BlockSpec(memory_space=pltpu.SMEM)
VMEM = pl.BlockSpec(memory_space=pltpu.VMEM)


def dot(left, right, left_dim, right_dim):
    return lax.dot_general(
        left, right, (((left_dim,), (right_dim,)), ((), ())), preferred_element_type=F32
    )


def silu_slope(value):
    sigma = jax.nn.sigmoid(value)
    return sigma * (1.0 + value * (1.0 - sigma))


def lanes_of(place_ref, slot, heads):
    head = lax.rem(place_ref[0] * (heads // 2) + slot, heads)
    return head, pl.ds(pl.multiple_of(head * DH, DH), DH)


def column(block_len):
    return lax.broadcasted_iota(jnp.int32, (block_len, 1), 0).astype(F32)


def decay_within(rate, block_len):
    rows = lax.broadcasted_iota(jnp.int32, (block_len, block_len), 0)
    cols = lax.broadcasted_iota(jnp.int32, (block_len, block_len), 1)
    distance = (rows - cols).astype(F32)
    return jnp.where(distance >= 0.0, jnp.exp(-rate * jnp.maximum(distance, 0.0)), 0.0)


def key_state_kernel(place_ref, rates_ref, k_ref, v_ref, mine_ref, other_ref):
    block_len, half = k_ref.shape[0], mine_ref.shape[0]
    steps = column(block_len)
    for slot in [*range(half, 2 * half), *range(half)]:
        head, lanes = lanes_of(place_ref, slot, 2 * half)
        power = jnp.exp(-rates_ref[head] * (block_len - steps))
        scaled = (k_ref[:, lanes].astype(F32) * power).astype(BF16)
        state_ref = (mine_ref, other_ref)[slot // half]
        state_ref[slot % half] = dot(scaled, v_ref[:, lanes], 0, 0).astype(BF16)


def pick_rows(choose_ref, rows, send_refs):
    capacity = choose_ref.shape[1]
    if capacity % 8:
        for k, send_ref in enumerate(send_refs):
            send_ref[...] = dot(choose_ref[k], rows, 1, 0).astype(BF16)
        return
    table = choose_ref[...].reshape(len(send_refs) * capacity, rows.shape[0])
    picked = dot(table.astype(BF16), rows, 1, 0)
    for k, send_ref in enumerate(send_refs):
        send_ref[...] = picked[k * capacity : (k + 1) * capacity].astype(BF16)


def route_kernel(
    place_ref, routes_ref, gates_ref, grad_ref, choose_ref, weigh_ref, *send_refs
):
    experts, capacity, block_len = choose_ref.shape
    rows = lax.broadcasted_iota(jnp.int32, (block_len, block_len), 0)
    cols = lax.broadcasted_iota(jnp.int32, (block_len, block_len), 1)

    first, second = routes_ref[0:1, :], routes_ref[1:2, :]
    names = lax.broadcasted_iota(jnp.int32, (32, block_len), 0)
    hit_first = jnp.where(names == first, 1.0, 0.0)
    hit_second = jnp.where(names == second, 1.0, 0.0)
    earlier = jnp.where(rows < cols, 1.0, 0.0).astype(BF16)
    before = dot((hit_first + hit_second).astype(BF16), earlier, 1, 0)
    slot_first = jnp.sum(before * hit_first, axis=0, keepdims=True).astype(jnp.int32)
    slot_second = jnp.sum(before * hit_second, axis=0, keepdims=True).astype(jnp.int32)
    slots = lax.broadcasted_iota(jnp.int32, (capacity, block_len), 0)
    for k in range(experts):
        expert = place_ref[1] ^ k
        named = ((slots == slot_first) & (first == expert)) | (
            (slots == slot_second) & (second == expert)
        )
        choose_ref[k] = jnp.where(named, 1.0, 0.0)
    pick_rows(choose_ref, grad_ref[...], send_refs)

    columns = jnp.concatenate(
        [first.astype(F32), second.astype(F32), slot_first.astype(F32), slot_second.astype(F32)]
        + [gates_ref[0:1, :], gates_ref[1:2, :]] + [jnp.zeros((2, block_len), F32)],
        axis=0,
    ).T
    first, second, slot_first, slot_second = [
        columns[:, i : i + 1].astype(jnp.int32) for i in range(4)
    ]
    slots = lax.broadcasted_iota(jnp.int32, (block_len, capacity), 1)
    for k in range(experts):
        expert = place_ref[1] ^ k
        one = jnp.where((slots == slot_first) & (first == expert), columns[:, 4:5], 0.0)
        two = jnp.where((slots == slot_second) & (second == expert), columns[:, 5:6], 0.0)
        weigh_ref[k] = (one + two).astype(BF16)


def intra_kernel(place_ref, rates_ref, q_ref, k_ref, v_ref, intra_ref, weights_ref):
    block_len, heads = q_ref.shape[0], weights_ref.shape[0]
    for slot in range(heads):
        head, lanes = lanes_of(place_ref, slot, heads)
        within = decay_within(rates_ref[head], block_len)
        scores = dot(q_ref[:, lanes], k_ref[:, lanes], 1, 1)
        weights = (SCALE * scores * within).astype(BF16)
        weights_ref[slot] = weights
        intra_ref[:, lanes] = dot(weights, v_ref[:, lanes], 1, 0)


def attend_kernel(
    place_ref, rates_ref, q_ref, intra_ref, choose_ref, mine_ref, other_ref, *refs
):
    send_refs, attn_ref = refs[:-1], refs[-1]
    block_len, half = q_ref.shape[0], mine_ref.shape[0]
    steps = column(block_len)
    for slot in range(2 * half):
        head, lanes = lanes_of(place_ref, slot, 2 * half)
        entering = (mine_ref, other_ref)[slot // half][slot % half]
        power = SCALE * jnp.exp(-rates_ref[head] * steps)
        inter = power * dot(q_ref[:, lanes], entering, 1, 0)
        attn_ref[:, lanes] = (intra_ref[:, lanes] + inter).astype(BF16)
    pick_rows(choose_ref, attn_ref[...], send_refs)


def grad_kernel(place_ref, rates_ref, q_ref, out_grad_ref, weigh_ref, *refs):
    experts = weigh_ref.shape[0]
    home_refs, (grad_ref, mine_ref, other_ref) = refs[:experts], refs[experts:]
    block_len, half = q_ref.shape[0], mine_ref.shape[0]
    steps = column(block_len)
    total = out_grad_ref[...].astype(F32)
    for k in range(experts):
        total = total + dot(weigh_ref[k], home_refs[k][...], 1, 0)
    grad_ref[...] = total.astype(BF16)
    for slot in [*range(half, 2 * half), *range(half)]:
        head, lanes = lanes_of(place_ref, slot, 2 * half)
        power = jnp.exp(-rates_ref[head] * (steps + 1.0))
        scaled = (q_ref[:, lanes].astype(F32) * power).astype(BF16)
        state_ref = (mine_ref, other_ref)[slot // half]
        state_ref[slot % half] = dot(scaled, grad_ref[:, lanes], 0, 0).astype(BF16)


def near_kernel(
    place_ref, rates_ref, q_ref, k_ref, v_ref, grad_ref, mine_ref, other_ref, weights_ref,
    query_ref, key_ref, value_ref,
):
    block_len, half = q_ref.shape[0], mine_ref.shape[0]
    steps = column(block_len)
    for slot in range(2 * half):
        head, lanes = lanes_of(place_ref, slot, 2 * half)
        rate = rates_ref[head]
        grad = grad_ref[:, lanes]
        entering = (mine_ref, other_ref)[slot // half][slot % half]
        within = decay_within(rate, block_len)
        dweights = (SCALE * dot(grad, v_ref[:, lanes], 1, 1) * within).astype(BF16)
        query = dot(dweights, k_ref[:, lanes], 1, 0)
        query = query + SCALE * jnp.exp(-rate * steps) * dot(grad, entering, 1, 1)
        query_ref[:, lanes] = query.astype(BF16)
        key_ref[:, lanes] = dot(dweights, q_ref[:, lanes], 0, 0)
        value_ref[:, lanes] = dot(weights_ref[slot], grad, 0, 0)


def far_kernel(
    place_ref, rates_ref, k_ref, v_ref, key_near, value_near, mine_ref, other_ref, key_ref, value_ref
):
    block_len, half = k_ref.shape[0], mine_ref.shape[0]
    steps = column(block_len)
    for slot in range(2 * half):
        head, lanes = lanes_of(place_ref, slot, 2 * half)
        leaving = (mine_ref, other_ref)[slot // half][slot % half]
        power = SCALE * jnp.exp(-rates_ref[head] * (block_len - 1.0 - steps))
        key_ref[:, lanes] = (
            key_near[:, lanes] + power * dot(v_ref[:, lanes], leaving, 1, 1)
        ).astype(BF16)
        value_ref[:, lanes] = (
            value_near[:, lanes] + power * dot(k_ref[:, lanes], leaving, 1, 0)
        ).astype(BF16)


def call(kernel, out_shapes, scalars, arrays, scratch=(), micros=1.0):
    return pl.pallas_call(
        kernel,
        out_shape=list(out_shapes),
        in_specs=[SMEM] * len(scalars) + [VMEM] * len(arrays),
        out_specs=[VMEM] * len(out_shapes),
        scratch_shapes=list(scratch),
        compiler_params=pltpu.CompilerParams(vmem_limit_bytes=16 * 1024 * 1024),
        cost_estimate=pl.CostEstimate(
            flops=1, bytes_accessed=int(micros * 3.69e6), transcendentals=0
        ),
    )(*scalars, *arrays)


def swap(array, axis, distance):
    size = lax.axis_size(axis)
    return lax.ppermute(array, axis, [(i, i ^ distance) for i in range(size)])


def trade(array, pairs, partner):
    return lax.ppermute(
        array, "ctx", [(2 * partner(i) + s, 2 * i + s) for i in range(pairs) for s in (0, 1)]
    )


def after(array, *events):
    return lax.optimization_barrier((array,) + events)[0]


def head_power(rates, place, half, tokens):
    mine = lax.dynamic_slice(rates, (place[0] * half,), (half,))[:, None, None]
    return jnp.exp(-mine * tokens)


def scan_total(mine, other, rates, place, block_len, reverse, *events):
    side = 1 - place[0] if reverse else place[0]
    whole = head_power(rates, place, mine.shape[0], block_len)
    partner = after(swap(other, "ctx", 1), *events)
    first = jnp.where(side == 0, mine, partner).astype(F32)
    second = jnp.where(side == 0, partner, mine).astype(F32)
    return (whole * first + second).astype(BF16), partner


def scan_step(before, total, reach, rates, place, block_len, reverse, *events):
    half = total.shape[0]
    pairs = lax.axis_size("ctx") // 2
    pair = pairs - 1 - place[1] if reverse else place[1]
    if before is None:
        upto = total
    else:
        whole = head_power(rates, place, half, 2.0 * block_len)
        upto = (whole * before + total.astype(F32)).astype(BF16)
    upto = after(upto, *events)
    lower, offset = (pair & reach) == 0, pair & (reach - 1)
    got = None
    for j in range(reach):

        def partner(i, j=j):
            i = pairs - 1 - i if reverse else i
            start = i - i % (2 * reach)
            first, second = start + reach - 1, start + reach + j
            i = {first: second, second: first}.get(i, i)
            return pairs - 1 - i if reverse else i

        one = trade(upto, pairs, partner)
        got = one if got is None else jnp.where(offset == j, one, got)
    scale = head_power(rates, place, half, 2.0 * block_len * offset.astype(F32))
    grown = scale * got.astype(F32)
    kept = 0.0 if before is None else before
    return jnp.where(lower, kept, kept + grown), upto


def scan_ends(before, mine, partner, rates, place, block_len, reverse):
    side = 1 - place[0] if reverse else place[0]
    whole = head_power(rates, place, mine.shape[0], block_len)
    first = jnp.where(side == 0, mine, partner).astype(F32)
    second_meets = whole * before + first
    keep = jnp.where(side == 0, before, second_meets).astype(BF16)
    give = jnp.where(side == 0, second_meets, before).astype(BF16)
    return keep, give


def sides_product(own, other, part, multiply, *events):
    rows = [side[k] for side in (own, other) for k in part]
    whole = multiply(after(jnp.concatenate(rows, axis=0), *events)).astype(BF16)
    return whole.reshape(2, whole.shape[0] // 2, whole.shape[1])


def sum_sides(whole):
    mine = lax.axis_index("exp") & 1
    sent = lax.dynamic_index_in_dim(whole, 1 - mine, 0, False)
    return over_cores(sent, lax.dynamic_index_in_dim(whole, mine, 0, False))


def sum_over_cores(own, other, part, multiply, *events):
    mine = lax.axis_index("exp") & 1
    rows = lambda flag: jnp.concatenate(
        [jnp.where(flag == 0, own[k], other[k]) for k in part], axis=0
    )
    sent = multiply(after(rows(1 - mine), *events)).astype(BF16)
    kept = multiply(after(rows(mine), sent)).astype(BF16)
    return sent, kept


def over_cores(sent, kept):
    return (kept.astype(F32) + swap(sent, "exp", 1).astype(F32)).astype(BF16)


def sum_over_rest(part, bits):
    for bit in range(1, bits):
        part = (part.astype(F32) + swap(part, "exp", 1 << bit).astype(F32)).astype(BF16)
    return part


def on_device(
    queries, keys, values, out_grad, up_weight, down_weight, decay_rates, routes, gate_weights
):
    block_len, group = queries.shape
    heads = group // DH
    half = heads // 2
    experts = lax.axis_size("ctx") // 2
    bits = (lax.axis_size("exp") - 1).bit_length()
    capacity = block_len * 9 // (4 * experts)
    position = lax.axis_index("ctx").astype(jnp.int32)
    core = lax.axis_index("exp").astype(jnp.int32) & 1
    place = jnp.stack([position & 1, position >> 1, core])
    scalars = (place, decay_rates)
    up_local, down_local = up_weight[0], down_weight[0]
    quarter = max(experts // 4, 1)
    near_part = range(experts // 2)
    first_far = range(experts - quarter, experts)
    second_far = range(experts // 2, experts - quarter)
    states = jax.ShapeDtypeStruct((half, DH, DH), BF16)
    weight_sq = jax.ShapeDtypeStruct((heads, block_len, block_len), BF16)
    wide = jax.ShapeDtypeStruct((block_len, group), F32)
    slim = jax.ShapeDtypeStruct((block_len, group), BF16)
    choose_table = jax.ShapeDtypeStruct((experts, capacity, block_len), F32)
    weigh_table = jax.ShapeDtypeStruct((experts, block_len, capacity), BF16)
    slots = jax.ShapeDtypeStruct((capacity, group), BF16)

    reaches = [1 << i for i in range((experts - 1).bit_length())]
    pairs_of = lambda rows, k: swap(rows, "ctx", 2 * k) if k else rows

    key_mine, key_other = call(key_state_kernel, [states] * 2, scalars, (keys, values))
    choose, weigh, *send_grad = call(
        route_kernel, [choose_table, weigh_table] + [slots] * experts,
        (place,), (routes.T, gate_weights.T, out_grad), micros=1.2
    )
    intra, weights = call(
        intra_kernel, [wide, weight_sq], scalars, (queries, keys, values), micros=2.5
    )

    total, partner = scan_total(
        key_mine, key_other, decay_rates, place, block_len, False, send_grad[0]
    )
    by_down = lambda rows: dot(rows, down_local, 1, 1)
    by_up = lambda rows: dot(rows, up_local, 1, 0)
    grad_own, grad_other = {0: send_grad[0]}, {0: swap(send_grad[0], "ctx", 1)}
    for k in near_part[1:]:
        grad_own[k] = pairs_of(after(send_grad[k], total), k)
        grad_other[k] = swap(grad_own[k], "ctx", 1)
    before = None
    for index, reach in enumerate(reaches):
        events = [intra, grad_other[0], *grad_own.values()] if index == 1 else []
        before, upto = scan_step(
            before, total, reach, decay_rates, place, block_len, False, *events
        )
    hidden_near = sides_product(grad_own, grad_other, near_part, by_down, upto)
    before, hidden_near = lax.optimization_barrier((before, hidden_near))
    hidden_near = sum_sides(hidden_near)
    keep, give = scan_ends(before, key_mine, partner, decay_rates, place, block_len, False)
    for k in first_far:
        grad_own[k] = pairs_of(after(send_grad[k], give), k)

    given = swap(give, "ctx", 1)
    given, hidden_near = lax.optimization_barrier((given, hidden_near))
    send_in = call(
        attend_kernel, [slots] * experts, scalars, (queries, intra, choose, keep, given),
        [pltpu.VMEM((block_len, group), BF16)],
    )
    hidden_near = sum_over_rest(hidden_near, bits)
    for k in first_far:
        grad_other[k] = swap(after(grad_own[k], send_in[0]), "ctx", 1)
    hidden_first = sum_sides(
        sides_product(grad_own, grad_other, first_far, by_down, send_in[0])
    )

    in_own, in_other = {0: send_in[0]}, {}
    for k in [*near_part[1:], *first_far]:
        in_own[k] = pairs_of(send_in[k], k)
    for k in second_far:
        in_own[k] = pairs_of(after(send_in[k], in_own[first_far[0]]), k)
        grad_own[k] = pairs_of(after(send_grad[k], in_own[first_far[0]]), k)
    for k in [*near_part, *first_far]:
        in_other[k] = swap(in_own[k], "ctx", 1)

    pre_near = over_cores(
        *sum_over_cores(in_own, in_other, near_part, by_up, hidden_first, hidden_near)
    )
    pre_first = sum_over_cores(in_own, in_other, first_far, by_up, pre_near)
    for k in second_far:
        grad_other[k] = swap(after(grad_own[k], pre_first[0]), "ctx", 1)
        in_other[k] = swap(after(in_own[k], pre_first[0]), "ctx", 1)
    pre_first = over_cores(*pre_first)
    hidden_second = sum_sides(
        sides_product(grad_own, grad_other, second_far, by_down, pre_first)
    )
    pre_second = over_cores(*sum_over_cores(in_own, in_other, second_far, by_up, hidden_second))

    homes = {}
    back = None
    for part, pre, hidden in (
        (near_part, pre_near, hidden_near),
        (first_far, pre_first, hidden_first),
        (second_far, pre_second, hidden_second),
    ):
        pre = sum_over_rest(pre, bits)
        if part is not near_part:
            hidden = sum_over_rest(hidden, bits)
        slope = (hidden.astype(F32) * silu_slope(pre.astype(F32))).astype(BF16)
        got = swap(slope, "exp", 1)
        if back is not None:
            got = after(got, back)
        slope = jnp.concatenate(
            [jnp.where(core == 0, slope, got), jnp.where(core == 0, got, slope)], axis=0
        )
        back = dot(slope, up_local, 1, 1).astype(BF16)
        blocks = back.reshape(2, len(part) * capacity, group)
        got = swap(blocks[1], "ctx", 1)
        rows = (blocks[0].astype(F32) + got.astype(F32)).astype(BF16)
        for i, k in enumerate(part):
            homes[k] = pairs_of(rows[i * capacity : (i + 1) * capacity], k)
    homes = [homes[k] for k in range(experts)]

    grad_out, query_mine, query_other = call(
        grad_kernel, [slim, states, states], scalars, (queries, out_grad, weigh, *homes)
    )
    total, partner = scan_total(
        query_mine, query_other, decay_rates, place, block_len, True
    )
    before = None
    for reach in reaches:
        before, _ = scan_step(before, total, reach, decay_rates, place, block_len, True)
    keep_in = keep
    keep, give = scan_ends(before, query_mine, partner, decay_rates, place, block_len, True)
    leaving = (keep, swap(give, "ctx", 1))
    query_g, key_near, value_near = call(
        near_kernel, [slim, wide, wide], scalars,
        (queries, keys, values, grad_out, keep_in, given, weights), micros=4.0
    )
    key_g, value_g = call(
        far_kernel, [slim, slim], scalars,
        (keys, values, key_near, value_near) + leaving, micros=2.0
    )
    return query_g, key_g, value_g


def solution(mesh):
    placed = (
        P("ctx", "exp"),
        P("ctx", "exp"),
        P("ctx", "exp"),
        P("ctx", "exp"),
        P("ctx", "exp", None),
        P("ctx", None, "exp"),
        P("exp"),
        P("ctx", None),
        P("ctx", None),
    )
    return jax.shard_map(
        on_device,
        mesh=mesh,
        in_specs=placed,
        out_specs=(P("ctx", "exp"), P("ctx", "exp"), P("ctx", "exp")),
        check_vma=False,
    )
```

```python
import functools

import jax
import jax.numpy as jnp
from jax import lax
from jax.experimental import pallas as pl
from jax.experimental.pallas import tpu as pltpu
from jax.sharding import PartitionSpec as P

DH = 128
F32 = jnp.float32
BF16 = jnp.bfloat16
SCALE = 1.0 / DH

SMEM = pl.BlockSpec(memory_space=pltpu.SMEM)
VMEM = pl.BlockSpec(memory_space=pltpu.VMEM)
LARGE = pl.CostEstimate(flops=1, bytes_accessed=40_000_000, transcendentals=0)
SMALL = pl.CostEstimate(flops=1, bytes_accessed=1, transcendentals=0)


def dot(left, right, left_dim, right_dim):
    return lax.dot_general(
        left, right, (((left_dim,), (right_dim,)), ((), ())), preferred_element_type=F32
    )


def silu_slope(value):
    sigma = jax.nn.sigmoid(value)
    return sigma * (1.0 + value * (1.0 - sigma))


def lanes_of(place_ref, slot, heads):
    head = lax.rem(place_ref[0] * (heads // 2) + slot, heads)
    return head, pl.ds(pl.multiple_of(head * DH, DH), DH)


def column(block_len):
    return lax.broadcasted_iota(jnp.int32, (block_len, 1), 0).astype(F32)


def decay_within(rate, block_len):
    rows = lax.broadcasted_iota(jnp.int32, (block_len, block_len), 0)
    cols = lax.broadcasted_iota(jnp.int32, (block_len, block_len), 1)
    distance = (rows - cols).astype(F32)
    return jnp.where(distance >= 0.0, jnp.exp(rate * jnp.maximum(distance, 0.0)), 0.0)


def key_state_kernel(place_ref, rates_ref, pair_ref, mine_ref, other_ref):
    block_len, half = pair_ref.shape[0] // 2, mine_ref.shape[0]
    steps = column(block_len)
    for slot in [*range(half, 2 * half), *range(half)]:
        head, lanes = lanes_of(place_ref, slot, 2 * half)
        power = jnp.exp(rates_ref[head] * (block_len - steps))
        scaled = (pair_ref[:block_len, lanes].astype(F32) * power).astype(BF16)
        state_ref = (mine_ref, other_ref)[slot // half]
        state_ref[slot % half] = dot(scaled, pair_ref[block_len:, lanes], 0, 0).astype(BF16)


def pick_rows(choose_ref, rows, send_refs):
    capacity = choose_ref.shape[1]
    if capacity % 8:
        for k, send_ref in enumerate(send_refs):
            send_ref[...] = dot(choose_ref[k], rows, 1, 0).astype(BF16)
        return
    table = choose_ref[...].reshape(len(send_refs) * capacity, rows.shape[0])
    picked = dot(table.astype(BF16), rows, 1, 0)
    for k, send_ref in enumerate(send_refs):
        send_ref[...] = picked[k * capacity : (k + 1) * capacity].astype(BF16)


def route_kernel(
    place_ref, slots_ref, grad_ref, choose_ref, weigh_ref, *send_refs
):
    experts, capacity, block_len = choose_ref.shape
    rows = lax.broadcasted_iota(jnp.int32, (block_len, block_len), 0)
    cols = lax.broadcasted_iota(jnp.int32, (block_len, block_len), 1)

    first, second = [slots_ref[i : i + 1, :].astype(jnp.int32) for i in range(2)]
    names = lax.broadcasted_iota(jnp.int32, (32, block_len), 0)
    hit_first = jnp.where(names == first, 1.0, 0.0)
    hit_second = jnp.where(names == second, 1.0, 0.0)
    earlier = jnp.where(rows < cols, 1.0, 0.0).astype(BF16)
    before = dot((hit_first + hit_second).astype(BF16), earlier, 1, 0)
    slot_first = jnp.sum(before * hit_first, axis=0, keepdims=True).astype(jnp.int32)
    slot_second = jnp.sum(before * hit_second, axis=0, keepdims=True).astype(jnp.int32)
    slots = lax.broadcasted_iota(jnp.int32, (capacity, block_len), 0)
    for k in range(experts):
        expert = place_ref[1] ^ k
        named = ((slots == slot_first) & (first == expert)) | (
            (slots == slot_second) & (second == expert)
        )
        choose_ref[k] = jnp.where(named, 1.0, 0.0)
    pick_rows(choose_ref, grad_ref[...], send_refs)

    columns = jnp.concatenate(
        [first.astype(F32), second.astype(F32), slot_first.astype(F32), slot_second.astype(F32)]
        + [slots_ref[2:3, :], slots_ref[3:4, :]] + [jnp.zeros((2, block_len), F32)],
        axis=0,
    ).T
    first, second, slot_first, slot_second = [
        columns[:, i : i + 1].astype(jnp.int32) for i in range(4)
    ]
    slots = lax.broadcasted_iota(jnp.int32, (block_len, capacity), 1)
    for k in range(experts):
        expert = place_ref[1] ^ k
        one = jnp.where((slots == slot_first) & (first == expert), columns[:, 4:5], 0.0)
        two = jnp.where((slots == slot_second) & (second == expert), columns[:, 5:6], 0.0)
        weigh_ref[k] = (one + two).astype(BF16)


def intra_kernel(place_ref, rates_ref, q_ref, pair_ref, intra_ref, weights_ref):
    block_len, heads = q_ref.shape[0], weights_ref.shape[0]
    for slot in range(heads):
        head, lanes = lanes_of(place_ref, slot, heads)
        within = decay_within(rates_ref[head], block_len)
        scores = dot(q_ref[:, lanes], pair_ref[:block_len, lanes], 1, 1)
        weights = (SCALE * scores * within).astype(BF16)
        weights_ref[slot] = weights
        intra_ref[:, lanes] = dot(weights, pair_ref[block_len:, lanes], 1, 0)


def attend_kernel(
    place_ref, rates_ref, q_ref, intra_ref, choose_ref, mine_ref, other_ref, *refs
):
    send_refs, attn_ref = refs[:-1], refs[-1]
    block_len, half = q_ref.shape[0], mine_ref.shape[0]
    steps = column(block_len)
    for slot in range(2 * half):
        head, lanes = lanes_of(place_ref, slot, 2 * half)
        entering = (mine_ref, other_ref)[slot // half][slot % half]
        power = SCALE * jnp.exp(rates_ref[head] * steps)
        inter = power * dot(q_ref[:, lanes], entering, 1, 0)
        attn_ref[:, lanes] = (intra_ref[:, lanes] + inter).astype(BF16)
    pick_rows(choose_ref, attn_ref[...], send_refs)


def grad_kernel(place_ref, rates_ref, q_ref, out_grad_ref, weigh_ref, *refs):
    experts = weigh_ref.shape[0]
    home_refs, (grad_ref, mine_ref, other_ref) = refs[:experts], refs[experts:]
    block_len, half = q_ref.shape[0], mine_ref.shape[0]
    steps = column(block_len)
    total = out_grad_ref[...].astype(F32)
    for k in range(experts):
        total = total + dot(weigh_ref[k], home_refs[k][...], 1, 0)
    grad_ref[...] = total.astype(BF16)
    for slot in [*range(half, 2 * half), *range(half)]:
        head, lanes = lanes_of(place_ref, slot, 2 * half)
        power = jnp.exp(rates_ref[head] * (steps + 1.0))
        scaled = (q_ref[:, lanes].astype(F32) * power).astype(BF16)
        state_ref = (mine_ref, other_ref)[slot // half]
        state_ref[slot % half] = dot(scaled, grad_ref[:, lanes], 0, 0).astype(BF16)


def near_kernel(
    place_ref, rates_ref, q_ref, pair_ref, grad_ref, mine_ref, other_ref, weights_ref,
    query_ref, key_ref, value_ref,
):
    block_len, half = q_ref.shape[0], mine_ref.shape[0]
    steps = column(block_len)
    for slot in range(2 * half):
        head, lanes = lanes_of(place_ref, slot, 2 * half)
        rate = rates_ref[head]
        grad = grad_ref[:, lanes]
        entering = (mine_ref, other_ref)[slot // half][slot % half]
        within = decay_within(rate, block_len)
        dweights = (SCALE * dot(grad, pair_ref[block_len:, lanes], 1, 1) * within).astype(BF16)
        query = dot(dweights, pair_ref[:block_len, lanes], 1, 0)
        query = query + SCALE * jnp.exp(rate * steps) * dot(grad, entering, 1, 1)
        query_ref[:, lanes] = query.astype(BF16)
        key_ref[:, lanes] = dot(dweights, q_ref[:, lanes], 0, 0)
        value_ref[:, lanes] = dot(weights_ref[slot], grad, 0, 0)


def far_kernel(
    place_ref, rates_ref, pair_ref, key_near, value_near, mine_ref, other_ref, key_ref, value_ref
):
    block_len, half = pair_ref.shape[0] // 2, mine_ref.shape[0]
    steps = column(block_len)
    for slot in range(2 * half):
        head, lanes = lanes_of(place_ref, slot, 2 * half)
        leaving = (mine_ref, other_ref)[slot // half][slot % half]
        power = SCALE * jnp.exp(rates_ref[head] * (block_len - 1.0 - steps))
        key_ref[:, lanes] = (
            key_near[:, lanes] + power * dot(pair_ref[block_len:, lanes], leaving, 1, 1)
        ).astype(BF16)
        value_ref[:, lanes] = (
            value_near[:, lanes] + power * dot(pair_ref[:block_len, lanes], leaving, 1, 0)
        ).astype(BF16)


def call(kernel, out_shapes, scalars, arrays, scratch=(), cost=SMALL):
    return pl.pallas_call(
        kernel,
        out_shape=list(out_shapes),
        in_specs=[SMEM] * len(scalars) + [VMEM] * len(arrays),
        out_specs=[VMEM] * len(out_shapes),
        scratch_shapes=list(scratch),
        compiler_params=pltpu.CompilerParams(vmem_limit_bytes=16 * 1024 * 1024),
        cost_estimate=cost,
    )(*scalars, *arrays)


def swap(array, axis, distance):
    size = lax.axis_size(axis)
    return lax.ppermute(array, axis, [(i, i ^ distance) for i in range(size)])


def trade(array, pairs, partner):
    return lax.ppermute(
        array, "ctx", [(2 * partner(i) + s, 2 * i + s) for i in range(pairs) for s in (0, 1)]
    )


def after(array, *events):
    return lax.optimization_barrier((array,) + events)[0]


def head_power(rates, place, half, tokens):
    mine = lax.dynamic_slice(rates, (place[0] * half,), (half,))[:, None, None]
    return jnp.exp(-mine * tokens)


def scan_total(mine, other, rates, place, block_len, reverse, *events):
    side = 1 - place[0] if reverse else place[0]
    whole = head_power(rates, place, mine.shape[0], block_len)
    partner = after(swap(other, "ctx", 1), *events)
    first = jnp.where(side == 0, mine, partner).astype(F32)
    second = jnp.where(side == 0, partner, mine).astype(F32)
    return (whole * first + second).astype(BF16), partner


def scan_step(before, total, reach, rates, place, block_len, reverse, *events):
    half = total.shape[0]
    pairs = lax.axis_size("ctx") // 2
    pair = pairs - 1 - place[1] if reverse else place[1]
    if before is None:
        upto = total
    else:
        whole = head_power(rates, place, half, 2.0 * block_len)
        upto = (whole * before + total.astype(F32)).astype(BF16)
    upto = after(upto, *events)
    lower, offset = (pair & reach) == 0, pair & (reach - 1)
    got = None
    for j in range(reach):

        def partner(i, j=j):
            i = pairs - 1 - i if reverse else i
            start = i - i % (2 * reach)
            first, second = start + reach - 1, start + reach + j
            i = {first: second, second: first}.get(i, i)
            return pairs - 1 - i if reverse else i

        one = trade(upto, pairs, partner)
        got = one if got is None else jnp.where(offset == j, one, got)
    scale = head_power(rates, place, half, 2.0 * block_len * offset.astype(F32))
    grown = scale * got.astype(F32)
    kept = 0.0 if before is None else before
    return jnp.where(lower, kept, kept + grown), upto


def scan_ends(before, mine, partner, rates, place, block_len, reverse):
    side = 1 - place[0] if reverse else place[0]
    whole = head_power(rates, place, mine.shape[0], block_len)
    first = jnp.where(side == 0, mine, partner).astype(F32)
    second_meets = whole * before + first
    keep = jnp.where(side == 0, before, second_meets).astype(BF16)
    give = jnp.where(side == 0, second_meets, before).astype(BF16)
    return keep, give


def two_products(own, other, part, multiply, *events):
    mine = lax.axis_index("exp") & 1
    rows = lambda flag: jnp.concatenate(
        [jnp.where(flag == 0, own[k], other[k]) for k in part], axis=0
    )
    sent = multiply(after(rows(1 - mine), *events)).astype(BF16)
    return sent, multiply(after(rows(mine), sent)).astype(BF16)


def one_product(own, other, part, multiply, *events):
    mine = lax.axis_index("exp") & 1
    rows = [side[k] for side in (own, other) for k in part]
    whole = multiply(after(jnp.concatenate(rows, axis=0), *events)).astype(BF16)
    whole = whole.reshape(2, whole.shape[0] // 2, whole.shape[1])
    sent = lax.dynamic_index_in_dim(whole, 1 - mine, 0, False)
    return sent, lax.dynamic_index_in_dim(whole, mine, 0, False)


def over_cores(sent, kept):
    return (kept.astype(F32) + swap(sent, "exp", 1).astype(F32)).astype(BF16)


def sum_over_rest(part, bits):
    for bit in range(1, bits):
        part = (part.astype(F32) + swap(part, "exp", 1 << bit).astype(F32)).astype(BF16)
    return part


def on_device(
    queries, keys, values, out_grad, up_weight, down_weight, decay_rates, routes, gate_weights
):
    block_len, group = queries.shape
    heads = group // DH
    half = heads // 2
    experts = lax.axis_size("ctx") // 2
    bits = (lax.axis_size("exp") - 1).bit_length()
    capacity = block_len * 9 // (4 * experts)
    position = lax.axis_index("ctx").astype(jnp.int32)
    core = lax.axis_index("exp").astype(jnp.int32) & 1
    place = jnp.stack([position & 1, position >> 1, core])
    scalars = (place, -decay_rates)
    pair = jnp.concatenate([keys, values], axis=0)
    up_local, down_local = up_weight[0], down_weight[0]
    quarter = max(experts // 4, 1)
    near_part = range(experts // 2)
    first_far = range(experts - quarter, experts)
    second_far = range(experts // 2, experts - quarter)
    states = jax.ShapeDtypeStruct((half, DH, DH), BF16)
    weight_sq = jax.ShapeDtypeStruct((heads, block_len, block_len), BF16)
    wide = jax.ShapeDtypeStruct((block_len, group), F32)
    slim = jax.ShapeDtypeStruct((block_len, group), BF16)
    choose_table = jax.ShapeDtypeStruct((experts, capacity, block_len), F32)
    weigh_table = jax.ShapeDtypeStruct((experts, block_len, capacity), BF16)
    slots = jax.ShapeDtypeStruct((capacity, group), BF16)

    slots_of = jnp.concatenate([routes.astype(F32), gate_weights], axis=1).T
    reaches = [1 << i for i in range((experts - 1).bit_length())]
    pairs_of = lambda rows, k: swap(rows, "ctx", 2 * k) if k else rows

    key_mine, key_other = call(key_state_kernel, [states] * 2, scalars, (pair,))
    choose, weigh, *send_grad = call(
        route_kernel, [choose_table, weigh_table] + [slots] * experts,
        (place,), (slots_of, out_grad)
    )
    intra, weights = call(
        intra_kernel, [wide, weight_sq], scalars, (queries, pair), cost=LARGE
    )

    total, partner = scan_total(
        key_mine, key_other, decay_rates, place, block_len, False, send_grad[0]
    )
    by_down = lambda rows: dot(rows, down_local, 1, 1)
    by_up = lambda rows: dot(rows, up_local, 1, 0)
    grad_own = {0: send_grad[0]}
    grad_other = {0: swap(after(send_grad[0], total), "ctx", 1)}
    for k in near_part[1:]:
        grad_own[k] = pairs_of(after(send_grad[k], total), k)
    before = None
    for index, reach in enumerate(reaches):
        events = [intra] if index == 1 else []
        before, upto = scan_step(
            before, total, reach, decay_rates, place, block_len, False, *events
        )
    for k in near_part[1:]:
        grad_other[k] = swap(after(grad_own[k], upto), "ctx", 1)
    for k in first_far:
        grad_own[k] = pairs_of(after(send_grad[k], upto), k)
    keep, give = scan_ends(before, key_mine, partner, decay_rates, place, block_len, False)
    for k in second_far:
        grad_own[k] = pairs_of(after(send_grad[k], give), k)
    for k in first_far:
        grad_other[k] = swap(grad_own[k], "ctx", 1)
    given = swap(give, "ctx", 1)
    hidden_near = one_product(grad_own, grad_other, near_part, by_down, give)
    hidden_near_sum = over_cores(*hidden_near)
    hidden_near_all = sum_over_rest(hidden_near_sum, bits)
    send_in = call(
        attend_kernel, [slots] * experts, scalars, (queries, intra, choose, keep, given),
        [pltpu.VMEM((block_len, group), BF16)],
    )
    in_own, in_other = {0: send_in[0]}, {0: swap(send_in[0], "ctx", 1)}
    for k in [*near_part[1:], *first_far]:
        in_own[k] = pairs_of(send_in[k], k)
    for k in second_far:
        grad_other[k] = swap(after(grad_own[k], send_in[0]), "ctx", 1)
    for k in near_part[1:]:
        in_other[k] = swap(in_own[k], "ctx", 1)
    hidden_first = one_product(grad_own, grad_other, first_far, by_down, send_in[0])
    hidden_first_sum = over_cores(*hidden_first)
    hidden_first_all = sum_over_rest(hidden_first_sum, bits)
    for k in second_far:
        in_own[k] = pairs_of(after(send_in[k], *[in_own[k] for k in first_far], hidden_near_sum), k)
    for k in first_far:
        in_other[k] = swap(in_own[k], "ctx", 1)
    for k in second_far:
        in_other[k] = swap(in_own[k], "ctx", 1)
    pre_near = two_products(in_own, in_other, near_part, by_up, hidden_first_sum)
    pre_near_sum = over_cores(*pre_near)
    pre_near_all = sum_over_rest(pre_near_sum, bits)
    pre_first = two_products(in_own, in_other, first_far, by_up, pre_near[0])
    pre_first_sum = over_cores(*pre_first)
    pre_first_all = sum_over_rest(pre_first_sum, bits)
    hidden_second = one_product(grad_own, grad_other, second_far, by_down, pre_first_sum)
    hidden_second_sum = over_cores(*hidden_second)
    hidden_second_all = sum_over_rest(hidden_second_sum, bits)
    pre_second = two_products(in_own, in_other, second_far, by_up, pre_first_sum)
    pre_second_sum = over_cores(*pre_second)
    pre_second_all = sum_over_rest(pre_second_sum, bits)

    returned = []
    for pre, hidden in (
        (pre_near_all, hidden_near_all),
        (pre_first_all, hidden_first_all),
        (pre_second_all, hidden_second_all),
    ):
        slope = (hidden.astype(F32) * silu_slope(pre.astype(F32))).astype(BF16)
        got = swap(slope, "exp", 1)
        if returned:
            got = after(got, returned[-1][0])
        slope = jnp.concatenate(
            [jnp.where(core == 0, slope, got), jnp.where(core == 0, got, slope)], axis=0
        )
        back = dot(slope, up_local, 1, 1).astype(BF16)
        back = back.reshape(2, back.shape[0] // 2, group)
        returned.append((back, swap(back[1], "ctx", 1)))
    homes = {}
    for index, part in enumerate((near_part, first_far, second_far)):
        back, got = returned[index]
        if index == 1:
            got = after(got, returned[2][0])
        rows = (back[0].astype(F32) + got.astype(F32)).astype(BF16)
        for i, k in enumerate(part):
            homes[k] = pairs_of(rows[i * capacity : (i + 1) * capacity], k)
    homes = [homes[k] for k in range(experts)]

    grad_out, query_mine, query_other = call(
        grad_kernel, [slim, states, states], scalars, (queries, out_grad, weigh, *homes)
    )
    total, partner = scan_total(
        query_mine, query_other, decay_rates, place, block_len, True
    )
    before = None
    for reach in reaches:
        before, _ = scan_step(before, total, reach, decay_rates, place, block_len, True)
    keep_in = keep
    keep, give = scan_ends(before, query_mine, partner, decay_rates, place, block_len, True)
    leaving = (keep, swap(give, "ctx", 1))
    query_g, key_near, value_near = call(
        near_kernel, [slim, wide, wide], scalars,
        (queries, pair, grad_out, keep_in, given, weights)
    )
    key_g, value_g = call(
        far_kernel, [slim, slim], scalars,
        (pair, key_near, value_near) + leaving
    )
    return query_g, key_g, value_g


def solution(mesh):
    placed = (
        P("ctx", "exp"),
        P("ctx", "exp"),
        P("ctx", "exp"),
        P("ctx", "exp"),
        P("ctx", "exp", None),
        P("ctx", None, "exp"),
        P("exp"),
        P("ctx", None),
        P("ctx", None),
    )
    return jax.shard_map(
        on_device,
        mesh=mesh,
        in_specs=placed,
        out_specs=(P("ctx", "exp"), P("ctx", "exp"), P("ctx", "exp")),
        check_vma=False,
    )
```

```python
import functools

import jax
import jax.numpy as jnp
from jax import lax
from jax.experimental import pallas as pl
from jax.experimental.pallas import tpu as pltpu
from jax.sharding import PartitionSpec as P

DH = 128
F32 = jnp.float32
BF16 = jnp.bfloat16
SCALE = 1.0 / DH

SMEM = pl.BlockSpec(memory_space=pltpu.SMEM)
VMEM = pl.BlockSpec(memory_space=pltpu.VMEM)
LARGE = pl.CostEstimate(flops=1, bytes_accessed=40_000_000, transcendentals=0)
SMALL = pl.CostEstimate(flops=1, bytes_accessed=1, transcendentals=0)


def dot(left, right, left_dim, right_dim):
    return lax.dot_general(
        left, right, (((left_dim,), (right_dim,)), ((), ())), preferred_element_type=F32
    )


def silu_slope(value):
    sigma = jax.nn.sigmoid(value)
    return sigma * (1.0 + value * (1.0 - sigma))


def lanes_of(place_ref, slot, heads):
    head = lax.rem(place_ref[0] * (heads // 2) + slot, heads)
    return head, pl.ds(pl.multiple_of(head * DH, DH), DH)


def column(block_len):
    return lax.broadcasted_iota(jnp.int32, (block_len, 1), 0).astype(F32)


def decay_within(rate, block_len):
    rows = lax.broadcasted_iota(jnp.int32, (block_len, block_len), 0)
    cols = lax.broadcasted_iota(jnp.int32, (block_len, block_len), 1)
    distance = (rows - cols).astype(F32)
    return jnp.where(distance >= 0.0, jnp.exp(rate * jnp.maximum(distance, 0.0)), 0.0)


def key_state_kernel(place_ref, rates_ref, pair_ref, mine_ref, other_ref):
    block_len, half = pair_ref.shape[0] // 2, mine_ref.shape[0]
    steps = column(block_len)
    for slot in [*range(half, 2 * half), *range(half)]:
        head, lanes = lanes_of(place_ref, slot, 2 * half)
        power = jnp.exp(rates_ref[head] * (block_len - steps))
        scaled = (pair_ref[:block_len, lanes].astype(F32) * power).astype(BF16)
        state_ref = (mine_ref, other_ref)[slot // half]
        state_ref[slot % half] = dot(scaled, pair_ref[block_len:, lanes], 0, 0).astype(BF16)


def pick_rows(choose_ref, rows, send_refs):
    capacity = choose_ref.shape[1]
    if capacity % 8:
        for k, send_ref in enumerate(send_refs):
            send_ref[...] = dot(choose_ref[k], rows, 1, 0).astype(BF16)
        return
    table = choose_ref[...].reshape(len(send_refs) * capacity, rows.shape[0])
    picked = dot(table.astype(BF16), rows, 1, 0)
    for k, send_ref in enumerate(send_refs):
        send_ref[...] = picked[k * capacity : (k + 1) * capacity].astype(BF16)


def route_kernel(
    place_ref, slots_ref, grad_ref, choose_ref, weigh_ref, *send_refs
):
    experts, capacity, block_len = choose_ref.shape
    rows = lax.broadcasted_iota(jnp.int32, (block_len, block_len), 0)
    cols = lax.broadcasted_iota(jnp.int32, (block_len, block_len), 1)

    first, second = [slots_ref[i : i + 1, :].astype(jnp.int32) for i in range(2)]
    names = lax.broadcasted_iota(jnp.int32, (32, block_len), 0)
    hit_first = jnp.where(names == first, 1.0, 0.0)
    hit_second = jnp.where(names == second, 1.0, 0.0)
    earlier = jnp.where(rows < cols, 1.0, 0.0).astype(BF16)
    before = dot((hit_first + hit_second).astype(BF16), earlier, 1, 0)
    slot_first = jnp.sum(before * hit_first, axis=0, keepdims=True).astype(jnp.int32)
    slot_second = jnp.sum(before * hit_second, axis=0, keepdims=True).astype(jnp.int32)
    slots = lax.broadcasted_iota(jnp.int32, (capacity, block_len), 0)
    for k in range(experts):
        expert = place_ref[1] ^ k
        named = ((slots == slot_first) & (first == expert)) | (
            (slots == slot_second) & (second == expert)
        )
        choose_ref[k] = jnp.where(named, 1.0, 0.0)
    pick_rows(choose_ref, grad_ref[...], send_refs)

    columns = jnp.concatenate(
        [first.astype(F32), second.astype(F32), slot_first.astype(F32), slot_second.astype(F32)]
        + [slots_ref[2:3, :], slots_ref[3:4, :]] + [jnp.zeros((2, block_len), F32)],
        axis=0,
    ).T
    first, second, slot_first, slot_second = [
        columns[:, i : i + 1].astype(jnp.int32) for i in range(4)
    ]
    slots = lax.broadcasted_iota(jnp.int32, (block_len, capacity), 1)
    for k in range(experts):
        expert = place_ref[1] ^ k
        one = jnp.where((slots == slot_first) & (first == expert), columns[:, 4:5], 0.0)
        two = jnp.where((slots == slot_second) & (second == expert), columns[:, 5:6], 0.0)
        weigh_ref[k] = (one + two).astype(BF16)


def intra_kernel(place_ref, rates_ref, q_ref, pair_ref, intra_ref, weights_ref):
    block_len, heads = q_ref.shape[0], weights_ref.shape[0]
    for slot in range(heads):
        head, lanes = lanes_of(place_ref, slot, heads)
        within = decay_within(rates_ref[head], block_len)
        scores = dot(q_ref[:, lanes], pair_ref[:block_len, lanes], 1, 1)
        weights = (SCALE * scores * within).astype(BF16)
        weights_ref[slot] = weights
        intra_ref[:, lanes] = dot(weights, pair_ref[block_len:, lanes], 1, 0)


def attend_kernel(
    place_ref, rates_ref, q_ref, intra_ref, choose_ref, mine_ref, other_ref, *refs
):
    send_refs, attn_ref = refs[:-1], refs[-1]
    block_len, half = q_ref.shape[0], mine_ref.shape[0]
    steps = column(block_len)
    for slot in range(2 * half):
        head, lanes = lanes_of(place_ref, slot, 2 * half)
        entering = (mine_ref, other_ref)[slot // half][slot % half]
        power = SCALE * jnp.exp(rates_ref[head] * steps)
        inter = power * dot(q_ref[:, lanes], entering, 1, 0)
        attn_ref[:, lanes] = (intra_ref[:, lanes] + inter).astype(BF16)
    pick_rows(choose_ref, attn_ref[...], send_refs)


def grad_kernel(place_ref, rates_ref, q_ref, out_grad_ref, weigh_ref, *refs):
    experts = weigh_ref.shape[0]
    home_refs, (grad_ref, mine_ref, other_ref) = refs[:experts], refs[experts:]
    block_len, half = q_ref.shape[0], mine_ref.shape[0]
    steps = column(block_len)
    total = out_grad_ref[...].astype(F32)
    for k in range(experts):
        total = total + dot(weigh_ref[k], home_refs[k][...], 1, 0)
    grad_ref[...] = total.astype(BF16)
    for slot in [*range(half, 2 * half), *range(half)]:
        head, lanes = lanes_of(place_ref, slot, 2 * half)
        power = jnp.exp(rates_ref[head] * (steps + 1.0))
        scaled = (q_ref[:, lanes].astype(F32) * power).astype(BF16)
        state_ref = (mine_ref, other_ref)[slot // half]
        state_ref[slot % half] = dot(scaled, grad_ref[:, lanes], 0, 0).astype(BF16)


def near_kernel(
    place_ref, rates_ref, q_ref, pair_ref, grad_ref, mine_ref, other_ref, weights_ref,
    query_ref, key_ref, value_ref,
):
    block_len, half = q_ref.shape[0], mine_ref.shape[0]
    steps = column(block_len)
    for slot in range(2 * half):
        head, lanes = lanes_of(place_ref, slot, 2 * half)
        rate = rates_ref[head]
        grad = grad_ref[:, lanes]
        entering = (mine_ref, other_ref)[slot // half][slot % half]
        within = decay_within(rate, block_len)
        dweights = (SCALE * dot(grad, pair_ref[block_len:, lanes], 1, 1) * within).astype(BF16)
        query = dot(dweights, pair_ref[:block_len, lanes], 1, 0)
        query = query + SCALE * jnp.exp(rate * steps) * dot(grad, entering, 1, 1)
        query_ref[:, lanes] = query.astype(BF16)
        key_ref[:, lanes] = dot(dweights, q_ref[:, lanes], 0, 0)
        value_ref[:, lanes] = dot(weights_ref[slot], grad, 0, 0)


def far_kernel(
    place_ref, rates_ref, pair_ref, key_near, value_near, mine_ref, other_ref, key_ref, value_ref
):
    block_len, half = pair_ref.shape[0] // 2, mine_ref.shape[0]
    steps = column(block_len)
    for slot in range(2 * half):
        head, lanes = lanes_of(place_ref, slot, 2 * half)
        leaving = (mine_ref, other_ref)[slot // half][slot % half]
        power = SCALE * jnp.exp(rates_ref[head] * (block_len - 1.0 - steps))
        key_ref[:, lanes] = (
            key_near[:, lanes] + power * dot(pair_ref[block_len:, lanes], leaving, 1, 1)
        ).astype(BF16)
        value_ref[:, lanes] = (
            value_near[:, lanes] + power * dot(pair_ref[:block_len, lanes], leaving, 1, 0)
        ).astype(BF16)


def call(kernel, out_shapes, scalars, arrays, scratch=(), cost=SMALL):
    return pl.pallas_call(
        kernel,
        out_shape=list(out_shapes),
        in_specs=[SMEM] * len(scalars) + [VMEM] * len(arrays),
        out_specs=[VMEM] * len(out_shapes),
        scratch_shapes=list(scratch),
        compiler_params=pltpu.CompilerParams(vmem_limit_bytes=16 * 1024 * 1024),
        cost_estimate=cost,
    )(*scalars, *arrays)


def swap(array, axis, distance):
    size = lax.axis_size(axis)
    return lax.ppermute(array, axis, [(i, i ^ distance) for i in range(size)])


def trade(array, pairs, partner):
    return lax.ppermute(
        array, "ctx", [(2 * partner(i) + s, 2 * i + s) for i in range(pairs) for s in (0, 1)]
    )


def after(array, *events):
    return lax.optimization_barrier((array,) + events)[0]


def head_power(rates, place, half, tokens):
    mine = lax.dynamic_slice(rates, (place[0] * half,), (half,))[:, None, None]
    return jnp.exp(-mine * tokens)


def scan_total(mine, other, rates, place, block_len, reverse, *events):
    side = 1 - place[0] if reverse else place[0]
    whole = head_power(rates, place, mine.shape[0], block_len)
    partner = after(swap(other, "ctx", 1), *events)
    first = jnp.where(side == 0, mine, partner).astype(F32)
    second = jnp.where(side == 0, partner, mine).astype(F32)
    return (whole * first + second).astype(BF16), partner


def scan_step(before, total, reach, rates, place, block_len, reverse, *events):
    half = total.shape[0]
    pairs = lax.axis_size("ctx") // 2
    pair = pairs - 1 - place[1] if reverse else place[1]
    if before is None:
        upto = total
    else:
        whole = head_power(rates, place, half, 2.0 * block_len)
        upto = (whole * before + total.astype(F32)).astype(BF16)
    upto = after(upto, *events)
    lower, offset = (pair & reach) == 0, pair & (reach - 1)
    got = None
    for j in range(reach):

        def partner(i, j=j):
            i = pairs - 1 - i if reverse else i
            start = i - i % (2 * reach)
            first, second = start + reach - 1, start + reach + j
            i = {first: second, second: first}.get(i, i)
            return pairs - 1 - i if reverse else i

        one = trade(upto, pairs, partner)
        got = one if got is None else jnp.where(offset == j, one, got)
    scale = head_power(rates, place, half, 2.0 * block_len * offset.astype(F32))
    grown = scale * got.astype(F32)
    kept = 0.0 if before is None else before
    return jnp.where(lower, kept, kept + grown), upto


def scan_ends(before, mine, partner, rates, place, block_len, reverse):
    side = 1 - place[0] if reverse else place[0]
    whole = head_power(rates, place, mine.shape[0], block_len)
    first = jnp.where(side == 0, mine, partner).astype(F32)
    second_meets = whole * before + first
    keep = jnp.where(side == 0, before, second_meets).astype(BF16)
    give = jnp.where(side == 0, second_meets, before).astype(BF16)
    return keep, give


def two_products(own, other, part, multiply, *events):
    mine = lax.axis_index("exp") & 1
    rows = lambda flag: jnp.concatenate(
        [jnp.where(flag == 0, own[k], other[k]) for k in part], axis=0
    )
    sent = multiply(after(rows(1 - mine), *events)).astype(BF16)
    return sent, multiply(after(rows(mine), sent)).astype(BF16)


def one_product(own, other, part, multiply, *events):
    mine = lax.axis_index("exp") & 1
    rows = [side[k] for side in (own, other) for k in part]
    whole = multiply(after(jnp.concatenate(rows, axis=0), *events)).astype(BF16)
    whole = whole.reshape(2, whole.shape[0] // 2, whole.shape[1])
    sent = lax.dynamic_index_in_dim(whole, 1 - mine, 0, False)
    return sent, lax.dynamic_index_in_dim(whole, mine, 0, False)


def over_cores(sent, kept):
    return (kept.astype(F32) + swap(sent, "exp", 1).astype(F32)).astype(BF16)


def sum_over_rest(part, bits):
    for bit in range(1, bits):
        part = (part.astype(F32) + swap(part, "exp", 1 << bit).astype(F32)).astype(BF16)
    return part


def on_device(
    queries, keys, values, out_grad, up_weight, down_weight, decay_rates, routes, gate_weights
):
    block_len, group = queries.shape
    heads = group // DH
    half = heads // 2
    experts = lax.axis_size("ctx") // 2
    bits = (lax.axis_size("exp") - 1).bit_length()
    capacity = block_len * 9 // (4 * experts)
    position = lax.axis_index("ctx").astype(jnp.int32)
    core = lax.axis_index("exp").astype(jnp.int32) & 1
    place = jnp.stack([position & 1, position >> 1, core])
    scalars = (place, -decay_rates)
    pair = jnp.concatenate([keys, values], axis=0)
    up_local, down_local = up_weight[0], down_weight[0]
    quarter = max(experts // 4, 1)
    near_part = range(experts // 2)
    first_far = range(experts - quarter, experts)
    second_far = range(experts // 2, experts - quarter)
    states = jax.ShapeDtypeStruct((half, DH, DH), BF16)
    weight_sq = jax.ShapeDtypeStruct((heads, block_len, block_len), BF16)
    wide = jax.ShapeDtypeStruct((block_len, group), F32)
    slim = jax.ShapeDtypeStruct((block_len, group), BF16)
    choose_table = jax.ShapeDtypeStruct((experts, capacity, block_len), F32)
    weigh_table = jax.ShapeDtypeStruct((experts, block_len, capacity), BF16)
    slots = jax.ShapeDtypeStruct((capacity, group), BF16)

    slots_of = jnp.concatenate([routes.astype(F32), gate_weights], axis=1).T
    reaches = [1 << i for i in range((experts - 1).bit_length())]
    pairs_of = lambda rows, k: swap(rows, "ctx", 2 * k) if k else rows

    key_mine, key_other = call(key_state_kernel, [states] * 2, scalars, (pair,))
    choose, weigh, *send_grad = call(
        route_kernel, [choose_table, weigh_table] + [slots] * experts,
        (place,), (slots_of, out_grad)
    )
    intra, weights = call(
        intra_kernel, [wide, weight_sq], scalars, (queries, pair), cost=LARGE
    )

    total, partner = scan_total(
        key_mine, key_other, decay_rates, place, block_len, False, send_grad[0]
    )
    by_down = lambda rows: dot(rows, down_local, 1, 1)
    by_up = lambda rows: dot(rows, up_local, 1, 0)
    grad_own = {0: send_grad[0]}
    grad_other = {0: swap(after(send_grad[0], total), "ctx", 1)}
    for k in near_part[1:]:
        grad_own[k] = pairs_of(after(send_grad[k], total), k)
    for k in near_part[1:]:
        grad_other[k] = swap(grad_own[k], "ctx", 1)
    before = None
    for index, reach in enumerate(reaches):
        events = [intra] if index == 1 else []
        before, upto = scan_step(
            before, total, reach, decay_rates, place, block_len, False, *events
        )
    keep, give = scan_ends(before, key_mine, partner, decay_rates, place, block_len, False)
    for k in first_far:
        grad_own[k] = pairs_of(after(send_grad[k], give), k)
    for k in first_far:
        grad_other[k] = swap(grad_own[k], "ctx", 1)
    given = swap(give, "ctx", 1)
    hidden_near = one_product(grad_own, grad_other, near_part, by_down, give)
    hidden_near_sum = over_cores(*hidden_near)
    hidden_near_all = sum_over_rest(hidden_near_sum, bits)
    given, hidden_near_sum = lax.optimization_barrier((given, hidden_near_sum))
    hidden_near_all = sum_over_rest(hidden_near_sum, bits)
    send_in = call(
        attend_kernel, [slots] * experts, scalars, (queries, intra, choose, keep, given),
        [pltpu.VMEM((block_len, group), BF16)],
    )
    in_own, in_other = {0: send_in[0]}, {0: swap(send_in[0], "ctx", 1)}
    for k in [*near_part[1:], *first_far]:
        in_own[k] = pairs_of(send_in[k], k)
    for k in near_part[1:]:
        in_other[k] = swap(in_own[k], "ctx", 1)
    hidden_first = one_product(grad_own, grad_other, first_far, by_down, hidden_near_sum, *[in_own[k] for k in first_far])
    hidden_first_sum = over_cores(*hidden_first)
    hidden_first_all = sum_over_rest(hidden_first_sum, bits)
    for k in second_far:
        in_own[k] = pairs_of(after(send_in[k], *[in_own[k] for k in first_far]), k)
    for k in second_far:
        grad_own[k] = pairs_of(after(send_grad[k], *[in_own[k] for k in first_far]), k)
    for k in first_far:
        in_other[k] = swap(after(in_own[k], *[in_other[k] for k in near_part[1:]]), "ctx", 1)
    pre_near = two_products(in_own, in_other, near_part, by_up, hidden_first_sum, hidden_near_all)
    pre_near_sum = over_cores(*pre_near)
    pre_near_all = sum_over_rest(pre_near_sum, bits)
    for k in second_far:
        in_other[k] = swap(after(in_own[k], pre_near_sum), "ctx", 1)
    for k in second_far:
        grad_other[k] = swap(after(grad_own[k], pre_near_sum), "ctx", 1)
    pre_first = two_products(in_own, in_other, first_far, by_up, pre_near_sum, hidden_near_all)
    pre_first_sum = over_cores(*pre_first)
    pre_first_all = sum_over_rest(pre_first_sum, bits)
    hidden_second = one_product(grad_own, grad_other, second_far, by_down, pre_first_sum)
    hidden_second_sum = over_cores(*hidden_second)
    hidden_second_all = sum_over_rest(hidden_second_sum, bits)
    pre_second = two_products(in_own, in_other, second_far, by_up, hidden_second[0], pre_first_all)
    pre_second_sum = over_cores(*pre_second)
    pre_second_all = sum_over_rest(pre_second_sum, bits)

    returned = []
    for pre, hidden in (
        (pre_near_all, hidden_near_all),
        (pre_first_all, hidden_first_all),
        (pre_second_all, hidden_second_all),
    ):
        slope = (hidden.astype(F32) * silu_slope(pre.astype(F32))).astype(BF16)
        got = swap(slope, "exp", 1)
        if returned:
            got = after(got, returned[-1][2])
        slope = jnp.concatenate(
            [jnp.where(core == 0, slope, got), jnp.where(core == 0, got, slope)], axis=0
        )
        back = dot(slope, up_local, 1, 1).astype(BF16)
        sides = back.reshape(2, back.shape[0] // 2, group)
        returned.append((sides[0], swap(sides[1], "ctx", 1), back))
    homes = {}
    for index, part in enumerate((near_part, first_far, second_far)):
        kept, got, _ = returned[index]
        rows = (kept.astype(F32) + got.astype(F32)).astype(BF16)
        for i, k in enumerate(part):
            homes[k] = pairs_of(rows[i * capacity : (i + 1) * capacity], k)
    homes = [homes[k] for k in range(experts)]

    grad_out, query_mine, query_other = call(
        grad_kernel, [slim, states, states], scalars, (queries, out_grad, weigh, *homes)
    )
    total, partner = scan_total(
        query_mine, query_other, decay_rates, place, block_len, True
    )
    before = None
    for reach in reaches:
        before, _ = scan_step(before, total, reach, decay_rates, place, block_len, True)
    keep_in = keep
    keep, give = scan_ends(before, query_mine, partner, decay_rates, place, block_len, True)
    leaving = (keep, swap(give, "ctx", 1))
    query_g, key_near, value_near = call(
        near_kernel, [slim, wide, wide], scalars,
        (queries, pair, grad_out, keep_in, given, weights)
    )
    key_g, value_g = call(
        far_kernel, [slim, slim], scalars,
        (pair, key_near, value_near) + leaving
    )
    return query_g, key_g, value_g


def solution(mesh):
    placed = (
        P("ctx", "exp"),
        P("ctx", "exp"),
        P("ctx", "exp"),
        P("ctx", "exp"),
        P("ctx", "exp", None),
        P("ctx", None, "exp"),
        P("exp"),
        P("ctx", None),
        P("ctx", None),
    )
    return jax.shard_map(
        on_device,
        mesh=mesh,
        in_specs=placed,
        out_specs=(P("ctx", "exp"), P("ctx", "exp"), P("ctx", "exp")),
        check_vma=False,
    )
```

```python
import functools

import jax
import jax.numpy as jnp
from jax import lax
from jax.experimental import pallas as pl
from jax.experimental.pallas import tpu as pltpu
from jax.sharding import PartitionSpec as P

DH = 128
F32 = jnp.float32
BF16 = jnp.bfloat16
SCALE = 1.0 / DH

SMEM = pl.BlockSpec(memory_space=pltpu.SMEM)
VMEM = pl.BlockSpec(memory_space=pltpu.VMEM)
LARGE = pl.CostEstimate(flops=1, bytes_accessed=40_000_000, transcendentals=0)
SMALL = pl.CostEstimate(flops=1, bytes_accessed=1, transcendentals=0)


def dot(left, right, left_dim, right_dim):
    return lax.dot_general(
        left, right, (((left_dim,), (right_dim,)), ((), ())), preferred_element_type=F32
    )


def silu_slope(value):
    sigma = jax.nn.sigmoid(value)
    return sigma * (1.0 + value * (1.0 - sigma))


def lanes_of(place_ref, slot, heads):
    head = lax.rem(place_ref[0] * (heads // 2) + slot, heads)
    return head, pl.ds(pl.multiple_of(head * DH, DH), DH)


def column(block_len):
    return lax.broadcasted_iota(jnp.int32, (block_len, 1), 0).astype(F32)


def decay_within(rate, block_len):
    rows = lax.broadcasted_iota(jnp.int32, (block_len, block_len), 0)
    cols = lax.broadcasted_iota(jnp.int32, (block_len, block_len), 1)
    distance = (rows - cols).astype(F32)
    return jnp.where(distance >= 0.0, jnp.exp(rate * jnp.maximum(distance, 0.0)), 0.0)


def key_state_kernel(place_ref, rates_ref, pair_ref, mine_ref, other_ref):
    block_len, half = pair_ref.shape[0] // 2, mine_ref.shape[0]
    steps = column(block_len)
    for slot in [*range(half, 2 * half), *range(half)]:
        head, lanes = lanes_of(place_ref, slot, 2 * half)
        power = jnp.exp(rates_ref[head] * (block_len - steps))
        scaled = (pair_ref[:block_len, lanes].astype(F32) * power).astype(BF16)
        state_ref = (mine_ref, other_ref)[slot // half]
        state_ref[slot % half] = dot(scaled, pair_ref[block_len:, lanes], 0, 0).astype(BF16)


def pick_rows(choose_ref, rows, send_refs):
    capacity = choose_ref.shape[1]
    if capacity % 8:
        for k, send_ref in enumerate(send_refs):
            send_ref[...] = dot(choose_ref[k], rows, 1, 0).astype(BF16)
        return
    table = choose_ref[...].reshape(len(send_refs) * capacity, rows.shape[0])
    picked = dot(table.astype(BF16), rows, 1, 0)
    for k, send_ref in enumerate(send_refs):
        send_ref[...] = picked[k * capacity : (k + 1) * capacity].astype(BF16)


def route_kernel(
    place_ref, slots_ref, grad_ref, choose_ref, weigh_ref, *send_refs
):
    experts, capacity, block_len = choose_ref.shape
    rows = lax.broadcasted_iota(jnp.int32, (block_len, block_len), 0)
    cols = lax.broadcasted_iota(jnp.int32, (block_len, block_len), 1)

    first, second = [slots_ref[i : i + 1, :].astype(jnp.int32) for i in range(2)]
    names = lax.broadcasted_iota(jnp.int32, (32, block_len), 0)
    hit_first = jnp.where(names == first, 1.0, 0.0)
    hit_second = jnp.where(names == second, 1.0, 0.0)
    earlier = jnp.where(rows < cols, 1.0, 0.0).astype(BF16)
    before = dot((hit_first + hit_second).astype(BF16), earlier, 1, 0)
    slot_first = jnp.sum(before * hit_first, axis=0, keepdims=True).astype(jnp.int32)
    slot_second = jnp.sum(before * hit_second, axis=0, keepdims=True).astype(jnp.int32)
    slots = lax.broadcasted_iota(jnp.int32, (capacity, block_len), 0)
    for k in range(experts):
        expert = place_ref[1] ^ k
        named = ((slots == slot_first) & (first == expert)) | (
            (slots == slot_second) & (second == expert)
        )
        choose_ref[k] = jnp.where(named, 1.0, 0.0)
    pick_rows(choose_ref, grad_ref[...], send_refs)

    columns = jnp.concatenate(
        [first.astype(F32), second.astype(F32), slot_first.astype(F32), slot_second.astype(F32)]
        + [slots_ref[2:3, :], slots_ref[3:4, :]] + [jnp.zeros((2, block_len), F32)],
        axis=0,
    ).T
    first, second, slot_first, slot_second = [
        columns[:, i : i + 1].astype(jnp.int32) for i in range(4)
    ]
    slots = lax.broadcasted_iota(jnp.int32, (block_len, capacity), 1)
    for k in range(experts):
        expert = place_ref[1] ^ k
        one = jnp.where((slots == slot_first) & (first == expert), columns[:, 4:5], 0.0)
        two = jnp.where((slots == slot_second) & (second == expert), columns[:, 5:6], 0.0)
        weigh_ref[k] = (one + two).astype(BF16)


def intra_kernel(place_ref, rates_ref, q_ref, pair_ref, intra_ref, weights_ref):
    block_len, heads = q_ref.shape[0], weights_ref.shape[0]
    for slot in range(heads):
        head, lanes = lanes_of(place_ref, slot, heads)
        within = decay_within(rates_ref[head], block_len)
        scores = dot(q_ref[:, lanes], pair_ref[:block_len, lanes], 1, 1)
        weights = (SCALE * scores * within).astype(BF16)
        weights_ref[slot] = weights
        intra_ref[:, lanes] = dot(weights, pair_ref[block_len:, lanes], 1, 0)


def attend_kernel(
    place_ref, rates_ref, q_ref, intra_ref, choose_ref, mine_ref, other_ref, *refs
):
    send_refs, attn_ref = refs[:-1], refs[-1]
    block_len, half = q_ref.shape[0], mine_ref.shape[0]
    steps = column(block_len)
    for slot in range(2 * half):
        head, lanes = lanes_of(place_ref, slot, 2 * half)
        entering = (mine_ref, other_ref)[slot // half][slot % half]
        power = SCALE * jnp.exp(rates_ref[head] * steps)
        inter = power * dot(q_ref[:, lanes], entering, 1, 0)
        attn_ref[:, lanes] = (intra_ref[:, lanes] + inter).astype(BF16)
    pick_rows(choose_ref, attn_ref[...], send_refs)


def grad_kernel(place_ref, rates_ref, q_ref, out_grad_ref, weigh_ref, *refs):
    experts = weigh_ref.shape[0]
    home_refs, (grad_ref, mine_ref, other_ref) = refs[:experts], refs[experts:]
    block_len, half = q_ref.shape[0], mine_ref.shape[0]
    steps = column(block_len)
    total = out_grad_ref[...].astype(F32)
    for k in range(experts):
        total = total + dot(weigh_ref[k], home_refs[k][...], 1, 0)
    grad_ref[...] = total.astype(BF16)
    for slot in [*range(half, 2 * half), *range(half)]:
        head, lanes = lanes_of(place_ref, slot, 2 * half)
        power = jnp.exp(rates_ref[head] * (steps + 1.0))
        scaled = (q_ref[:, lanes].astype(F32) * power).astype(BF16)
        state_ref = (mine_ref, other_ref)[slot // half]
        state_ref[slot % half] = dot(scaled, grad_ref[:, lanes], 0, 0).astype(BF16)


def near_kernel(
    place_ref, rates_ref, q_ref, pair_ref, grad_ref, mine_ref, other_ref, weights_ref,
    query_ref, key_ref, value_ref,
):
    block_len, half = q_ref.shape[0], mine_ref.shape[0]
    steps = column(block_len)
    for slot in range(2 * half):
        head, lanes = lanes_of(place_ref, slot, 2 * half)
        rate = rates_ref[head]
        grad = grad_ref[:, lanes]
        entering = (mine_ref, other_ref)[slot // half][slot % half]
        within = decay_within(rate, block_len)
        dweights = (SCALE * dot(grad, pair_ref[block_len:, lanes], 1, 1) * within).astype(BF16)
        query = dot(dweights, pair_ref[:block_len, lanes], 1, 0)
        query = query + SCALE * jnp.exp(rate * steps) * dot(grad, entering, 1, 1)
        query_ref[:, lanes] = query.astype(BF16)
        key_ref[:, lanes] = dot(dweights, q_ref[:, lanes], 0, 0)
        value_ref[:, lanes] = dot(weights_ref[slot], grad, 0, 0)


def far_kernel(
    place_ref, rates_ref, pair_ref, key_near, value_near, mine_ref, other_ref, key_ref, value_ref
):
    block_len, half = pair_ref.shape[0] // 2, mine_ref.shape[0]
    steps = column(block_len)
    for slot in range(2 * half):
        head, lanes = lanes_of(place_ref, slot, 2 * half)
        leaving = (mine_ref, other_ref)[slot // half][slot % half]
        power = SCALE * jnp.exp(rates_ref[head] * (block_len - 1.0 - steps))
        key_ref[:, lanes] = (
            key_near[:, lanes] + power * dot(pair_ref[block_len:, lanes], leaving, 1, 1)
        ).astype(BF16)
        value_ref[:, lanes] = (
            value_near[:, lanes] + power * dot(pair_ref[:block_len, lanes], leaving, 1, 0)
        ).astype(BF16)


def call(kernel, out_shapes, scalars, arrays, scratch=(), cost=SMALL):
    return pl.pallas_call(
        kernel,
        out_shape=list(out_shapes),
        in_specs=[SMEM] * len(scalars) + [VMEM] * len(arrays),
        out_specs=[VMEM] * len(out_shapes),
        scratch_shapes=list(scratch),
        compiler_params=pltpu.CompilerParams(vmem_limit_bytes=16 * 1024 * 1024),
        cost_estimate=cost,
    )(*scalars, *arrays)


def swap(array, axis, distance):
    size = lax.axis_size(axis)
    return lax.ppermute(array, axis, [(i, i ^ distance) for i in range(size)])


def trade(array, pairs, partner):
    return lax.ppermute(
        array, "ctx", [(2 * partner(i) + s, 2 * i + s) for i in range(pairs) for s in (0, 1)]
    )


def after(array, *events):
    return lax.optimization_barrier((array,) + events)[0]


def head_power(rates, place, half, tokens):
    mine = lax.dynamic_slice(rates, (place[0] * half,), (half,))[:, None, None]
    return jnp.exp(-mine * tokens)


def scan_total(mine, other, rates, place, block_len, reverse, *events):
    side = 1 - place[0] if reverse else place[0]
    whole = head_power(rates, place, mine.shape[0], block_len)
    partner = after(swap(other, "ctx", 1), *events)
    first = jnp.where(side == 0, mine, partner).astype(F32)
    second = jnp.where(side == 0, partner, mine).astype(F32)
    return (whole * first + second).astype(BF16), partner


def scan_step(before, total, reach, rates, place, block_len, reverse, *events):
    half = total.shape[0]
    pairs = lax.axis_size("ctx") // 2
    pair = pairs - 1 - place[1] if reverse else place[1]
    if before is None:
        upto = total
    else:
        whole = head_power(rates, place, half, 2.0 * block_len)
        upto = (whole * before + total.astype(F32)).astype(BF16)
    upto = after(upto, *events)
    lower, offset = (pair & reach) == 0, pair & (reach - 1)
    got = None
    for j in range(reach):

        def partner(i, j=j):
            i = pairs - 1 - i if reverse else i
            start = i - i % (2 * reach)
            first, second = start + reach - 1, start + reach + j
            i = {first: second, second: first}.get(i, i)
            return pairs - 1 - i if reverse else i

        one = trade(upto, pairs, partner)
        got = one if got is None else jnp.where(offset == j, one, got)
    scale = head_power(rates, place, half, 2.0 * block_len * offset.astype(F32))
    grown = scale * got.astype(F32)
    kept = 0.0 if before is None else before
    return jnp.where(lower, kept, kept + grown), upto


def scan_ends(before, mine, partner, rates, place, block_len, reverse):
    side = 1 - place[0] if reverse else place[0]
    whole = head_power(rates, place, mine.shape[0], block_len)
    first = jnp.where(side == 0, mine, partner).astype(F32)
    second_meets = whole * before + first
    keep = jnp.where(side == 0, before, second_meets).astype(BF16)
    give = jnp.where(side == 0, second_meets, before).astype(BF16)
    return keep, give


def two_products(own, other, part, multiply, *events):
    mine = lax.axis_index("exp") & 1
    rows = lambda flag: jnp.concatenate(
        [jnp.where(flag == 0, own[k], other[k]) for k in part], axis=0
    )
    sent = multiply(after(rows(1 - mine), *events)).astype(BF16)
    return sent, multiply(after(rows(mine), sent)).astype(BF16)


def over_cores(sent, kept):
    return (kept.astype(F32) + swap(sent, "exp", 1).astype(F32)).astype(BF16)


def sum_over_rest(part, bits):
    for bit in range(1, bits):
        part = (part.astype(F32) + swap(part, "exp", 1 << bit).astype(F32)).astype(BF16)
    return part


def on_device(
    queries, keys, values, out_grad, up_weight, down_weight, decay_rates, routes, gate_weights
):
    block_len, group = queries.shape
    heads = group // DH
    half = heads // 2
    experts = lax.axis_size("ctx") // 2
    bits = (lax.axis_size("exp") - 1).bit_length()
    capacity = block_len * 9 // (4 * experts)
    position = lax.axis_index("ctx").astype(jnp.int32)
    core = lax.axis_index("exp").astype(jnp.int32) & 1
    place = jnp.stack([position & 1, position >> 1, core])
    scalars = (place, -decay_rates)
    pair = jnp.concatenate([keys, values], axis=0)
    up_local, down_local = up_weight[0], down_weight[0]
    quarter = max(experts // 4, 1)
    near_part = range(experts // 2)
    first_far = range(experts - quarter, experts)
    second_far = range(experts // 2, experts - quarter)
    states = jax.ShapeDtypeStruct((half, DH, DH), BF16)
    weight_sq = jax.ShapeDtypeStruct((heads, block_len, block_len), BF16)
    wide = jax.ShapeDtypeStruct((block_len, group), F32)
    slim = jax.ShapeDtypeStruct((block_len, group), BF16)
    choose_table = jax.ShapeDtypeStruct((experts, capacity, block_len), F32)
    weigh_table = jax.ShapeDtypeStruct((experts, block_len, capacity), BF16)
    slots = jax.ShapeDtypeStruct((capacity, group), BF16)

    slots_of = jnp.concatenate([routes.astype(F32), gate_weights], axis=1).T
    reaches = [1 << i for i in range((experts - 1).bit_length())]
    pairs_of = lambda rows, k: swap(rows, "ctx", 2 * k) if k else rows

    key_mine, key_other = call(key_state_kernel, [states] * 2, scalars, (pair,))
    choose, weigh, *send_grad = call(
        route_kernel, [choose_table, weigh_table] + [slots] * experts,
        (place,), (slots_of, out_grad)
    )
    intra, weights = call(
        intra_kernel, [wide, weight_sq], scalars, (queries, pair), cost=LARGE
    )

    total, partner = scan_total(
        key_mine, key_other, decay_rates, place, block_len, False, send_grad[0]
    )
    by_down = lambda rows: dot(rows, down_local, 1, 1)
    by_up = lambda rows: dot(rows, up_local, 1, 0)
    grad_own = {0: send_grad[0]}
    grad_other = {0: swap(after(send_grad[0], total), "ctx", 1)}
    for k in near_part[1:]:
        grad_own[k] = pairs_of(after(send_grad[k], total), k)
    for k in first_far:
        grad_own[k] = pairs_of(after(send_grad[k], total), k)
    before = None
    for index, reach in enumerate(reaches):
        events = [intra] if index == 1 else []
        before, upto = scan_step(
            before, total, reach, decay_rates, place, block_len, False, *events
        )
    for k in near_part[1:]:
        grad_other[k] = swap(after(grad_own[k], upto), "ctx", 1)
    for k in first_far:
        grad_other[k] = swap(after(grad_own[k], upto), "ctx", 1)
    keep, give = scan_ends(before, key_mine, partner, decay_rates, place, block_len, False)
    for k in second_far:
        grad_own[k] = pairs_of(after(send_grad[k], give), k)
    given = swap(give, "ctx", 1)
    hidden_near = two_products(grad_own, grad_other, near_part, by_down, give)
    hidden_near_sum = over_cores(*hidden_near)
    hidden_near_all = sum_over_rest(hidden_near_sum, bits)
    given, hidden_near_sum = lax.optimization_barrier((given, hidden_near_sum))
    hidden_near_all = sum_over_rest(hidden_near_sum, bits)
    send_in = call(
        attend_kernel, [slots] * experts, scalars, (queries, intra, choose, keep, given),
        [pltpu.VMEM((block_len, group), BF16)],
    )
    in_own, in_other = {0: send_in[0]}, {0: swap(send_in[0], "ctx", 1)}
    for k in [*near_part[1:], *first_far]:
        in_own[k] = pairs_of(send_in[k], k)
    for k in near_part[1:]:
        in_other[k] = swap(in_own[k], "ctx", 1)
    hidden_first = two_products(grad_own, grad_other, first_far, by_down, send_in[0])
    hidden_first_sum = over_cores(*hidden_first)
    hidden_first_all = sum_over_rest(hidden_first_sum, bits)
    for k in second_far:
        in_own[k] = pairs_of(after(send_in[k], *[in_own[k] for k in first_far], hidden_first_sum), k)
    for k in first_far:
        in_other[k] = swap(in_own[k], "ctx", 1)
    pre_near = two_products(in_own, in_other, near_part, by_up, hidden_first_sum)
    pre_near_sum = over_cores(*pre_near)
    pre_near_all = sum_over_rest(pre_near_sum, bits)
    for k in second_far:
        in_other[k] = swap(after(in_own[k], pre_near_sum), "ctx", 1)
    for k in second_far:
        grad_other[k] = swap(after(grad_own[k], pre_near_sum), "ctx", 1)
    pre_first = two_products(in_own, in_other, first_far, by_up, pre_near_sum)
    pre_first_sum = over_cores(*pre_first)
    pre_first_all = sum_over_rest(pre_first_sum, bits)
    hidden_second = two_products(grad_own, grad_other, second_far, by_down, pre_first_sum)
    hidden_second_sum = over_cores(*hidden_second)
    hidden_second_all = sum_over_rest(hidden_second_sum, bits)
    pre_second = two_products(in_own, in_other, second_far, by_up, hidden_second_sum)
    pre_second_sum = over_cores(*pre_second)
    pre_second_all = sum_over_rest(pre_second_sum, bits)

    returned = []
    for pre, hidden in (
        (pre_near_all, hidden_near_all),
        (pre_first_all, hidden_first_all),
        (pre_second_all, hidden_second_all),
    ):
        slope = (hidden.astype(F32) * silu_slope(pre.astype(F32))).astype(BF16)
        got = swap(slope, "exp", 1)
        if returned:
            got = after(got, returned[-1][2])
        slope = jnp.concatenate(
            [jnp.where(core == 0, slope, got), jnp.where(core == 0, got, slope)], axis=0
        )
        back = dot(slope, up_local, 1, 1).astype(BF16)
        sides = back.reshape(2, back.shape[0] // 2, group)
        returned.append((sides[0], swap(sides[1], "ctx", 1), back))
    homes = {}
    for index, part in enumerate((near_part, first_far, second_far)):
        kept, got, _ = returned[index]
        rows = (kept.astype(F32) + got.astype(F32)).astype(BF16)
        for i, k in enumerate(part):
            homes[k] = pairs_of(rows[i * capacity : (i + 1) * capacity], k)
    homes = [homes[k] for k in range(experts)]

    grad_out, query_mine, query_other = call(
        grad_kernel, [slim, states, states], scalars, (queries, out_grad, weigh, *homes)
    )
    total, partner = scan_total(
        query_mine, query_other, decay_rates, place, block_len, True
    )
    before = None
    for reach in reaches:
        before, _ = scan_step(before, total, reach, decay_rates, place, block_len, True)
    keep_in = keep
    keep, give = scan_ends(before, query_mine, partner, decay_rates, place, block_len, True)
    leaving = (keep, swap(give, "ctx", 1))
    query_g, key_near, value_near = call(
        near_kernel, [slim, wide, wide], scalars,
        (queries, pair, grad_out, keep_in, given, weights)
    )
    key_g, value_g = call(
        far_kernel, [slim, slim], scalars,
        (pair, key_near, value_near) + leaving
    )
    return query_g, key_g, value_g


def solution(mesh):
    placed = (
        P("ctx", "exp"),
        P("ctx", "exp"),
        P("ctx", "exp"),
        P("ctx", "exp"),
        P("ctx", "exp", None),
        P("ctx", None, "exp"),
        P("exp"),
        P("ctx", None),
        P("ctx", None),
    )
    return jax.shard_map(
        on_device,
        mesh=mesh,
        in_specs=placed,
        out_specs=(P("ctx", "exp"), P("ctx", "exp"), P("ctx", "exp")),
        check_vma=False,
    )
```

```python
import functools

import jax
import jax.numpy as jnp
from jax import lax
from jax.experimental import pallas as pl
from jax.experimental.pallas import tpu as pltpu
from jax.sharding import PartitionSpec as P

DH = 128
F32 = jnp.float32
BF16 = jnp.bfloat16
SCALE = 1.0 / DH

SMEM = pl.BlockSpec(memory_space=pltpu.SMEM)
VMEM = pl.BlockSpec(memory_space=pltpu.VMEM)
LARGE = pl.CostEstimate(flops=1, bytes_accessed=40_000_000, transcendentals=0)
SMALL = pl.CostEstimate(flops=1, bytes_accessed=1, transcendentals=0)


def dot(left, right, left_dim, right_dim):
    return lax.dot_general(
        left, right, (((left_dim,), (right_dim,)), ((), ())), preferred_element_type=F32
    )


def silu_slope(value):
    sigma = jax.nn.sigmoid(value)
    return sigma * (1.0 + value * (1.0 - sigma))


def lanes_of(place_ref, slot, heads):
    head = lax.rem(place_ref[0] * (heads // 2) + slot, heads)
    return head, pl.ds(pl.multiple_of(head * DH, DH), DH)


def column(block_len):
    return lax.broadcasted_iota(jnp.int32, (block_len, 1), 0).astype(F32)


def decay_within(rate, block_len):
    rows = lax.broadcasted_iota(jnp.int32, (block_len, block_len), 0)
    cols = lax.broadcasted_iota(jnp.int32, (block_len, block_len), 1)
    distance = (rows - cols).astype(F32)
    return jnp.where(distance >= 0.0, jnp.exp(rate * jnp.maximum(distance, 0.0)), 0.0)


def key_state_kernel(place_ref, rates_ref, pair_ref, mine_ref, other_ref):
    block_len, half = pair_ref.shape[0] // 2, mine_ref.shape[0]
    steps = column(block_len)
    for slot in [*range(half, 2 * half), *range(half)]:
        head, lanes = lanes_of(place_ref, slot, 2 * half)
        power = jnp.exp(rates_ref[head] * (block_len - steps))
        scaled = (pair_ref[:block_len, lanes].astype(F32) * power).astype(BF16)
        state_ref = (mine_ref, other_ref)[slot // half]
        state_ref[slot % half] = dot(scaled, pair_ref[block_len:, lanes], 0, 0).astype(BF16)


def pick_rows(choose_ref, rows, send_refs):
    capacity = choose_ref.shape[1]
    if capacity % 8:
        for k, send_ref in enumerate(send_refs):
            send_ref[...] = dot(choose_ref[k], rows, 1, 0).astype(BF16)
        return
    table = choose_ref[...].reshape(len(send_refs) * capacity, rows.shape[0])
    picked = dot(table.astype(BF16), rows, 1, 0)
    for k, send_ref in enumerate(send_refs):
        send_ref[...] = picked[k * capacity : (k + 1) * capacity].astype(BF16)


def route_kernel(
    place_ref, slots_ref, grad_ref, choose_ref, weigh_ref, *send_refs
):
    experts, capacity, block_len = choose_ref.shape
    rows = lax.broadcasted_iota(jnp.int32, (block_len, block_len), 0)
    cols = lax.broadcasted_iota(jnp.int32, (block_len, block_len), 1)

    first, second = [slots_ref[i : i + 1, :].astype(jnp.int32) for i in range(2)]
    names = lax.broadcasted_iota(jnp.int32, (32, block_len), 0)
    hit_first = jnp.where(names == first, 1.0, 0.0)
    hit_second = jnp.where(names == second, 1.0, 0.0)
    earlier = jnp.where(rows < cols, 1.0, 0.0).astype(BF16)
    before = dot((hit_first + hit_second).astype(BF16), earlier, 1, 0)
    slot_first = jnp.sum(before * hit_first, axis=0, keepdims=True).astype(jnp.int32)
    slot_second = jnp.sum(before * hit_second, axis=0, keepdims=True).astype(jnp.int32)
    slots = lax.broadcasted_iota(jnp.int32, (capacity, block_len), 0)
    for k in range(experts):
        expert = place_ref[1] ^ k
        named = ((slots == slot_first) & (first == expert)) | (
            (slots == slot_second) & (second == expert)
        )
        choose_ref[k] = jnp.where(named, 1.0, 0.0)
    pick_rows(choose_ref, grad_ref[...], send_refs)

    columns = jnp.concatenate(
        [first.astype(F32), second.astype(F32), slot_first.astype(F32), slot_second.astype(F32)]
        + [slots_ref[2:3, :], slots_ref[3:4, :]] + [jnp.zeros((2, block_len), F32)],
        axis=0,
    ).T
    first, second, slot_first, slot_second = [
        columns[:, i : i + 1].astype(jnp.int32) for i in range(4)
    ]
    slots = lax.broadcasted_iota(jnp.int32, (block_len, capacity), 1)
    for k in range(experts):
        expert = place_ref[1] ^ k
        one = jnp.where((slots == slot_first) & (first == expert), columns[:, 4:5], 0.0)
        two = jnp.where((slots == slot_second) & (second == expert), columns[:, 5:6], 0.0)
        weigh_ref[k] = (one + two).astype(BF16)


def intra_kernel(place_ref, rates_ref, q_ref, pair_ref, intra_ref, weights_ref):
    block_len, heads = q_ref.shape[0], weights_ref.shape[0]
    for slot in range(heads):
        head, lanes = lanes_of(place_ref, slot, heads)
        within = decay_within(rates_ref[head], block_len)
        scores = dot(q_ref[:, lanes], pair_ref[:block_len, lanes], 1, 1)
        weights = (SCALE * scores * within).astype(BF16)
        weights_ref[slot] = weights
        intra_ref[:, lanes] = dot(weights, pair_ref[block_len:, lanes], 1, 0)


def attend_kernel(
    place_ref, rates_ref, q_ref, intra_ref, choose_ref, mine_ref, other_ref, *refs
):
    send_refs, attn_ref = refs[:-1], refs[-1]
    block_len, half = q_ref.shape[0], mine_ref.shape[0]
    steps = column(block_len)
    for slot in range(2 * half):
        head, lanes = lanes_of(place_ref, slot, 2 * half)
        entering = (mine_ref, other_ref)[slot // half][slot % half]
        power = SCALE * jnp.exp(rates_ref[head] * steps)
        inter = power * dot(q_ref[:, lanes], entering, 1, 0)
        attn_ref[:, lanes] = (intra_ref[:, lanes] + inter).astype(BF16)
    pick_rows(choose_ref, attn_ref[...], send_refs)


def grad_kernel(place_ref, rates_ref, q_ref, out_grad_ref, weigh_ref, *refs):
    experts = weigh_ref.shape[0]
    home_refs, (grad_ref, mine_ref, other_ref) = refs[:experts], refs[experts:]
    block_len, half = q_ref.shape[0], mine_ref.shape[0]
    steps = column(block_len)
    total = out_grad_ref[...].astype(F32)
    for k in range(experts):
        total = total + dot(weigh_ref[k], home_refs[k][...], 1, 0)
    grad_ref[...] = total.astype(BF16)
    for slot in [*range(half, 2 * half), *range(half)]:
        head, lanes = lanes_of(place_ref, slot, 2 * half)
        power = jnp.exp(rates_ref[head] * (steps + 1.0))
        scaled = (q_ref[:, lanes].astype(F32) * power).astype(BF16)
        state_ref = (mine_ref, other_ref)[slot // half]
        state_ref[slot % half] = dot(scaled, grad_ref[:, lanes], 0, 0).astype(BF16)


def near_kernel(
    place_ref, rates_ref, q_ref, pair_ref, grad_ref, mine_ref, other_ref, weights_ref,
    query_ref, key_ref, value_ref,
):
    block_len, half = q_ref.shape[0], mine_ref.shape[0]
    steps = column(block_len)
    for slot in range(2 * half):
        head, lanes = lanes_of(place_ref, slot, 2 * half)
        rate = rates_ref[head]
        grad = grad_ref[:, lanes]
        entering = (mine_ref, other_ref)[slot // half][slot % half]
        within = decay_within(rate, block_len)
        dweights = (SCALE * dot(grad, pair_ref[block_len:, lanes], 1, 1) * within).astype(BF16)
        query = dot(dweights, pair_ref[:block_len, lanes], 1, 0)
        query = query + SCALE * jnp.exp(rate * steps) * dot(grad, entering, 1, 1)
        query_ref[:, lanes] = query.astype(BF16)
        key_ref[:, lanes] = dot(dweights, q_ref[:, lanes], 0, 0)
        value_ref[:, lanes] = dot(weights_ref[slot], grad, 0, 0)


def far_kernel(
    place_ref, rates_ref, pair_ref, key_near, value_near, mine_ref, other_ref, key_ref, value_ref
):
    block_len, half = pair_ref.shape[0] // 2, mine_ref.shape[0]
    steps = column(block_len)
    for slot in range(2 * half):
        head, lanes = lanes_of(place_ref, slot, 2 * half)
        leaving = (mine_ref, other_ref)[slot // half][slot % half]
        power = SCALE * jnp.exp(rates_ref[head] * (block_len - 1.0 - steps))
        key_ref[:, lanes] = (
            key_near[:, lanes] + power * dot(pair_ref[block_len:, lanes], leaving, 1, 1)
        ).astype(BF16)
        value_ref[:, lanes] = (
            value_near[:, lanes] + power * dot(pair_ref[:block_len, lanes], leaving, 1, 0)
        ).astype(BF16)


def call(kernel, out_shapes, scalars, arrays, scratch=(), cost=SMALL):
    return pl.pallas_call(
        kernel,
        out_shape=list(out_shapes),
        in_specs=[SMEM] * len(scalars) + [VMEM] * len(arrays),
        out_specs=[VMEM] * len(out_shapes),
        scratch_shapes=list(scratch),
        compiler_params=pltpu.CompilerParams(vmem_limit_bytes=16 * 1024 * 1024),
        cost_estimate=cost,
    )(*scalars, *arrays)


def swap(array, axis, distance):
    size = lax.axis_size(axis)
    return lax.ppermute(array, axis, [(i, i ^ distance) for i in range(size)])


def trade(array, pairs, partner):
    return lax.ppermute(
        array, "ctx", [(2 * partner(i) + s, 2 * i + s) for i in range(pairs) for s in (0, 1)]
    )


def after(array, *events):
    return lax.optimization_barrier((array,) + events)[0]


def head_power(rates, place, half, tokens):
    mine = lax.dynamic_slice(rates, (place[0] * half,), (half,))[:, None, None]
    return jnp.exp(-mine * tokens)


def scan_total(mine, other, rates, place, block_len, reverse, *events):
    side = 1 - place[0] if reverse else place[0]
    whole = head_power(rates, place, mine.shape[0], block_len)
    partner = after(swap(other, "ctx", 1), *events)
    first = jnp.where(side == 0, mine, partner).astype(F32)
    second = jnp.where(side == 0, partner, mine).astype(F32)
    return (whole * first + second).astype(BF16), partner


def scan_step(before, total, reach, rates, place, block_len, reverse, *events):
    half = total.shape[0]
    pairs = lax.axis_size("ctx") // 2
    pair = pairs - 1 - place[1] if reverse else place[1]
    if before is None:
        upto = total
    else:
        whole = head_power(rates, place, half, 2.0 * block_len)
        upto = (whole * before + total.astype(F32)).astype(BF16)
    upto = after(upto, *events)
    lower, offset = (pair & reach) == 0, pair & (reach - 1)
    got = None
    for j in range(reach):

        def partner(i, j=j):
            i = pairs - 1 - i if reverse else i
            start = i - i % (2 * reach)
            first, second = start + reach - 1, start + reach + j
            i = {first: second, second: first}.get(i, i)
            return pairs - 1 - i if reverse else i

        one = trade(upto, pairs, partner)
        got = one if got is None else jnp.where(offset == j, one, got)
    scale = head_power(rates, place, half, 2.0 * block_len * offset.astype(F32))
    grown = scale * got.astype(F32)
    kept = 0.0 if before is None else before
    return jnp.where(lower, kept, kept + grown), upto


def scan_ends(before, mine, partner, rates, place, block_len, reverse):
    side = 1 - place[0] if reverse else place[0]
    whole = head_power(rates, place, mine.shape[0], block_len)
    first = jnp.where(side == 0, mine, partner).astype(F32)
    second_meets = whole * before + first
    keep = jnp.where(side == 0, before, second_meets).astype(BF16)
    give = jnp.where(side == 0, second_meets, before).astype(BF16)
    return keep, give


def two_products(own, other, part, multiply, *events):
    mine = lax.axis_index("exp") & 1
    rows = lambda flag: jnp.concatenate(
        [jnp.where(flag == 0, own[k], other[k]) for k in part], axis=0
    )
    sent = multiply(after(rows(1 - mine), *events)).astype(BF16)
    return sent, multiply(after(rows(mine), sent)).astype(BF16)


def over_cores(sent, kept):
    return (kept.astype(F32) + swap(sent, "exp", 1).astype(F32)).astype(BF16)


def sum_over_rest(part, bits):
    for bit in range(1, bits):
        part = (part.astype(F32) + swap(part, "exp", 1 << bit).astype(F32)).astype(BF16)
    return part


def on_device(
    queries, keys, values, out_grad, up_weight, down_weight, decay_rates, routes, gate_weights
):
    block_len, group = queries.shape
    heads = group // DH
    half = heads // 2
    experts = lax.axis_size("ctx") // 2
    bits = (lax.axis_size("exp") - 1).bit_length()
    capacity = block_len * 9 // (4 * experts)
    position = lax.axis_index("ctx").astype(jnp.int32)
    core = lax.axis_index("exp").astype(jnp.int32) & 1
    place = jnp.stack([position & 1, position >> 1, core])
    scalars = (place, -decay_rates)
    pair = jnp.concatenate([keys, values], axis=0)
    up_local, down_local = up_weight[0], down_weight[0]
    quarter = max(experts // 4, 1)
    near_part = range(experts // 2)
    first_far = range(experts - quarter, experts)
    second_far = range(experts // 2, experts - quarter)
    states = jax.ShapeDtypeStruct((half, DH, DH), BF16)
    weight_sq = jax.ShapeDtypeStruct((heads, block_len, block_len), BF16)
    wide = jax.ShapeDtypeStruct((block_len, group), F32)
    slim = jax.ShapeDtypeStruct((block_len, group), BF16)
    choose_table = jax.ShapeDtypeStruct((experts, capacity, block_len), F32)
    weigh_table = jax.ShapeDtypeStruct((experts, block_len, capacity), BF16)
    slots = jax.ShapeDtypeStruct((capacity, group), BF16)

    slots_of = jnp.concatenate([routes.astype(F32), gate_weights], axis=1).T
    reaches = [1 << i for i in range((experts - 1).bit_length())]
    pairs_of = lambda rows, k: swap(rows, "ctx", 2 * k) if k else rows

    key_mine, key_other = call(key_state_kernel, [states] * 2, scalars, (pair,))
    choose, weigh, *send_grad = call(
        route_kernel, [choose_table, weigh_table] + [slots] * experts,
        (place,), (slots_of, out_grad)
    )
    intra, weights = call(
        intra_kernel, [wide, weight_sq], scalars, (queries, pair), cost=LARGE
    )

    total, partner = scan_total(
        key_mine, key_other, decay_rates, place, block_len, False, send_grad[0]
    )
    by_down = lambda rows: dot(rows, down_local, 1, 1)
    by_up = lambda rows: dot(rows, up_local, 1, 0)
    grad_own = {0: send_grad[0]}
    grad_other = {0: swap(after(send_grad[0], total), "ctx", 1)}
    for k in near_part[1:]:
        grad_own[k] = pairs_of(after(send_grad[k], total), k)
    for k in first_far:
        grad_own[k] = pairs_of(after(send_grad[k], total), k)
    before = None
    for index, reach in enumerate(reaches):
        events = [intra] if index == 1 else []
        before, upto = scan_step(
            before, total, reach, decay_rates, place, block_len, False, *events
        )
    for k in near_part[1:]:
        grad_other[k] = swap(after(grad_own[k], upto), "ctx", 1)
    for k in first_far:
        grad_other[k] = swap(after(grad_own[k], upto), "ctx", 1)
    keep, give = scan_ends(before, key_mine, partner, decay_rates, place, block_len, False)
    for k in second_far:
        grad_own[k] = pairs_of(after(send_grad[k], give), k)
    given = swap(give, "ctx", 1)
    hidden_near = two_products(grad_own, grad_other, near_part, by_down, give)
    hidden_near_sum = over_cores(*hidden_near)
    hidden_near_all = sum_over_rest(hidden_near_sum, bits)
    given, hidden_near_sum = lax.optimization_barrier((given, hidden_near_sum))
    hidden_near_all = sum_over_rest(hidden_near_sum, bits)
    send_in = call(
        attend_kernel, [slots] * experts, scalars, (queries, intra, choose, keep, given),
        [pltpu.VMEM((block_len, group), BF16)],
    )
    in_own, in_other = {0: send_in[0]}, {0: swap(send_in[0], "ctx", 1)}
    for k in [*near_part[1:], *first_far]:
        in_own[k] = pairs_of(send_in[k], k)
    for k in near_part[1:]:
        in_other[k] = swap(in_own[k], "ctx", 1)
    hidden_first = two_products(grad_own, grad_other, first_far, by_down, send_in[0])
    hidden_first_sum = over_cores(*hidden_first)
    hidden_first_all = sum_over_rest(hidden_first_sum, bits)
    for k in second_far:
        in_own[k] = pairs_of(after(send_in[k], *[in_own[k] for k in first_far], hidden_first_sum), k)
    for k in first_far:
        in_other[k] = swap(after(in_own[k], *[in_other[k] for k in near_part[1:]]), "ctx", 1)
    pre_near = two_products(in_own, in_other, near_part, by_up, hidden_first_sum)
    pre_near_sum = over_cores(*pre_near)
    pre_near_all = sum_over_rest(pre_near_sum, bits)
    for k in second_far:
        in_other[k] = swap(after(in_own[k], pre_near_sum), "ctx", 1)
    for k in second_far:
        grad_other[k] = swap(after(grad_own[k], pre_near_sum), "ctx", 1)
    pre_first = two_products(in_own, in_other, first_far, by_up, pre_near_sum)
    pre_first_sum = over_cores(*pre_first)
    pre_first_all = sum_over_rest(pre_first_sum, bits)
    hidden_second = two_products(grad_own, grad_other, second_far, by_down, pre_first_sum)
    hidden_second_sum = over_cores(*hidden_second)
    hidden_second_all = sum_over_rest(hidden_second_sum, bits)
    pre_second = two_products(in_own, in_other, second_far, by_up, hidden_second_sum)
    pre_second_sum = over_cores(*pre_second)
    pre_second_all = sum_over_rest(pre_second_sum, bits)

    returned = []
    for pre, hidden in (
        (pre_near_all, hidden_near_all),
        (pre_first_all, hidden_first_all),
        (pre_second_all, hidden_second_all),
    ):
        slope = (hidden.astype(F32) * silu_slope(pre.astype(F32))).astype(BF16)
        got = swap(slope, "exp", 1)
        if returned:
            got = after(got, returned[-1][2])
        slope = jnp.concatenate(
            [jnp.where(core == 0, slope, got), jnp.where(core == 0, got, slope)], axis=0
        )
        back = dot(slope, up_local, 1, 1).astype(BF16)
        sides = back.reshape(2, back.shape[0] // 2, group)
        returned.append((sides[0], swap(sides[1], "ctx", 1), back))
    homes = {}
    for index, part in enumerate((near_part, first_far, second_far)):
        kept, got, _ = returned[index]
        rows = (kept.astype(F32) + got.astype(F32)).astype(BF16)
        for i, k in enumerate(part):
            homes[k] = pairs_of(rows[i * capacity : (i + 1) * capacity], k)
    homes = [homes[k] for k in range(experts)]

    grad_out, query_mine, query_other = call(
        grad_kernel, [slim, states, states], scalars, (queries, out_grad, weigh, *homes)
    )
    total, partner = scan_total(
        query_mine, query_other, decay_rates, place, block_len, True
    )
    before = None
    for reach in reaches:
        before, _ = scan_step(before, total, reach, decay_rates, place, block_len, True)
    keep_in = keep
    keep, give = scan_ends(before, query_mine, partner, decay_rates, place, block_len, True)
    leaving = (keep, swap(give, "ctx", 1))
    query_g, key_near, value_near = call(
        near_kernel, [slim, wide, wide], scalars,
        (queries, pair, grad_out, keep_in, given, weights)
    )
    key_g, value_g = call(
        far_kernel, [slim, slim], scalars,
        (pair, key_near, value_near) + leaving
    )
    return query_g, key_g, value_g


def solution(mesh):
    placed = (
        P("ctx", "exp"),
        P("ctx", "exp"),
        P("ctx", "exp"),
        P("ctx", "exp"),
        P("ctx", "exp", None),
        P("ctx", None, "exp"),
        P("exp"),
        P("ctx", None),
        P("ctx", None),
    )
    return jax.shard_map(
        on_device,
        mesh=mesh,
        in_specs=placed,
        out_specs=(P("ctx", "exp"), P("ctx", "exp"), P("ctx", "exp")),
        check_vma=False,
    )
```

```python
import functools

import jax
import jax.numpy as jnp
from jax import lax
from jax.experimental import pallas as pl
from jax.experimental.pallas import tpu as pltpu
from jax.sharding import PartitionSpec as P

DH = 128
F32 = jnp.float32
BF16 = jnp.bfloat16
SCALE = 1.0 / DH

SMEM = pl.BlockSpec(memory_space=pltpu.SMEM)
VMEM = pl.BlockSpec(memory_space=pltpu.VMEM)
LARGE = pl.CostEstimate(flops=1, bytes_accessed=40_000_000, transcendentals=0)
SMALL = pl.CostEstimate(flops=1, bytes_accessed=1, transcendentals=0)


def dot(left, right, left_dim, right_dim):
    return lax.dot_general(
        left, right, (((left_dim,), (right_dim,)), ((), ())), preferred_element_type=F32
    )


def silu_slope(value):
    sigma = jax.nn.sigmoid(value)
    return sigma * (1.0 + value * (1.0 - sigma))


def lanes_of(place_ref, slot, heads):
    head = lax.rem(place_ref[0] * (heads // 2) + slot, heads)
    return head, pl.ds(pl.multiple_of(head * DH, DH), DH)


def column(block_len):
    return lax.broadcasted_iota(jnp.int32, (block_len, 1), 0).astype(F32)


def decay_within(rate, block_len):
    rows = lax.broadcasted_iota(jnp.int32, (block_len, block_len), 0)
    cols = lax.broadcasted_iota(jnp.int32, (block_len, block_len), 1)
    distance = (rows - cols).astype(F32)
    return jnp.where(distance >= 0.0, jnp.exp(rate * jnp.maximum(distance, 0.0)), 0.0)


def key_state_kernel(place_ref, rates_ref, pair_ref, mine_ref, other_ref):
    block_len, half = pair_ref.shape[0] // 2, mine_ref.shape[0]
    steps = column(block_len)
    for slot in [*range(half, 2 * half), *range(half)]:
        head, lanes = lanes_of(place_ref, slot, 2 * half)
        power = jnp.exp(rates_ref[head] * (block_len - steps))
        scaled = (pair_ref[:block_len, lanes].astype(F32) * power).astype(BF16)
        state_ref = (mine_ref, other_ref)[slot // half]
        state_ref[slot % half] = dot(scaled, pair_ref[block_len:, lanes], 0, 0).astype(BF16)


def pick_rows(choose_ref, rows, send_refs):
    capacity = choose_ref.shape[1]
    if capacity % 8:
        for k, send_ref in enumerate(send_refs):
            send_ref[...] = dot(choose_ref[k], rows, 1, 0).astype(BF16)
        return
    table = choose_ref[...].reshape(len(send_refs) * capacity, rows.shape[0])
    picked = dot(table.astype(BF16), rows, 1, 0)
    for k, send_ref in enumerate(send_refs):
        send_ref[...] = picked[k * capacity : (k + 1) * capacity].astype(BF16)


def route_kernel(
    place_ref, slots_ref, grad_ref, choose_ref, weigh_ref, *send_refs
):
    experts, capacity, block_len = choose_ref.shape
    rows = lax.broadcasted_iota(jnp.int32, (block_len, block_len), 0)
    cols = lax.broadcasted_iota(jnp.int32, (block_len, block_len), 1)

    first, second = [slots_ref[i : i + 1, :].astype(jnp.int32) for i in range(2)]
    names = lax.broadcasted_iota(jnp.int32, (32, block_len), 0)
    hit_first = jnp.where(names == first, 1.0, 0.0)
    hit_second = jnp.where(names == second, 1.0, 0.0)
    earlier = jnp.where(rows < cols, 1.0, 0.0).astype(BF16)
    before = dot((hit_first + hit_second).astype(BF16), earlier, 1, 0)
    slot_first = jnp.sum(before * hit_first, axis=0, keepdims=True).astype(jnp.int32)
    slot_second = jnp.sum(before * hit_second, axis=0, keepdims=True).astype(jnp.int32)
    slots = lax.broadcasted_iota(jnp.int32, (capacity, block_len), 0)
    for k in range(experts):
        expert = place_ref[1] ^ k
        named = ((slots == slot_first) & (first == expert)) | (
            (slots == slot_second) & (second == expert)
        )
        choose_ref[k] = jnp.where(named, 1.0, 0.0)
    pick_rows(choose_ref, grad_ref[...], send_refs)

    columns = jnp.concatenate(
        [first.astype(F32), second.astype(F32), slot_first.astype(F32), slot_second.astype(F32)]
        + [slots_ref[2:3, :], slots_ref[3:4, :]] + [jnp.zeros((2, block_len), F32)],
        axis=0,
    ).T
    first, second, slot_first, slot_second = [
        columns[:, i : i + 1].astype(jnp.int32) for i in range(4)
    ]
    slots = lax.broadcasted_iota(jnp.int32, (block_len, capacity), 1)
    for k in range(experts):
        expert = place_ref[1] ^ k
        one = jnp.where((slots == slot_first) & (first == expert), columns[:, 4:5], 0.0)
        two = jnp.where((slots == slot_second) & (second == expert), columns[:, 5:6], 0.0)
        weigh_ref[k] = (one + two).astype(BF16)


def intra_kernel(place_ref, rates_ref, q_ref, pair_ref, intra_ref, weights_ref):
    block_len, heads = q_ref.shape[0], weights_ref.shape[0]
    for slot in range(heads):
        head, lanes = lanes_of(place_ref, slot, heads)
        within = decay_within(rates_ref[head], block_len)
        scores = dot(q_ref[:, lanes], pair_ref[:block_len, lanes], 1, 1)
        weights = (SCALE * scores * within).astype(BF16)
        weights_ref[slot] = weights
        intra_ref[:, lanes] = dot(weights, pair_ref[block_len:, lanes], 1, 0)


def attend_kernel(
    place_ref, rates_ref, q_ref, intra_ref, choose_ref, mine_ref, other_ref, *refs
):
    send_refs, attn_ref = refs[:-1], refs[-1]
    block_len, half = q_ref.shape[0], mine_ref.shape[0]
    steps = column(block_len)
    for slot in range(2 * half):
        head, lanes = lanes_of(place_ref, slot, 2 * half)
        entering = (mine_ref, other_ref)[slot // half][slot % half]
        power = SCALE * jnp.exp(rates_ref[head] * steps)
        inter = power * dot(q_ref[:, lanes], entering, 1, 0)
        attn_ref[:, lanes] = (intra_ref[:, lanes] + inter).astype(BF16)
    pick_rows(choose_ref, attn_ref[...], send_refs)


def grad_kernel(place_ref, rates_ref, q_ref, out_grad_ref, weigh_ref, *refs):
    experts = weigh_ref.shape[0]
    home_refs, (grad_ref, mine_ref, other_ref) = refs[:experts], refs[experts:]
    block_len, half = q_ref.shape[0], mine_ref.shape[0]
    steps = column(block_len)
    total = out_grad_ref[...].astype(F32)
    for k in range(experts):
        total = total + dot(weigh_ref[k], home_refs[k][...], 1, 0)
    grad_ref[...] = total.astype(BF16)
    for slot in [*range(half, 2 * half), *range(half)]:
        head, lanes = lanes_of(place_ref, slot, 2 * half)
        power = jnp.exp(rates_ref[head] * (steps + 1.0))
        scaled = (q_ref[:, lanes].astype(F32) * power).astype(BF16)
        state_ref = (mine_ref, other_ref)[slot // half]
        state_ref[slot % half] = dot(scaled, grad_ref[:, lanes], 0, 0).astype(BF16)


def near_kernel(
    place_ref, rates_ref, q_ref, pair_ref, grad_ref, mine_ref, other_ref, weights_ref,
    query_ref, key_ref, value_ref,
):
    block_len, half = q_ref.shape[0], mine_ref.shape[0]
    steps = column(block_len)
    for slot in range(2 * half):
        head, lanes = lanes_of(place_ref, slot, 2 * half)
        rate = rates_ref[head]
        grad = grad_ref[:, lanes]
        entering = (mine_ref, other_ref)[slot // half][slot % half]
        within = decay_within(rate, block_len)
        dweights = (SCALE * dot(grad, pair_ref[block_len:, lanes], 1, 1) * within).astype(BF16)
        query = dot(dweights, pair_ref[:block_len, lanes], 1, 0)
        query = query + SCALE * jnp.exp(rate * steps) * dot(grad, entering, 1, 1)
        query_ref[:, lanes] = query.astype(BF16)
        key_ref[:, lanes] = dot(dweights, q_ref[:, lanes], 0, 0)
        value_ref[:, lanes] = dot(weights_ref[slot], grad, 0, 0)


def far_kernel(
    place_ref, rates_ref, pair_ref, key_near, value_near, mine_ref, other_ref, key_ref, value_ref
):
    block_len, half = pair_ref.shape[0] // 2, mine_ref.shape[0]
    steps = column(block_len)
    for slot in range(2 * half):
        head, lanes = lanes_of(place_ref, slot, 2 * half)
        leaving = (mine_ref, other_ref)[slot // half][slot % half]
        power = SCALE * jnp.exp(rates_ref[head] * (block_len - 1.0 - steps))
        key_ref[:, lanes] = (
            key_near[:, lanes] + power * dot(pair_ref[block_len:, lanes], leaving, 1, 1)
        ).astype(BF16)
        value_ref[:, lanes] = (
            value_near[:, lanes] + power * dot(pair_ref[:block_len, lanes], leaving, 1, 0)
        ).astype(BF16)


def call(kernel, out_shapes, scalars, arrays, scratch=(), cost=SMALL):
    return pl.pallas_call(
        kernel,
        out_shape=list(out_shapes),
        in_specs=[SMEM] * len(scalars) + [VMEM] * len(arrays),
        out_specs=[VMEM] * len(out_shapes),
        scratch_shapes=list(scratch),
        compiler_params=pltpu.CompilerParams(vmem_limit_bytes=16 * 1024 * 1024),
        cost_estimate=cost,
    )(*scalars, *arrays)


def swap(array, axis, distance):
    size = lax.axis_size(axis)
    return lax.ppermute(array, axis, [(i, i ^ distance) for i in range(size)])


def trade(array, pairs, partner):
    return lax.ppermute(
        array, "ctx", [(2 * partner(i) + s, 2 * i + s) for i in range(pairs) for s in (0, 1)]
    )


def after(array, *events):
    return lax.optimization_barrier((array,) + events)[0]


def head_power(rates, place, half, tokens):
    mine = lax.dynamic_slice(rates, (place[0] * half,), (half,))[:, None, None]
    return jnp.exp(-mine * tokens)


def scan_total(mine, other, rates, place, block_len, reverse, *events):
    side = 1 - place[0] if reverse else place[0]
    whole = head_power(rates, place, mine.shape[0], block_len)
    partner = after(swap(other, "ctx", 1), *events)
    first = jnp.where(side == 0, mine, partner).astype(F32)
    second = jnp.where(side == 0, partner, mine).astype(F32)
    return (whole * first + second).astype(BF16), partner


def scan_step(before, total, reach, rates, place, block_len, reverse, *events):
    half = total.shape[0]
    pairs = lax.axis_size("ctx") // 2
    pair = pairs - 1 - place[1] if reverse else place[1]
    if before is None:
        upto = total
    else:
        whole = head_power(rates, place, half, 2.0 * block_len)
        upto = (whole * before + total.astype(F32)).astype(BF16)
    upto = after(upto, *events)
    lower, offset = (pair & reach) == 0, pair & (reach - 1)
    got = None
    for j in range(reach):

        def partner(i, j=j):
            i = pairs - 1 - i if reverse else i
            start = i - i % (2 * reach)
            first, second = start + reach - 1, start + reach + j
            i = {first: second, second: first}.get(i, i)
            return pairs - 1 - i if reverse else i

        one = trade(upto, pairs, partner)
        got = one if got is None else jnp.where(offset == j, one, got)
    scale = head_power(rates, place, half, 2.0 * block_len * offset.astype(F32))
    grown = scale * got.astype(F32)
    kept = 0.0 if before is None else before
    return jnp.where(lower, kept, kept + grown), upto


def scan_ends(before, mine, partner, rates, place, block_len, reverse):
    side = 1 - place[0] if reverse else place[0]
    whole = head_power(rates, place, mine.shape[0], block_len)
    first = jnp.where(side == 0, mine, partner).astype(F32)
    second_meets = whole * before + first
    keep = jnp.where(side == 0, before, second_meets).astype(BF16)
    give = jnp.where(side == 0, second_meets, before).astype(BF16)
    return keep, give


def two_products(own, other, part, multiply, *events):
    mine = lax.axis_index("exp") & 1
    rows = lambda flag: jnp.concatenate(
        [jnp.where(flag == 0, own[k], other[k]) for k in part], axis=0
    )
    sent = multiply(after(rows(1 - mine), *events)).astype(BF16)
    return sent, multiply(after(rows(mine), sent)).astype(BF16)


def one_product(own, other, part, multiply, *events):
    mine = lax.axis_index("exp") & 1
    rows = [side[k] for side in (own, other) for k in part]
    whole = multiply(after(jnp.concatenate(rows, axis=0), *events)).astype(BF16)
    whole = whole.reshape(2, whole.shape[0] // 2, whole.shape[1])
    sent = lax.dynamic_index_in_dim(whole, 1 - mine, 0, False)
    return sent, lax.dynamic_index_in_dim(whole, mine, 0, False)


def over_cores(sent, kept):
    return (kept.astype(F32) + swap(sent, "exp", 1).astype(F32)).astype(BF16)


def sum_over_rest(part, bits):
    for bit in range(1, bits):
        part = (part.astype(F32) + swap(part, "exp", 1 << bit).astype(F32)).astype(BF16)
    return part


def on_device(
    queries, keys, values, out_grad, up_weight, down_weight, decay_rates, routes, gate_weights
):
    block_len, group = queries.shape
    heads = group // DH
    half = heads // 2
    experts = lax.axis_size("ctx") // 2
    bits = (lax.axis_size("exp") - 1).bit_length()
    capacity = block_len * 9 // (4 * experts)
    position = lax.axis_index("ctx").astype(jnp.int32)
    core = lax.axis_index("exp").astype(jnp.int32) & 1
    place = jnp.stack([position & 1, position >> 1, core])
    scalars = (place, -decay_rates)
    pair = jnp.concatenate([keys, values], axis=0)
    up_local, down_local = up_weight[0], down_weight[0]
    quarter = max(experts // 4, 1)
    near_part = range(experts // 2)
    first_far = range(experts - quarter, experts)
    second_far = range(experts // 2, experts - quarter)
    states = jax.ShapeDtypeStruct((half, DH, DH), BF16)
    weight_sq = jax.ShapeDtypeStruct((heads, block_len, block_len), BF16)
    wide = jax.ShapeDtypeStruct((block_len, group), F32)
    slim = jax.ShapeDtypeStruct((block_len, group), BF16)
    choose_table = jax.ShapeDtypeStruct((experts, capacity, block_len), F32)
    weigh_table = jax.ShapeDtypeStruct((experts, block_len, capacity), BF16)
    slots = jax.ShapeDtypeStruct((capacity, group), BF16)

    slots_of = jnp.concatenate([routes.astype(F32), gate_weights], axis=1).T
    reaches = [1 << i for i in range((experts - 1).bit_length())]
    pairs_of = lambda rows, k: swap(rows, "ctx", 2 * k) if k else rows

    key_mine, key_other = call(key_state_kernel, [states] * 2, scalars, (pair,))
    choose, weigh, *send_grad = call(
        route_kernel, [choose_table, weigh_table] + [slots] * experts,
        (place,), (slots_of, out_grad)
    )
    intra, weights = call(
        intra_kernel, [wide, weight_sq], scalars, (queries, pair), cost=LARGE
    )

    total, partner = scan_total(
        key_mine, key_other, decay_rates, place, block_len, False, send_grad[0]
    )
    by_down = lambda rows: dot(rows, down_local, 1, 1)
    by_up = lambda rows: dot(rows, up_local, 1, 0)
    grad_own = {0: send_grad[0]}
    grad_other = {0: swap(after(send_grad[0], total), "ctx", 1)}
    for k in near_part[1:]:
        grad_own[k] = pairs_of(after(send_grad[k], total), k)
    for k in first_far:
        grad_own[k] = pairs_of(after(send_grad[k], total), k)
    before = None
    for index, reach in enumerate(reaches):
        events = [intra] if index == 1 else []
        before, upto = scan_step(
            before, total, reach, decay_rates, place, block_len, False, *events
        )
    for k in near_part[1:]:
        grad_other[k] = swap(after(grad_own[k], upto), "ctx", 1)
    keep, give = scan_ends(before, key_mine, partner, decay_rates, place, block_len, False)
    for k in second_far:
        grad_own[k] = pairs_of(after(send_grad[k], give), k)
    for k in first_far:
        grad_other[k] = swap(grad_own[k], "ctx", 1)
    given = swap(give, "ctx", 1)
    hidden_near = one_product(grad_own, grad_other, near_part, by_down, give)
    hidden_near_sum = over_cores(*hidden_near)
    hidden_near_all = sum_over_rest(hidden_near_sum, bits)
    given, hidden_near_sum = lax.optimization_barrier((given, hidden_near_sum))
    hidden_near_all = sum_over_rest(hidden_near_sum, bits)
    send_in = call(
        attend_kernel, [slots] * experts, scalars, (queries, intra, choose, keep, given),
        [pltpu.VMEM((block_len, group), BF16)],
    )
    in_own, in_other = {0: send_in[0]}, {0: swap(send_in[0], "ctx", 1)}
    for k in [*near_part[1:], *first_far]:
        in_own[k] = pairs_of(send_in[k], k)
    for k in near_part[1:]:
        in_other[k] = swap(in_own[k], "ctx", 1)
    hidden_first = two_products(grad_own, grad_other, first_far, by_down, send_in[0])
    hidden_first_sum = over_cores(*hidden_first)
    hidden_first_all = sum_over_rest(hidden_first_sum, bits)
    for k in second_far:
        in_own[k] = pairs_of(after(send_in[k], *[in_own[k] for k in first_far], hidden_first_sum), k)
    for k in first_far:
        in_other[k] = swap(after(in_own[k], *[in_other[k] for k in near_part[1:]]), "ctx", 1)
    pre_near = two_products(in_own, in_other, near_part, by_up, hidden_first_sum)
    pre_near_sum = over_cores(*pre_near)
    pre_near_all = sum_over_rest(pre_near_sum, bits)
    for k in second_far:
        in_other[k] = swap(after(in_own[k], pre_near_sum), "ctx", 1)
    for k in second_far:
        grad_other[k] = swap(after(grad_own[k], pre_near_sum), "ctx", 1)
    pre_first = two_products(in_own, in_other, first_far, by_up, pre_near_sum)
    pre_first_sum = over_cores(*pre_first)
    pre_first_all = sum_over_rest(pre_first_sum, bits)
    hidden_second = two_products(grad_own, grad_other, second_far, by_down, pre_first_sum)
    hidden_second_sum = over_cores(*hidden_second)
    hidden_second_all = sum_over_rest(hidden_second_sum, bits)
    pre_second = two_products(in_own, in_other, second_far, by_up, hidden_second_sum)
    pre_second_sum = over_cores(*pre_second)
    pre_second_all = sum_over_rest(pre_second_sum, bits)

    returned = []
    for pre, hidden in (
        (pre_near_all, hidden_near_all),
        (pre_first_all, hidden_first_all),
        (pre_second_all, hidden_second_all),
    ):
        slope = (hidden.astype(F32) * silu_slope(pre.astype(F32))).astype(BF16)
        got = swap(slope, "exp", 1)
        if returned:
            got = after(got, returned[-1][2])
        slope = jnp.concatenate(
            [jnp.where(core == 0, slope, got), jnp.where(core == 0, got, slope)], axis=0
        )
        back = dot(slope, up_local, 1, 1).astype(BF16)
        sides = back.reshape(2, back.shape[0] // 2, group)
        returned.append((sides[0], swap(sides[1], "ctx", 1), back))
    homes = {}
    for index, part in enumerate((near_part, first_far, second_far)):
        kept, got, _ = returned[index]
        rows = (kept.astype(F32) + got.astype(F32)).astype(BF16)
        for i, k in enumerate(part):
            homes[k] = pairs_of(rows[i * capacity : (i + 1) * capacity], k)
    homes = [homes[k] for k in range(experts)]

    grad_out, query_mine, query_other = call(
        grad_kernel, [slim, states, states], scalars, (queries, out_grad, weigh, *homes)
    )
    total, partner = scan_total(
        query_mine, query_other, decay_rates, place, block_len, True
    )
    before = None
    for reach in reaches:
        before, _ = scan_step(before, total, reach, decay_rates, place, block_len, True)
    keep_in = keep
    keep, give = scan_ends(before, query_mine, partner, decay_rates, place, block_len, True)
    leaving = (keep, swap(give, "ctx", 1))
    query_g, key_near, value_near = call(
        near_kernel, [slim, wide, wide], scalars,
        (queries, pair, grad_out, keep_in, given, weights)
    )
    key_g, value_g = call(
        far_kernel, [slim, slim], scalars,
        (pair, key_near, value_near) + leaving
    )
    return query_g, key_g, value_g


def solution(mesh):
    placed = (
        P("ctx", "exp"),
        P("ctx", "exp"),
        P("ctx", "exp"),
        P("ctx", "exp"),
        P("ctx", "exp", None),
        P("ctx", None, "exp"),
        P("exp"),
        P("ctx", None),
        P("ctx", None),
    )
    return jax.shard_map(
        on_device,
        mesh=mesh,
        in_specs=placed,
        out_specs=(P("ctx", "exp"), P("ctx", "exp"), P("ctx", "exp")),
        check_vma=False,
    )
```
